256 devices in a mesh: space: 32 (over y, z_lo, core), harm: 8 (over z_hi, x).
Axes of the slice: x: 4, y: 4, z: 8 (z_hi: 2, z_lo: 4; z = z_hi * 4 + z_lo), core: 2. Of those that a mesh axis runs over, the one named last changes fastest.
Arguments:
- coeffs: bfloat16 [120, 32, 256, 256], P('harm', 'space'), may hold values from -6 to 6
- synthesis: bfloat16 [256, 120], replicated, may hold values from -0.5 to 0.5
- projection: bfloat16 [120, 256], replicated, may hold values from -0.375 to 0.375
- turn_projection: bfloat16 [3, 120, 256], replicated, may hold values from -0.375 to 0.375
- damping: float32 [120], replicated, may hold values from 0.2 to 2
Outputs:
- rate: bfloat16 [120, 32, 256, 256], P('harm', 'space')
- velocity: float32 [3, 32, 256, 256], P(None, 'space', 'harm')
The draws below stay inside these ranges and needn't reach their ends.
All inputs are finite; a program needn't handle non-finite values.
Results may differ from the reference program's by a relative error of at most 0.0042.
Values may be sent and summed in bfloat16 or wider, within the bound.
No kernel may reach another device: no remote copies, remote signals or barrier semaphores. Data moves between devices by JAX's collectives and lax.ppermute only.
A program may use at most 128 MiB of HBM per device.

```python
import math
import jax
import jax.numpy as jnp
from jax import lax

NX = 256
NY = 256
COEFS = 120
QUAD = 256
NZ = 32


def levels(own_key, extent, shards, smallest, high):
    factor_of, own = 1.0, jax.random.fold_in(own_key, 6)
    for dim, parts in shards:
        draws = jnp.exp(jax.random.uniform(jax.random.fold_in(own, dim), (parts,), jnp.float32, smallest / len(shards), high / len(shards)))
        factor_of = factor_of * jnp.repeat(draws, extent[dim] // parts).reshape([-1 if axis == dim else 1 for axis in range(len(extent))])
    return factor_of


def noise(stream_key, extent, deviation, limit, shards=(), held_as=jnp.bfloat16):
    loudness = levels(stream_key, extent, shards, -0.22, 0.18) if shards else 1.0
    values = jax.random.normal(stream_key, extent, jnp.float32) * deviation * loudness
    return jnp.minimum(jnp.maximum(values, -limit), limit).astype(held_as)


def setup_inputs(seed: int = 0) -> dict:
    streams_of = jax.random.split(jax.random.key(seed), 6)
    coeffs = noise(streams_of[0], (COEFS, NZ, NY, NX), 1.0, 6.0, ((0, 8), (1, 32)))
    synthesis = noise(streams_of[1], (QUAD, COEFS), COEFS ** -0.5, 0.5)
    projection = noise(streams_of[2], (COEFS, QUAD), QUAD ** -0.5, 0.375)
    turn_projection = noise(streams_of[3], (3, COEFS, QUAD), QUAD ** -0.5, 0.375)
    damping = jnp.clip(jnp.exp(jax.random.uniform(streams_of[4], (COEFS,), jnp.float32, math.log(0.2), math.log(2.0))), 0.2, 2.0)
    return {"coeffs": coeffs, "synthesis": synthesis, "projection": projection, "turn_projection": turn_projection, "damping": damping}


activity = -3.0
swim_speed = 1.0
transl_diff = 0.25
shape_factor = 0.9
golden_angle = math.pi * (3.0 - math.sqrt(5.0))
stress_pairs = ((0, 3, 4), (3, 1, 5), (4, 5, 2))

def sphere_directions(count):
    position = jnp.arange(count, dtype=jnp.float32)
    height = 1.0 - (2.0 * position + 1.0) / count
    radius = jnp.sqrt(1.0 - height * height)
    turning = position * golden_angle
    return jnp.stack([radius * jnp.cos(turning), radius * jnp.sin(turning), height])

def moment_table(synthesis, directions):
    dir_x, dir_y, dir_z = (directions[0], directions[1], directions[2])
    third = 1.0 / 3.0
    moments = jnp.stack([dir_x * dir_x - third, dir_y * dir_y - third, dir_z * dir_z - third, dir_x * dir_y, dir_x * dir_z, dir_y * dir_z])
    table = jnp.dot(moments, synthesis.astype(jnp.float32), precision=lax.Precision.HIGHEST)
    return (table * (activity / math.sqrt(synthesis.shape[0]))).astype(jnp.bfloat16)

def signed_wave(position, length):
    signed = jnp.where(position < length // 2, position, position - length)
    signed = jnp.where(position == length // 2, 0, signed)
    return 2.0 * math.pi / length * signed.astype(jnp.float32)

def differences(center, lower_z, upper_z, lower_y, upper_y):
    middle = center.astype(jnp.float32)
    upper_x = jnp.roll(middle, -1, 3)
    lower_x = jnp.roll(middle, 1, 3)
    lower_y = lower_y.astype(jnp.float32)
    upper_y = upper_y.astype(jnp.float32)
    lower_z = lower_z.astype(jnp.float32)
    upper_z = upper_z.astype(jnp.float32)
    gradients = ((0.5 * (upper_x - lower_x)).astype(jnp.bfloat16), (0.5 * (upper_y - lower_y)).astype(jnp.bfloat16), (0.5 * (upper_z - lower_z)).astype(jnp.bfloat16))
    laplacian = (upper_x + lower_x + upper_y + lower_y + upper_z + lower_z - 6.0 * middle).astype(jnp.bfloat16)
    return (gradients, laplacian)

def orient_rates(coef_block, gradients, laplacian, flow, directions, synthesis, projection, turn_projection, damping):
    density = jnp.dot(synthesis, coef_block, preferred_element_type=jnp.float32)
    advection = jnp.zeros_like(density)
    for j in range(3):
        slope = jnp.dot(synthesis, gradients[j], preferred_element_type=jnp.float32)
        advection = advection - (swim_speed * directions[j][:, None] + flow[j][None, :]) * slope
    strained = []
    for i in range(3):
        total = jnp.zeros_like(density)
        for j in range(3):
            forward_term = flow[3 + 3 * i + j]
            mirror_term = flow[3 + 3 * j + i]
            coupling = 0.5 * shape_factor * (forward_term + mirror_term) + 0.5 * (forward_term - mirror_term)
            total = total + coupling[None, :] * directions[j][:, None]
        strained.append(total)
    radial = directions[0][:, None] * strained[0] + directions[1][:, None] * strained[1] + directions[2][:, None] * strained[2]
    result = jnp.dot(projection, advection.astype(jnp.bfloat16), preferred_element_type=jnp.float32)
    for k in range(3):
        twist = ((strained[k] - directions[k][:, None] * radial) * density).astype(jnp.bfloat16)
        result = result + jnp.dot(turn_projection[k], twist, preferred_element_type=jnp.float32)
    result = result + transl_diff * laplacian.astype(jnp.float32) - damping[:, None] * coef_block.astype(jnp.float32)
    return result.astype(jnp.bfloat16)

def cell_rates(flat_coefs, flat_grads, flat_lap, flat_flow, directions, synthesis, projection, turn_projection, damping):
    cell_count = flat_coefs.shape[1]
    block_len = min(2048, cell_count)

    def advance(block_index, rate_cells):
        offset = block_index * block_len

        def window(array):
            return lax.dynamic_slice_in_dim(array, offset, block_len, 1)
        result = orient_rates(window(flat_coefs), tuple((window(g) for g in flat_grads)), window(flat_lap), window(flat_flow), directions, synthesis, projection, turn_projection, damping)
        return lax.dynamic_update_slice_in_dim(rate_cells, result, offset, 1)
    empty = jnp.zeros(flat_coefs.shape, jnp.bfloat16)
    return lax.fori_loop(0, cell_count // block_len, advance, empty)

def reference(coeffs, synthesis, projection, turn_projection, damping):
    directions = sphere_directions(QUAD)
    table = moment_table(synthesis, directions)
    stress = jnp.dot(table, coeffs.reshape(COEFS, -1), preferred_element_type=jnp.float32).reshape(6, NZ, NY, NX)
    spectrum = jnp.fft.fftn(stress, axes=(1, 2, 3))
    wave_x = signed_wave(jnp.arange(NX, dtype=jnp.int32), NX)[None, None, :]
    wave_y = signed_wave(jnp.arange(NY, dtype=jnp.int32), NY)[None, :, None]
    wave_z = signed_wave(jnp.arange(NZ, dtype=jnp.int32), NZ)[:, None, None]
    wave_vec = (wave_x, wave_y, wave_z)
    wave_sq = wave_x * wave_x + wave_y * wave_y + wave_z * wave_z
    inverse = jnp.where(wave_sq > 0, 1.0 / jnp.where(wave_sq > 0, wave_sq, 1.0), 0.0)
    force = []
    for i in range(3):
        total = spectrum[stress_pairs[i][0]] * wave_vec[0]
        total = total + spectrum[stress_pairs[i][1]] * wave_vec[1]
        total = total + spectrum[stress_pairs[i][2]] * wave_vec[2]
        force.append(1j * total)
    along = wave_vec[0] * force[0] + wave_vec[1] * force[1] + wave_vec[2] * force[2]
    flow_hat = [(force[i] - wave_vec[i] * along * inverse) * inverse for i in range(3)]
    pieces = list(flow_hat)
    for i in range(3):
        for j in range(3):
            pieces.append(1j * wave_vec[j] * flow_hat[i])
    fields = jnp.real(jnp.fft.ifftn(jnp.stack(pieces), axes=(1, 2, 3))).astype(jnp.float32)

    def one_plane(plane):
        center = lax.dynamic_index_in_dim(coeffs, plane, 1, True)
        lower_z = lax.dynamic_index_in_dim(coeffs, (plane + NZ - 1) % NZ, 1, True)
        upper_z = lax.dynamic_index_in_dim(coeffs, (plane + 1) % NZ, 1, True)
        gradients, laplacian = differences(center, lower_z, upper_z, jnp.roll(center, 1, 2), jnp.roll(center, -1, 2))
        flow = lax.dynamic_index_in_dim(fields, plane, 1, True).reshape(12, -1)
        return cell_rates(center.reshape(COEFS, -1), tuple((g.reshape(COEFS, -1) for g in gradients)), laplacian.reshape(COEFS, -1), flow, directions, synthesis, projection, turn_projection, damping)
    stacked = lax.map(one_plane, jnp.arange(NZ, dtype=jnp.int32))
    rate = jnp.transpose(stacked, (1, 0, 2)).reshape(COEFS, NZ, NY, NX)
    return (rate, fields[0:3])
```

```python
import functools
import math

import jax
import jax.numpy as jnp
import ml_dtypes
import numpy as np
from jax import lax
from jax.experimental import pallas as pl
from jax.experimental.pallas import tpu as pltpu
from jax.sharding import PartitionSpec as P

activity = -3.0
swim_speed = 1.0
transl_diff = 0.25
shape_factor = 0.9
golden_angle = math.pi * (3.0 - math.sqrt(5.0))

NX, NY, NZ = 256, 256, 32
COEFS, QUAD = 120, 256
SPACES, GROUPS = 32, 8
OWN = COEFS // GROUPS
PAD = 16
ROWS = NY // GROUPS
CELLS = ROWS * NX
HALF = NX // 2
ALL_PAD = GROUPS * PAD
LANES = 128
BLOCKS = 12
bf16, f32 = jnp.bfloat16, jnp.float32
VMEM = pl.BlockSpec(memory_space=pltpu.VMEM)
SMEM = pl.BlockSpec(memory_space=pltpu.SMEM)
PARAMS = pltpu.CompilerParams(vmem_limit_bytes=56 * 1024 * 1024)


def split_table(table):
    high = table.astype(ml_dtypes.bfloat16)
    low = (table - high.astype(np.float64)).astype(ml_dtypes.bfloat16)
    return (high, low)


def signed_wave(length):
    index = np.arange(length)
    signed = np.where(index < length // 2, index, index - length)
    return 2.0 * math.pi / length * np.where(index == length // 2, 0, signed)


def sphere_directions():
    position = np.arange(QUAD, dtype=np.float64)
    height = 1.0 - (2.0 * position + 1.0) / QUAD
    radius = np.sqrt(1.0 - height * height)
    turning = position * golden_angle
    return np.stack([radius * np.cos(turning), radius * np.sin(turning), height])


def tables():
    x = np.arange(NX)[None, :]
    k = np.arange(HALF)[:, None]
    angle = 2.0 * math.pi * (k * x % NX) / NX
    cos_x, sin_x = np.cos(angle), np.sin(angle)
    sign = (-1.0) ** x[0]
    minus = -sin_x
    minus[0] = sign
    forward_x = np.concatenate([cos_x, minus])
    scale = 1.0 / (NX * NY * NZ)
    weight = np.where(k == 0, 1.0, 2.0) * scale
    wave = 2.0 * math.pi / NX * k
    real_x = weight * cos_x
    imag_x = -weight * sin_x
    imag_x[0] = sign * scale
    slope_real = -weight * wave * sin_x
    slope_imag = -weight * wave * cos_x
    back_x = np.concatenate([real_x, imag_x, slope_real, slope_imag], axis=1)
    back_x = np.concatenate([back_x, back_x])

    z = np.arange(NZ)
    angle = 2.0 * math.pi * (z[:, None] * z[None, :] % NZ) / NZ
    both_z = np.concatenate([np.cos(angle), np.sin(angle)])
    forward_z = np.tile(both_z, (1, GROUPS))

    y = np.arange(HALF)[:, None]
    ky = np.arange(NY)[None, :]
    angle = 2.0 * math.pi * (y * ky % NY) / NY
    forward_y = np.block([[np.cos(angle), -np.sin(angle)], [np.sin(angle), np.cos(angle)]])

    ky = np.arange(NY)[:, None]
    angle = 2.0 * math.pi * (ky * np.arange(NY)[None, :] % NY) / NY
    cos_y = np.cos(angle).reshape(NY, GROUPS, 1, ROWS)
    sin_y = np.sin(angle).reshape(NY, GROUPS, 1, ROWS)
    from_real = np.concatenate([cos_y, sin_y], axis=2).reshape(NY, 2 * NY)
    from_imag = np.concatenate([-sin_y, cos_y], axis=2).reshape(NY, 2 * NY)
    back_y = np.concatenate([from_real, from_imag])
    return forward_x, forward_z, forward_y, both_z, back_y, back_x


def halves(value):
    high = value.astype(bf16)
    return high, (value - high.astype(f32)).astype(bf16)


def dot(a, b):
    return jnp.dot(a, b, preferred_element_type=f32)


def regroup_kernel(group_ref, coef_ref, *refs):
    outs, stages = refs[:GROUPS], refs[GROUPS:]
    group = group_ref[0]
    for stage in stages:
        stage[pl.ds(OWN * ROWS, ROWS), :] = jnp.zeros((ROWS, LANES), f32)
    for j in range(GROUPS):
        first = pl.multiple_of((group ^ j) * ROWS, ROWS)
        rows = coef_ref[:, pl.ds(first, ROWS), :].astype(f32)
        rows = rows.reshape(OWN * ROWS, NX)
        for side, stage in enumerate(stages):
            stage[pl.ds(0, OWN * ROWS), :] = rows[:, side * LANES : (side + 1) * LANES]
            for r in range(ROWS):
                lane = r * NX + side * LANES
                outs[j][:, lane : lane + LANES] = stage[pl.ds(r, PAD, stride=ROWS), :].astype(bf16)


def stress_kernel(table_ref, coef_ref, high_ref, low_ref, out_ref, stress_high, stress_low):
    step = 32

    def rows(i, carry):
        first = pl.multiple_of(i * step, step)
        sums = [jnp.zeros((step, NX), f32)] * 5
        for c in range(OWN):
            value = coef_ref[c, pl.ds(first, step), :].astype(f32)
            sums = [s + table_ref[r, c] * value for r, s in enumerate(sums)]
        for r in range(5):
            high, low = halves(sums[r])
            stress_high[r, pl.ds(first, step), :] = high
            stress_low[r, pl.ds(first, step), :] = low
        return carry

    lax.fori_loop(0, NY // step, rows, 0)

    def across(a, b):
        return lax.dot_general(a, b, (((1,), (1,)), ((), ())), preferred_element_type=f32)

    for r in range(5):
        high, low = high_ref[...], low_ref[...]
        result = (
            across(high, stress_high[r]) + across(low, stress_high[r]) + across(high, stress_low[r])
        ).astype(bf16)
        for half in range(2):
            for part in range(2):
                lane = (2 * r + part) * HALF
                out_ref[half * HALF : (half + 1) * HALF, lane : lane + HALF] = result[
                    part * HALF : (part + 1) * HALF, half * HALF : (half + 1) * HALF
                ]


def solve_kernel(
    wave_ref, half_ref, ky_ref, kz_ref, recv_ref,
    fz_high, fz_low, fy_high, fy_low, bz, by_high, by_low, out_ref,
):
    recv = recv_ref[...]
    by_z = dot(fz_high[...], recv) + dot(fz_low[...], recv)
    lines = []
    for r in range(5):
        lane = 2 * r * HALF
        cos_re, cos_im = by_z[:NZ, lane : lane + HALF], by_z[:NZ, lane + HALF : lane + 2 * HALF]
        sin_re, sin_im = by_z[NZ:, lane : lane + HALF], by_z[NZ:, lane + HALF : lane + 2 * HALF]
        lines.append(jnp.concatenate([cos_re + sin_im, cos_im - sin_re], axis=1))
    high, low = halves(jnp.concatenate(lines))
    spec = dot(high, fy_high[...]) + dot(low, fy_high[...]) + dot(high, fy_low[...])
    lane = lax.broadcasted_iota(jnp.int32, (NZ, NY), 1)
    flip = jnp.where((lane % 2) * half_ref[0] == 1, -1.0, 1.0)
    real = [spec[r * NZ : (r + 1) * NZ, :NY] * flip for r in range(5)]
    imag = [spec[r * NZ : (r + 1) * NZ, NY:] * flip for r in range(5)]
    kx = jnp.full((NZ, NY), wave_ref[0], f32)
    ky = jnp.broadcast_to(ky_ref[...], (NZ, NY))
    kz = jnp.broadcast_to(kz_ref[...], (NZ, NY))
    square = kx * kx + ky * ky + kz * kz
    inverse = jnp.where(square > 0, 1.0 / jnp.where(square > 0, square, 1.0), 0.0)

    def force(part):
        xx, yy, xy, xz, yz = part
        return (
            kx * xx + ky * xy + kz * xz,
            kx * xy + ky * yy + kz * yz,
            kx * xz + ky * yz,
        )

    def solve(f):
        along = (kx * f[0] + ky * f[1] + kz * f[2]) * inverse
        return [(f[i] - k * along) * inverse for i, k in enumerate((kx, ky, kz))]

    flow_re = solve([-f for f in force(imag)])
    flow_im = solve(force(real))
    fields = list(zip(flow_re, flow_im))
    fields += [(-ky * flow_im[i], ky * flow_re[i]) for i in range(3)]
    fields += [(-kz * flow_im[i], kz * flow_re[i]) for i in range(2)]
    back = []
    for re, im in fields:
        high, low = halves(jnp.concatenate([re, im], axis=1))
        both = dot(bz[...], jnp.concatenate([high, low, high]))
        back.append(
            jnp.concatenate(
                [both[:NZ, :NY] - both[NZ:, NY:], both[:NZ, NY:] + both[NZ:, :NY]], axis=1
            )
        )
    high, low = halves(jnp.concatenate(back))
    done = dot(high, by_high[...]) + dot(low, by_high[...]) + dot(high, by_low[...])
    for h in range(GROUPS):
        lane = 2 * ROWS * h
        pieces = [done[f * NZ : (f + 1) * NZ, lane : lane + 2 * ROWS] for f in range(8)]
        out_ref[h * NZ : (h + 1) * NZ, :] = jnp.concatenate(pieces, axis=1).astype(bf16)


def fields_kernel(recv_ref, high_ref, low_ref, out_ref):
    flat = recv_ref[...].astype(f32).T.astype(bf16)
    both = dot(flat, high_ref[...]) + dot(flat, low_ref[...])

    def field(f, lane):
        row = 2 * ROWS * f
        return (
            both[row : row + ROWS, lane : lane + NX]
            + both[row + ROWS : row + 2 * ROWS, lane + NX : lane + 2 * NX]
        )

    for i in range(3):
        out_ref[i] = field(i, 0)
        out_ref[3 + i] = field(i, 2 * NX)
    for i in range(5):
        out_ref[6 + i] = field(3 + i, 0)


def weights_kernel(dir_ref, synth_ref, proj_ref, turn_ref, out_ref):
    synth = synth_ref[...]
    p = [dir_ref[j : j + 1, :] for j in range(3)]
    proj = proj_ref[...].astype(f32)
    turn = [turn_ref[k].astype(f32) for k in range(3)]
    radial = turn[0] * p[0] + turn[1] * p[1] + turn[2] * p[2]
    same = 0.5 * (shape_factor + 1.0)
    swap = 0.5 * (shape_factor - 1.0)

    def plain(i, j):
        return turn[i] * p[j] - radial * (p[i] * p[j])

    def strain(i, j):
        return same * plain(i, j) + swap * plain(j, i)

    left = [-0.5 * swim_speed * proj * p[j] for j in range(3)] + [-0.5 * proj]
    trace = strain(2, 2)
    left += [strain(0, 0) - trace, strain(1, 0), strain(2, 0)]
    left += [strain(0, 1), strain(1, 1) - trace, strain(2, 1)]
    left += [strain(0, 2), strain(1, 2)]
    for n, value in enumerate(left):
        high, low = halves(value)
        out_ref[:, n * ALL_PAD : (n + 1) * ALL_PAD] = (dot(high, synth) + dot(low, synth)).astype(bf16)


def assemble_kernel(group_ref, *refs):
    out_ref = refs[GROUPS]
    group = group_ref[0]
    for j in range(GROUPS):
        out_ref[pl.ds(pl.multiple_of((group ^ j) * PAD, PAD), PAD), :] = refs[j][...]


def rate_kernel(
    center_ref, zlow_ref, zhigh_ref, ylow_ref, yhigh_ref, flow_ref, weight_ref, damp_ref,
    out_ref, padded, operand, local_terms, *stages,
):
    chunk = 16
    padded[:, :NX] = ylow_ref[...]
    padded[:, NX : NX + CELLS] = center_ref[...]
    padded[:, NX + CELLS :] = yhigh_ref[...]

    def row(r, carry, part):
        y = part * chunk + r
        here = pl.multiple_of(y * NX, NX)
        flow = [flow_ref[f, pl.ds(y, 1), :] for f in range(11)]
        for g in range(GROUPS):
            rows = slice(g * PAD, (g + 1) * PAD)
            value = padded[rows, pl.ds(here + NX, NX)].astype(f32)
            y_low = padded[rows, pl.ds(here, NX)].astype(f32)
            y_high = padded[rows, pl.ds(here + 2 * NX, NX)].astype(f32)
            z_low = zlow_ref[rows, pl.ds(here, NX)].astype(f32)
            z_high = zhigh_ref[rows, pl.ds(here, NX)].astype(f32)
            x_low = pltpu.roll(value, 1, 1)
            x_high = pltpu.roll(value, NX - 1, 1)
            diffs = (x_high - x_low, y_high - y_low, z_high - z_low)
            drift = flow[0] * diffs[0] + flow[1] * diffs[1] + flow[2] * diffs[2]
            lap = x_high + x_low + y_high + y_low + z_high + z_low - 6.0 * value
            local_terms[rows, :] = transl_diff * lap - damp_ref[rows, :] * value
            terms = list(diffs) + [drift] + [flow[3 + n] * value for n in range(8)]
            for n, term in enumerate(terms):
                operand[n * ALL_PAD + g * PAD : n * ALL_PAD + (g + 1) * PAD, :] = term.astype(bf16)
        result = dot(weight_ref[...], operand[...]) + local_terms[...]
        for side, stage in enumerate(stages):
            stage[pl.ds(r, ALL_PAD, stride=chunk), :] = result[:, side * LANES : (side + 1) * LANES]
        return carry

    for part in range(ROWS // chunk):
        lax.fori_loop(0, chunk, functools.partial(row, part=part), 0)
        for g in range(GROUPS):
            for c in range(OWN):
                first = (g * PAD + c) * chunk
                for side, stage in enumerate(stages):
                    out_ref[
                        g, c, part * chunk : (part + 1) * chunk, side * LANES : (side + 1) * LANES
                    ] = stage[first : first + chunk, :].astype(bf16)


def call(kernel, out_shape, ins, scratch=(), scalars=0, flops=0, byte_count=0):
    return pl.pallas_call(
        kernel,
        out_shape=out_shape,
        in_specs=[SMEM] * scalars + [VMEM] * (len(ins) - scalars),
        out_specs=jax.tree.map(lambda _: VMEM, out_shape),
        scratch_shapes=list(scratch),
        compiler_params=PARAMS,
        cost_estimate=pl.CostEstimate(flops=flops, bytes_accessed=byte_count, transcendentals=0),
    )(*ins)


def shape(*dims, dtype=bf16):
    return jax.ShapeDtypeStruct(dims, dtype)


def pad_groups(value, axis):
    parts = value.reshape(*value.shape[:axis], GROUPS, OWN, *value.shape[axis + 1 :])
    widths = [(0, 0)] * parts.ndim
    widths[axis + 1] = (0, PAD - OWN)
    parts = jnp.pad(parts, widths)
    return parts.reshape(*value.shape[:axis], ALL_PAD, *value.shape[axis + 1 :])


def stress_table(synthesis, directions, group):
    dir_x, dir_y, dir_z = directions
    third = 1.0 / 3.0
    moments = np.stack(
        [
            dir_x * dir_x - third,
            dir_y * dir_y - third,
            dir_z * dir_z - third,
            dir_x * dir_y,
            dir_x * dir_z,
            dir_y * dir_z,
        ]
    ).astype(np.float32)
    own = lax.dynamic_slice_in_dim(synthesis, group * OWN, OWN, 1).astype(f32)
    table = jnp.dot(moments, own, precision=lax.Precision.HIGHEST)
    table = (table * (activity / math.sqrt(QUAD))).astype(bf16).astype(f32)
    return jnp.concatenate([table[0:2] - table[2:3], table[3:6]])


def local(coeffs, synthesis, projection, turn_projection, damping):
    group = lax.axis_index("harm")
    plane = lax.axis_index("space")
    everyone = ("harm", "space")
    position = group * SPACES + plane
    forward_x, forward_z, forward_y, back_z, back_y, back_x = tables()
    directions = sphere_directions()
    own = coeffs.reshape(OWN, NY, NX)
    group_arg = group.astype(jnp.int32).reshape(1)

    chunks = call(
        regroup_kernel, [shape(PAD, CELLS)] * GROUPS, [group_arg, own],
        [pltpu.VMEM((PAD * ROWS, LANES), f32)] * 2, 1, 0, 4 << 20,
    )
    arrived = [chunks[0]]
    for j in range(1, GROUPS):
        arrived.append(lax.ppermute(chunks[j], "harm", [(i, i ^ j) for i in range(GROUPS)]))

    table = stress_table(synthesis, directions, group)
    high, low = split_table(forward_x)
    sent = call(
        stress_kernel, shape(NX, 10 * HALF), [table, own, high, low],
        [pltpu.VMEM((5, NY, NX), bf16)] * 2, 1, 1 << 30, 3 << 20,
    )
    columns = lax.all_to_all(sent, everyone, 0, 0, tiled=True)

    wave = (position % HALF).astype(f32) * (2.0 * math.pi / NX)
    half = (position // HALF).astype(jnp.int32)
    bz_high, bz_low = split_table(back_z)
    sent = call(
        solve_kernel, shape(NX, 16 * ROWS),
        [
            wave.reshape(1), half.reshape(1),
            signed_wave(NY).astype(np.float32)[None, :], signed_wave(NZ).astype(np.float32)[:, None],
            columns, *split_table(forward_z), *split_table(forward_y),
            np.concatenate([bz_high, bz_high, bz_low], axis=1), *split_table(back_y),
        ],
        (), 2, 1 << 30, 3 << 20,
    )
    mixed = lax.all_to_all(sent, everyone, 0, 0, tiled=True)
    flow = call(fields_kernel, shape(11, ROWS, NX, dtype=f32), [mixed, *split_table(back_x)], (), 0, 1 << 29, 2 << 20)

    weights = call(
        weights_kernel, shape(ALL_PAD, BLOCKS * ALL_PAD),
        [
            directions.astype(np.float32), pad_groups(synthesis, 1),
            pad_groups(projection, 0), pad_groups(turn_projection, 1),
        ],
        (), 0, 1 << 28, 1 << 20,
    )
    center = call(assemble_kernel, shape(ALL_PAD, CELLS), [group_arg, *arrived], (), 1, 0, 4 << 20)
    up = [(i, (i + 1) % SPACES) for i in range(SPACES)]
    z_low = lax.ppermute(center, "space", up)
    z_high = lax.ppermute(center, "space", [(b, a) for a, b in up])
    up = [(i, (i + 1) % GROUPS) for i in range(GROUPS)]
    y_low = lax.ppermute(center[:, -NX:], "harm", up)
    y_high = lax.ppermute(center[:, :NX], "harm", [(b, a) for a, b in up])

    rates = call(
        rate_kernel, shape(GROUPS, OWN, ROWS, NX),
        [center, z_low, z_high, y_low, y_high, flow, weights, pad_groups(damping, 0)[:, None]],
        [
            pltpu.VMEM((ALL_PAD, CELLS + 2 * NX), bf16),
            pltpu.VMEM((BLOCKS * ALL_PAD, NX), bf16),
            pltpu.VMEM((ALL_PAD, NX), f32),
            pltpu.VMEM((ALL_PAD * 16, LANES), f32),
            pltpu.VMEM((ALL_PAD * 16, LANES), f32),
        ],
        0, 7 << 30, 9 << 20,
    )
    back = lax.all_to_all(rates, "harm", 0, 0, tiled=True)
    rate = jnp.moveaxis(back, 0, 1).reshape(OWN, 1, NY, NX)
    return (rate, flow[0:3].reshape(3, 1, ROWS, NX))


def solution(mesh):
    in_specs = (P("harm", "space", None, None), P(), P(), P(), P())
    out_specs = (P("harm", "space", None, None), P(None, "space", "harm", None))
    return jax.shard_map(local, mesh=mesh, in_specs=in_specs, out_specs=out_specs, check_vma=False)
```

```python
import functools
import math

import jax
import jax.numpy as jnp
import ml_dtypes
import numpy as np
from jax import lax
from jax.experimental import pallas as pl
from jax.experimental.pallas import tpu as pltpu
from jax.sharding import PartitionSpec as P

activity = -3.0
swim_speed = 1.0
transl_diff = 0.25
shape_factor = 0.9
golden_angle = math.pi * (3.0 - math.sqrt(5.0))

NX, NY, NZ = 256, 256, 32
COEFS, QUAD = 120, 256
SPACES, GROUPS = 32, 8
OWN = COEFS // GROUPS
PAD = 16
ROWS = NY // GROUPS
CELLS = ROWS * NX
HALF = NX // 2
ALL_PAD = GROUPS * PAD
LANES = 128
RUN = 8
FLIP = GROUPS // 2
PARTS = 2
CHUNK = ROWS // PARTS
BLOCKS = 12
bf16, f32 = jnp.bfloat16, jnp.float32
VMEM = pl.BlockSpec(memory_space=pltpu.VMEM)
SMEM = pl.BlockSpec(memory_space=pltpu.SMEM)
PARAMS = pltpu.CompilerParams(vmem_limit_bytes=56 * 1024 * 1024)


def split_table(table):
    high = table.astype(ml_dtypes.bfloat16)
    low = (table - high.astype(np.float64)).astype(ml_dtypes.bfloat16)
    return (high, low)


def signed_wave(length):
    index = np.arange(length)
    signed = np.where(index < length // 2, index, index - length)
    return 2.0 * math.pi / length * np.where(index == length // 2, 0, signed)


def sphere_directions():
    position = np.arange(QUAD, dtype=np.float64)
    height = 1.0 - (2.0 * position + 1.0) / QUAD
    radius = np.sqrt(1.0 - height * height)
    turning = position * golden_angle
    return np.stack([radius * np.cos(turning), radius * np.sin(turning), height])


def tables():
    x = np.arange(NX)[None, :]
    k = np.arange(HALF)[:, None]
    angle = 2.0 * math.pi * (k * x % NX) / NX
    cos_x, sin_x = np.cos(angle), np.sin(angle)
    sign = (-1.0) ** x[0]
    minus = -sin_x
    minus[0] = sign
    forward_x = np.concatenate([cos_x, minus])
    scale = 1.0 / (NX * NY * NZ)
    weight = np.where(k == 0, 1.0, 2.0) * scale
    wave = 2.0 * math.pi / NX * k
    real_x = weight * cos_x
    imag_x = -weight * sin_x
    imag_x[0] = sign * scale
    slope_real = -weight * wave * sin_x
    slope_imag = -weight * wave * cos_x
    back_x = np.concatenate([real_x, imag_x, slope_real, slope_imag], axis=1)
    back_x = np.concatenate([back_x, back_x])

    z = np.arange(NZ)
    angle = 2.0 * math.pi * (z[:, None] * z[None, :] % NZ) / NZ
    both_z = np.concatenate([np.cos(angle), np.sin(angle)])
    forward_z = np.tile(both_z, (1, GROUPS))

    y = np.arange(HALF)[:, None]
    ky = np.arange(NY)[None, :]
    angle = 2.0 * math.pi * (y * ky % NY) / NY
    forward_y = np.block([[np.cos(angle), -np.sin(angle)], [np.sin(angle), np.cos(angle)]])

    ky = np.arange(NY)[:, None]
    angle = 2.0 * math.pi * (ky * np.arange(NY)[None, :] % NY) / NY
    cos_y = np.cos(angle).reshape(NY, GROUPS, 1, ROWS)
    sin_y = np.sin(angle).reshape(NY, GROUPS, 1, ROWS)
    from_real = np.concatenate([cos_y, sin_y], axis=2).reshape(NY, 2 * NY)
    from_imag = np.concatenate([-sin_y, cos_y], axis=2).reshape(NY, 2 * NY)
    back_y = np.concatenate([from_real, from_imag])
    return forward_x, forward_z, forward_y, both_z, back_y, back_x


def halves(value):
    high = value.astype(bf16)
    return high, (value - high.astype(f32)).astype(bf16)


def dot(a, b):
    return jnp.dot(a, b, preferred_element_type=f32)


def regroup_kernel(block_ref, coef_ref, *refs):
    outs, stages = refs[:GROUPS], refs[GROUPS:]
    block = block_ref[0]
    for stage in stages:
        stage[pl.ds(OWN * ROWS, ROWS), :] = jnp.zeros((ROWS, LANES), f32)
    for j in range(GROUPS):
        first = pl.multiple_of((block ^ j) * ROWS, ROWS)
        rows = coef_ref[:, pl.ds(first, ROWS), :].astype(f32)
        rows = rows.reshape(OWN * ROWS, NX)
        for side, stage in enumerate(stages):
            stage[pl.ds(0, OWN * ROWS), :] = rows[:, side * LANES : (side + 1) * LANES]
            for r in range(ROWS):
                lane = r * NX + side * LANES
                outs[j][:, lane : lane + LANES] = stage[pl.ds(r, PAD, stride=ROWS), :].astype(bf16)


def stress_kernel(table_ref, coef_ref, high_ref, low_ref, out_ref, stress_high, stress_low):
    step = 32

    def rows(i, carry):
        first = pl.multiple_of(i * step, step)
        sums = [jnp.zeros((step, NX), f32)] * 5
        for c in range(OWN):
            value = coef_ref[c, pl.ds(first, step), :].astype(f32)
            sums = [s + table_ref[r, c] * value for r, s in enumerate(sums)]
        for r in range(5):
            high, low = halves(sums[r])
            stress_high[r, pl.ds(first, step), :] = high
            stress_low[r, pl.ds(first, step), :] = low
        return carry

    lax.fori_loop(0, NY // step, rows, 0)

    def across(a, b):
        return lax.dot_general(a, b, (((1,), (1,)), ((), ())), preferred_element_type=f32)

    for r in range(5):
        high, low = high_ref[...], low_ref[...]
        result = (
            across(high, stress_high[r]) + across(low, stress_high[r]) + across(high, stress_low[r])
        ).astype(bf16)
        for half in range(2):
            for part in range(2):
                lane = (2 * r + part) * HALF
                out_ref[half * HALF : (half + 1) * HALF, lane : lane + HALF] = result[
                    part * HALF : (part + 1) * HALF, half * HALF : (half + 1) * HALF
                ]


def solve_kernel(
    wave_ref, half_ref, ky_ref, kz_ref, recv_ref,
    fz_high, fz_low, fy_high, fy_low, bz, by_high, by_low, out_ref,
):
    recv = recv_ref[...]
    by_z = dot(fz_high[...], recv) + dot(fz_low[...], recv)
    lines = []
    for r in range(5):
        lane = 2 * r * HALF
        cos_re, cos_im = by_z[:NZ, lane : lane + HALF], by_z[:NZ, lane + HALF : lane + 2 * HALF]
        sin_re, sin_im = by_z[NZ:, lane : lane + HALF], by_z[NZ:, lane + HALF : lane + 2 * HALF]
        lines.append(jnp.concatenate([cos_re + sin_im, cos_im - sin_re], axis=1))
    high, low = halves(jnp.concatenate(lines))
    spec = dot(high, fy_high[...]) + dot(low, fy_high[...]) + dot(high, fy_low[...])
    lane = lax.broadcasted_iota(jnp.int32, (NZ, NY), 1)
    flip = jnp.where((lane % 2) * half_ref[0] == 1, -1.0, 1.0)
    real = [spec[r * NZ : (r + 1) * NZ, :NY] * flip for r in range(5)]
    imag = [spec[r * NZ : (r + 1) * NZ, NY:] * flip for r in range(5)]
    kx = jnp.full((NZ, NY), wave_ref[0], f32)
    ky = jnp.broadcast_to(ky_ref[...], (NZ, NY))
    kz = jnp.broadcast_to(kz_ref[...], (NZ, NY))
    square = kx * kx + ky * ky + kz * kz
    inverse = jnp.where(square > 0, 1.0 / jnp.where(square > 0, square, 1.0), 0.0)

    def force(part):
        xx, yy, xy, xz, yz = part
        return (
            kx * xx + ky * xy + kz * xz,
            kx * xy + ky * yy + kz * yz,
            kx * xz + ky * yz,
        )

    def solve(f):
        along = (kx * f[0] + ky * f[1] + kz * f[2]) * inverse
        return [(f[i] - k * along) * inverse for i, k in enumerate((kx, ky, kz))]

    flow_re = solve([-f for f in force(imag)])
    flow_im = solve(force(real))
    fields = list(zip(flow_re, flow_im))
    fields += [(-ky * flow_im[i], ky * flow_re[i]) for i in range(3)]
    fields += [(-kz * flow_im[i], kz * flow_re[i]) for i in range(2)]
    back = []
    for re, im in fields:
        high, low = halves(jnp.concatenate([re, im], axis=1))
        both = dot(bz[...], jnp.concatenate([high, low, high]))
        back.append(
            jnp.concatenate(
                [both[:NZ, :NY] - both[NZ:, NY:], both[:NZ, NY:] + both[NZ:, :NY]], axis=1
            )
        )
    high, low = halves(jnp.concatenate(back))
    done = dot(high, by_high[...]) + dot(low, by_high[...]) + dot(high, by_low[...])
    blocks = []
    for h in range(GROUPS):
        lane = 2 * ROWS * h
        pieces = [done[f * NZ : (f + 1) * NZ, lane : lane + 2 * ROWS] for f in range(8)]
        blocks.append(jnp.concatenate(pieces, axis=1))
    plane = lax.broadcasted_iota(jnp.int32, blocks[0].shape, 0)
    flipped = (plane // RUN) % 2 == 1
    for h in range(GROUPS):
        value = jnp.where(flipped, blocks[h ^ FLIP], blocks[h])
        out_ref[h * NZ : (h + 1) * NZ, :] = value.astype(bf16)


def fields_kernel(recv_ref, high_ref, low_ref, out_ref):
    flat = recv_ref[...].astype(f32).T.astype(bf16)
    both = dot(flat, high_ref[...]) + dot(flat, low_ref[...])

    def field(f, lane):
        row = 2 * ROWS * f
        return (
            both[row : row + ROWS, lane : lane + NX]
            + both[row + ROWS : row + 2 * ROWS, lane + NX : lane + 2 * NX]
        )

    for i in range(3):
        out_ref[i] = field(i, 0)
        out_ref[3 + i] = field(i, 2 * NX)
    for i in range(5):
        out_ref[6 + i] = field(3 + i, 0)


def weights_kernel(dir_ref, synth_ref, proj_ref, turn_ref, out_ref):
    synth = synth_ref[...]
    p = [dir_ref[j : j + 1, :] for j in range(3)]
    proj = proj_ref[...].astype(f32)
    turn = [turn_ref[k].astype(f32) for k in range(3)]
    radial = turn[0] * p[0] + turn[1] * p[1] + turn[2] * p[2]
    same = 0.5 * (shape_factor + 1.0)
    swap = 0.5 * (shape_factor - 1.0)

    def plain(i, j):
        return turn[i] * p[j] - radial * (p[i] * p[j])

    def strain(i, j):
        return same * plain(i, j) + swap * plain(j, i)

    left = [-0.5 * swim_speed * proj * p[j] for j in range(3)] + [-0.5 * proj]
    trace = strain(2, 2)
    left += [strain(0, 0) - trace, strain(1, 0), strain(2, 0)]
    left += [strain(0, 1), strain(1, 1) - trace, strain(2, 1)]
    left += [strain(0, 2), strain(1, 2)]
    for n, value in enumerate(left):
        high, low = halves(value)
        out_ref[:, n * ALL_PAD : (n + 1) * ALL_PAD] = (dot(high, synth) + dot(low, synth)).astype(bf16)


def assemble_kernel(group_ref, *refs):
    out_ref = refs[GROUPS]
    group = group_ref[0]
    for j in range(GROUPS):
        out_ref[pl.ds(pl.multiple_of((group ^ j) * PAD, PAD), PAD), :] = refs[j][...]


def rate_kernel(
    group_ref, center_ref, zlow_ref, zhigh_ref, ylow_ref, yhigh_ref, flow_ref, weight_ref, damp_ref,
    *refs,
):
    outs, (padded, operands, locals_, *stages) = refs[:GROUPS], refs[GROUPS:]
    group = group_ref[0]
    cells = CHUNK * NX
    padded[:, :NX] = ylow_ref[...]
    padded[:, NX : NX + cells] = center_ref[...]
    padded[:, NX + cells :] = yhigh_ref[...]

    def build(r, operand, local_terms):
        here = pl.multiple_of(r * NX, NX)
        flow = [flow_ref[f, pl.ds(r, 1), :] for f in range(11)]
        for g in range(GROUPS):
            rows = slice(g * PAD, (g + 1) * PAD)
            value = padded[rows, pl.ds(here + NX, NX)].astype(f32)
            y_low = padded[rows, pl.ds(here, NX)].astype(f32)
            y_high = padded[rows, pl.ds(here + 2 * NX, NX)].astype(f32)
            z_low = zlow_ref[rows, pl.ds(here, NX)].astype(f32)
            z_high = zhigh_ref[rows, pl.ds(here, NX)].astype(f32)
            x_low = pltpu.roll(value, 1, 1)
            x_high = pltpu.roll(value, NX - 1, 1)
            diffs = (x_high - x_low, y_high - y_low, z_high - z_low)
            drift = flow[0] * diffs[0] + flow[1] * diffs[1] + flow[2] * diffs[2]
            lap = x_high + x_low + y_high + y_low + z_high + z_low - 6.0 * value
            local_terms[rows, :] = transl_diff * lap - damp_ref[rows, :] * value
            terms = list(diffs) + [drift] + [flow[3 + n] * value for n in range(8)]
            for n, term in enumerate(terms):
                operand[n * ALL_PAD + g * PAD : n * ALL_PAD + (g + 1) * PAD, :] = term.astype(bf16)

    def rows(i, carry):
        for n in range(2):
            build(2 * i + n, operands.at[n], locals_.at[n])
        for n in range(2):
            result = dot(weight_ref[...], operands[n]) + locals_[n]
            for side, stage in enumerate(stages):
                stage[pl.ds(2 * i + n, ALL_PAD, stride=CHUNK), :] = result[
                    :, side * LANES : (side + 1) * LANES
                ]
        return carry

    lax.fori_loop(0, CHUNK // 2, rows, 0)
    for j in range(GROUPS):
        for c in range(OWN):
            first = pl.multiple_of(((group ^ j) * PAD + c) * CHUNK, CHUNK)
            for side, stage in enumerate(stages):
                outs[j][c, :, side * LANES : (side + 1) * LANES] = stage[
                    pl.ds(first, CHUNK), :
                ].astype(bf16)


def place_kernel(block_ref, *refs):
    out_ref = refs[-1]
    for part in range(PARTS):
        for j in range(GROUPS):
            first = pl.multiple_of((block_ref[0] ^ j) * ROWS + part * CHUNK, CHUNK)
            out_ref[:, pl.ds(first, CHUNK), :] = refs[part * GROUPS + j][...]


def call(kernel, out_shape, ins, scratch=(), scalars=0, flops=0, byte_count=0, specs=None):
    return pl.pallas_call(
        kernel,
        out_shape=out_shape,
        grid=(1,) if specs else (),
        in_specs=specs or [SMEM] * scalars + [VMEM] * (len(ins) - scalars),
        out_specs=jax.tree.map(lambda _: VMEM, out_shape),
        scratch_shapes=list(scratch),
        compiler_params=PARAMS,
        cost_estimate=pl.CostEstimate(flops=flops, bytes_accessed=byte_count, transcendentals=0),
    )(*ins)


def shape(*dims, dtype=bf16):
    return jax.ShapeDtypeStruct(dims, dtype)


def pad_groups(value, axis):
    parts = value.reshape(*value.shape[:axis], GROUPS, OWN, *value.shape[axis + 1 :])
    widths = [(0, 0)] * parts.ndim
    widths[axis + 1] = (0, PAD - OWN)
    parts = jnp.pad(parts, widths)
    return parts.reshape(*value.shape[:axis], ALL_PAD, *value.shape[axis + 1 :])


def stress_table(synthesis, directions, group):
    dir_x, dir_y, dir_z = directions
    third = 1.0 / 3.0
    moments = np.stack(
        [
            dir_x * dir_x - third,
            dir_y * dir_y - third,
            dir_z * dir_z - third,
            dir_x * dir_y,
            dir_x * dir_z,
            dir_y * dir_z,
        ]
    ).astype(np.float32)
    own = lax.dynamic_slice_in_dim(synthesis, group * OWN, OWN, 1).astype(f32)
    table = jnp.dot(moments, own, precision=lax.Precision.HIGHEST)
    table = (table * (activity / math.sqrt(QUAD))).astype(bf16).astype(f32)
    return jnp.concatenate([table[0:2] - table[2:3], table[3:6]])


def odd(plane):
    return (plane // RUN) % 2


def pairs(target):
    found = []
    for plane in range(SPACES):
        for group in range(GROUPS):
            to_plane, to_block = target(plane, group ^ (FLIP * odd(plane)))
            to_group = to_block ^ (FLIP * odd(to_plane))
            found.append((plane * GROUPS + group, to_plane * GROUPS + to_group))
    return found


def local(coeffs, synthesis, projection, turn_projection, damping):
    group = lax.axis_index("harm")
    plane = lax.axis_index("space")
    both = ("space", "harm")
    everyone = ("harm", "space")
    position = group * SPACES + plane
    forward_x, forward_z, forward_y, back_z, back_y, back_x = tables()
    directions = sphere_directions()
    own = coeffs.reshape(OWN, NY, NX)
    group_arg = group.astype(jnp.int32).reshape(1)
    block_arg = group_arg ^ (FLIP * odd(plane)).astype(jnp.int32)

    table = stress_table(synthesis, directions, group)
    high, low = split_table(forward_x)
    sent = call(
        stress_kernel, shape(NX, 10 * HALF), [table, own, high, low],
        [pltpu.VMEM((5, NY, NX), bf16)] * 2, 1, 1 << 30, 3 << 20,
    )
    columns = lax.all_to_all(sent, everyone, 0, 0, tiled=True)

    later, _ = lax.optimization_barrier((own, sent))
    chunks = call(
        regroup_kernel, [shape(PAD, CELLS)] * GROUPS, [block_arg, later],
        [pltpu.VMEM((PAD * ROWS, LANES), f32)] * 2, 1, 0, 4 << 20,
    )
    arrived = [chunks[0]]
    for j in range(1, GROUPS):
        arrived.append(lax.ppermute(chunks[j], "harm", [(i, i ^ j) for i in range(GROUPS)]))

    wave = (position % HALF).astype(f32) * (2.0 * math.pi / NX)
    half = (position // HALF).astype(jnp.int32)
    bz_high, bz_low = split_table(back_z)
    sent = call(
        solve_kernel, shape(NX, 16 * ROWS),
        [
            wave.reshape(1), half.reshape(1),
            signed_wave(NY).astype(np.float32)[None, :], signed_wave(NZ).astype(np.float32)[:, None],
            columns, *split_table(forward_z), *split_table(forward_y),
            np.concatenate([bz_high, bz_high, bz_low], axis=1), *split_table(back_y),
        ],
        (), 2, 1 << 30, 3 << 20,
    )
    mixed = lax.all_to_all(sent, everyone, 0, 0, tiled=True)
    arrived, _ = lax.optimization_barrier((arrived, sent))
    center = call(assemble_kernel, shape(ALL_PAD, CELLS), [group_arg, *arrived], (), 1, 0, 4 << 20)
    z_low = lax.ppermute(center, both, pairs(lambda s, b: ((s + 1) % SPACES, b)))
    z_high = lax.ppermute(center, both, pairs(lambda s, b: ((s - 1) % SPACES, b)))
    y_low = lax.ppermute(center[:, -NX:], both, pairs(lambda s, b: (s, (b + 1) % GROUPS)))
    y_high = lax.ppermute(center[:, :NX], both, pairs(lambda s, b: (s, (b - 1) % GROUPS)))

    weights = call(
        weights_kernel, shape(ALL_PAD, BLOCKS * ALL_PAD),
        [
            directions.astype(np.float32), pad_groups(synthesis, 1),
            pad_groups(projection, 0), pad_groups(turn_projection, 1),
        ],
        (), 0, 1 << 28, 1 << 20,
    )
    flow = call(fields_kernel, shape(11, ROWS, NX, dtype=f32), [mixed, *split_table(back_x)], (), 0, 1 << 29, 2 << 20)
    damp = pad_groups(damping, 0)[:, None]
    returned, parts = [], []
    for part in range(PARTS):
        here = pl.BlockSpec((ALL_PAD, CHUNK * NX), lambda i, part=part: (0, part))
        first, last = part * CHUNK, (part + 1) * CHUNK

        def edge(row):
            return pl.BlockSpec((ALL_PAD, NX), lambda i: (0, row))

        low = (y_low, VMEM) if first == 0 else (center, edge(first - 1))
        high = (y_high, VMEM) if last == ROWS else (center, edge(last))
        rates = call(
            rate_kernel, [shape(OWN, CHUNK, NX)] * GROUPS,
            [group_arg, center, z_low, z_high, low[0], high[0], flow, weights, damp],
            [
                pltpu.VMEM((ALL_PAD, (CHUNK + 2) * NX), bf16),
                pltpu.VMEM((2, BLOCKS * ALL_PAD, NX), bf16),
                pltpu.VMEM((2, ALL_PAD, NX), f32),
                pltpu.VMEM((ALL_PAD * CHUNK, LANES), f32),
                pltpu.VMEM((ALL_PAD * CHUNK, LANES), f32),
            ],
            1, 7 << 29, 9 << 19,
            [
                SMEM, here, here, here, low[1], high[1],
                pl.BlockSpec((11, CHUNK, NX), lambda i, part=part: (0, part, 0)), VMEM, VMEM,
            ],
        )
        parts.append(rates[0])
        returned.append(rates[0])
        for j in range(1, GROUPS):
            returned.append(lax.ppermute(rates[j], "harm", [(i, i ^ j) for i in range(GROUPS)]))
    swap = pairs(lambda s, b: (s, b ^ (FLIP * odd(s))))
    late, _ = lax.optimization_barrier((flow[0:3], parts))
    velocity = lax.ppermute(late, both, swap)
    rate = call(place_kernel, shape(OWN, NY, NX), [block_arg, *returned], (), 1, 0, 4 << 20)
    return (rate.reshape(OWN, 1, NY, NX), velocity.reshape(3, 1, ROWS, NX))


def solution(mesh):
    in_specs = (P("harm", "space", None, None), P(), P(), P(), P())
    out_specs = (P("harm", "space", None, None), P(None, "space", "harm", None))
    return jax.shard_map(local, mesh=mesh, in_specs=in_specs, out_specs=out_specs, check_vma=False)
```

```python
import functools
import math

import jax
import jax.numpy as jnp
import ml_dtypes
import numpy as np
from jax import lax
from jax.experimental import pallas as pl
from jax.experimental.pallas import tpu as pltpu
from jax.sharding import PartitionSpec as P

activity = -3.0
swim_speed = 1.0
transl_diff = 0.25
shape_factor = 0.9
golden_angle = math.pi * (3.0 - math.sqrt(5.0))

NX, NY, NZ = 256, 256, 32
COEFS, QUAD = 120, 256
SPACES, GROUPS = 32, 8
OWN = COEFS // GROUPS
PAD = 16
ROWS = NY // GROUPS
EDGED = ROWS + 2
CELLS = EDGED * NX
HALF = NX // 2
ALL_PAD = GROUPS * PAD
LANES = 128
RUN = 8
FLIP = GROUPS // 2
PARTS = 2
CHUNK = ROWS // PARTS
BLOCKS = 13
bf16, f32 = jnp.bfloat16, jnp.float32
VMEM = pl.BlockSpec(memory_space=pltpu.VMEM)
SMEM = pl.BlockSpec(memory_space=pltpu.SMEM)
PARAMS = pltpu.CompilerParams(vmem_limit_bytes=56 * 1024 * 1024)


def split_table(table):
    high = table.astype(ml_dtypes.bfloat16)
    low = (table - high.astype(np.float64)).astype(ml_dtypes.bfloat16)
    return (high, low)


def signed_wave(length):
    index = np.arange(length)
    signed = np.where(index < length // 2, index, index - length)
    return 2.0 * math.pi / length * np.where(index == length // 2, 0, signed)


def sphere_directions():
    position = np.arange(QUAD, dtype=np.float64)
    height = 1.0 - (2.0 * position + 1.0) / QUAD
    radius = np.sqrt(1.0 - height * height)
    turning = position * golden_angle
    return np.stack([radius * np.cos(turning), radius * np.sin(turning), height])


def tables():
    x = np.arange(NX)[None, :]
    k = np.arange(HALF)[:, None]
    angle = 2.0 * math.pi * (k * x % NX) / NX
    cos_x, sin_x = np.cos(angle), np.sin(angle)
    sign = (-1.0) ** x[0]
    minus = -sin_x
    minus[0] = sign
    forward_x = np.concatenate([cos_x, minus])
    scale = 1.0 / (NX * NY * NZ)
    weight = np.where(k == 0, 1.0, 2.0) * scale
    wave = 2.0 * math.pi / NX * k
    real_x = weight * cos_x
    imag_x = -weight * sin_x
    imag_x[0] = sign * scale
    slope_real = -weight * wave * sin_x
    slope_imag = -weight * wave * cos_x
    back_x = np.concatenate([real_x, imag_x, slope_real, slope_imag], axis=1)
    back_x = np.concatenate([back_x, back_x])

    z = np.arange(NZ)
    angle = 2.0 * math.pi * (z[:, None] * z[None, :] % NZ) / NZ
    both_z = np.concatenate([np.cos(angle), np.sin(angle)])
    forward_z = np.tile(both_z, (1, GROUPS))

    y = np.arange(HALF)[:, None]
    ky = np.arange(NY)[None, :]
    angle = 2.0 * math.pi * (y * ky % NY) / NY
    forward_y = np.block([[np.cos(angle), -np.sin(angle)], [np.sin(angle), np.cos(angle)]])

    ky = np.arange(NY)[:, None]
    angle = 2.0 * math.pi * (ky * np.arange(NY)[None, :] % NY) / NY
    cos_y = np.cos(angle).reshape(NY, GROUPS, 1, ROWS)
    sin_y = np.sin(angle).reshape(NY, GROUPS, 1, ROWS)
    from_real = np.concatenate([cos_y, sin_y], axis=2).reshape(NY, 2 * NY)
    from_imag = np.concatenate([-sin_y, cos_y], axis=2).reshape(NY, 2 * NY)
    back_y = np.concatenate([from_real, from_imag])
    return forward_x, forward_z, forward_y, both_z, back_y, back_x


def halves(value):
    high = value.astype(bf16)
    return high, (value - high.astype(f32)).astype(bf16)


def dot(a, b):
    return jnp.dot(a, b, preferred_element_type=f32)


def regroup_kernel(block_ref, coef_ref, *refs):
    near, far, stages = refs[:FLIP], refs[FLIP], refs[FLIP + 1 :]
    block = block_ref[0]
    height = ROWS + 2 * PAD
    for stage in stages:
        stage[pl.ds(OWN * height, height), :] = jnp.zeros((height, LANES), f32)
    for j in range(GROUPS):
        first = (block ^ j) * ROWS
        for start, size, at in ((NY - PAD, PAD, 0), (0, ROWS, PAD), (ROWS, PAD, PAD + ROWS)):
            rows = coef_ref[:, pl.ds(pl.multiple_of((first + start) % NY, PAD), size), :].astype(f32)
            for side, stage in enumerate(stages):
                for c in range(OWN):
                    stage[c * height + at : c * height + at + size, :] = rows[
                        c, :, side * LANES : (side + 1) * LANES
                    ]
        for side, stage in enumerate(stages):
            for r in range(EDGED):
                lane = r * NX + side * LANES
                rows = stage[pl.ds(PAD - 1 + r, PAD, stride=height), :]
                if j < FLIP:
                    near[j][:, lane : lane + LANES] = rows.astype(bf16)
                else:
                    far[(j - FLIP) * PAD : (j - FLIP + 1) * PAD, lane : lane + LANES] = rows.astype(bf16)


def stress_kernel(table_ref, coef_ref, high_ref, low_ref, out_ref, stress_high, stress_low):
    step = 32

    def rows(i, carry):
        first = pl.multiple_of(i * step, step)
        sums = [jnp.zeros((step, NX), f32)] * 5
        for c in range(OWN):
            value = coef_ref[c, pl.ds(first, step), :].astype(f32)
            sums = [s + table_ref[r, c] * value for r, s in enumerate(sums)]
        for r in range(5):
            high, low = halves(sums[r])
            stress_high[r, pl.ds(first, step), :] = high
            stress_low[r, pl.ds(first, step), :] = low
        return carry

    lax.fori_loop(0, NY // step, rows, 0)

    def across(a, b):
        return lax.dot_general(a, b, (((1,), (1,)), ((), ())), preferred_element_type=f32)

    for r in range(5):
        high, low = high_ref[...], low_ref[...]
        result = (
            across(high, stress_high[r]) + across(low, stress_high[r]) + across(high, stress_low[r])
        ).astype(bf16)
        for half in range(2):
            for part in range(2):
                lane = (2 * r + part) * HALF
                out_ref[half * HALF : (half + 1) * HALF, lane : lane + HALF] = result[
                    part * HALF : (part + 1) * HALF, half * HALF : (half + 1) * HALF
                ]


def solve_kernel(
    wave_ref, half_ref, ky_ref, kz_ref, recv_ref,
    fz_high, fz_low, fy_high, fy_low, bz, by_high, by_low, out_ref,
):
    recv = recv_ref[...]
    by_z = dot(fz_high[...], recv) + dot(fz_low[...], recv)
    lines = []
    for r in range(5):
        lane = 2 * r * HALF
        cos_re, cos_im = by_z[:NZ, lane : lane + HALF], by_z[:NZ, lane + HALF : lane + 2 * HALF]
        sin_re, sin_im = by_z[NZ:, lane : lane + HALF], by_z[NZ:, lane + HALF : lane + 2 * HALF]
        lines.append(jnp.concatenate([cos_re + sin_im, cos_im - sin_re], axis=1))
    high, low = halves(jnp.concatenate(lines))
    spec = dot(high, fy_high[...]) + dot(low, fy_high[...]) + dot(high, fy_low[...])
    lane = lax.broadcasted_iota(jnp.int32, (NZ, NY), 1)
    flip = jnp.where((lane % 2) * half_ref[0] == 1, -1.0, 1.0)
    real = [spec[r * NZ : (r + 1) * NZ, :NY] * flip for r in range(5)]
    imag = [spec[r * NZ : (r + 1) * NZ, NY:] * flip for r in range(5)]
    kx = jnp.full((NZ, NY), wave_ref[0], f32)
    ky = jnp.broadcast_to(ky_ref[...], (NZ, NY))
    kz = jnp.broadcast_to(kz_ref[...], (NZ, NY))
    square = kx * kx + ky * ky + kz * kz
    inverse = jnp.where(square > 0, 1.0 / jnp.where(square > 0, square, 1.0), 0.0)

    def force(part):
        xx, yy, xy, xz, yz = part
        return (
            kx * xx + ky * xy + kz * xz,
            kx * xy + ky * yy + kz * yz,
            kx * xz + ky * yz,
        )

    def solve(f):
        along = (kx * f[0] + ky * f[1] + kz * f[2]) * inverse
        return [(f[i] - k * along) * inverse for i, k in enumerate((kx, ky, kz))]

    flow_re = solve([-f for f in force(imag)])
    flow_im = solve(force(real))
    fields = list(zip(flow_re, flow_im))
    fields += [(-ky * flow_im[i], ky * flow_re[i]) for i in range(3)]
    fields += [(-kz * flow_im[i], kz * flow_re[i]) for i in range(2)]
    back = []
    for re, im in fields:
        high, low = halves(jnp.concatenate([re, im], axis=1))
        both = dot(bz[...], jnp.concatenate([high, low, high]))
        back.append(
            jnp.concatenate(
                [both[:NZ, :NY] - both[NZ:, NY:], both[:NZ, NY:] + both[NZ:, :NY]], axis=1
            )
        )
    high, low = halves(jnp.concatenate(back))
    done = dot(high, by_high[...]) + dot(low, by_high[...]) + dot(high, by_low[...])
    blocks = []
    for h in range(GROUPS):
        lane = 2 * ROWS * h
        pieces = [done[f * NZ : (f + 1) * NZ, lane : lane + 2 * ROWS] for f in range(8)]
        blocks.append(jnp.concatenate(pieces, axis=1))
    plane = lax.broadcasted_iota(jnp.int32, blocks[0].shape, 0)
    flipped = (plane // RUN) % 2 == 1
    for h in range(GROUPS):
        value = jnp.where(flipped, blocks[h ^ FLIP], blocks[h])
        out_ref[h * NZ : (h + 1) * NZ, :] = value.astype(bf16)


def fields_kernel(recv_ref, high_ref, low_ref, out_ref):
    flat = recv_ref[...].astype(f32).T.astype(bf16)
    both = dot(flat, high_ref[...]) + dot(flat, low_ref[...])

    def field(f, lane):
        row = 2 * ROWS * f
        return (
            both[row : row + ROWS, lane : lane + NX]
            + both[row + ROWS : row + 2 * ROWS, lane + NX : lane + 2 * NX]
        )

    for i in range(3):
        out_ref[i] = field(i, 0)
        out_ref[3 + i] = field(i, 2 * NX)
    for i in range(5):
        out_ref[6 + i] = field(3 + i, 0)


def weights_kernel(dir_ref, synth_ref, proj_ref, turn_ref, out_ref):
    synth = synth_ref[...]
    p = [dir_ref[j : j + 1, :] for j in range(3)]
    proj = proj_ref[...].astype(f32)
    turn = [turn_ref[k].astype(f32) for k in range(3)]
    radial = turn[0] * p[0] + turn[1] * p[1] + turn[2] * p[2]
    same = 0.5 * (shape_factor + 1.0)
    swap = 0.5 * (shape_factor - 1.0)

    def plain(i, j):
        return turn[i] * p[j] - radial * (p[i] * p[j])

    def strain(i, j):
        return same * plain(i, j) + swap * plain(j, i)

    left = [-0.5 * swim_speed * proj * p[j] for j in range(2)] + [-0.5 * proj]
    trace = strain(2, 2)
    left += [strain(0, 0) - trace, strain(1, 0), strain(2, 0)]
    left += [strain(0, 1), strain(1, 1) - trace, strain(2, 1)]
    left += [strain(0, 2), strain(1, 2)]
    left += [-0.5 * swim_speed * proj * p[2], -0.5 * proj]
    for n, value in enumerate(left):
        high, low = halves(value)
        out_ref[:, n * ALL_PAD : (n + 1) * ALL_PAD] = (dot(high, synth) + dot(low, synth)).astype(bf16)


def assemble_kernel(group_ref, *refs):
    out_ref = refs[GROUPS]
    group = group_ref[0]
    for j in range(GROUPS):
        out_ref[pl.ds(pl.multiple_of((group ^ j) * PAD, PAD), PAD), :] = refs[j][...]


def inner_kernel(center_ref, flow_ref, weight_ref, damp_ref, out_ref, operands, locals_):
    blocks = BLOCKS - 2

    def build(r, operand, local_terms):
        here = pl.multiple_of(r * NX, NX)
        flow = [flow_ref[f, pl.ds(r, 1), :] for f in range(11)]
        for g in range(GROUPS):
            rows = slice(g * PAD, (g + 1) * PAD)
            value = center_ref[rows, pl.ds(here + NX, NX)].astype(f32)
            y_low = center_ref[rows, pl.ds(here, NX)].astype(f32)
            y_high = center_ref[rows, pl.ds(here + 2 * NX, NX)].astype(f32)
            x_low = pltpu.roll(value, 1, 1)
            x_high = pltpu.roll(value, NX - 1, 1)
            diff_x, diff_y = x_high - x_low, y_high - y_low
            lap = x_high + x_low + y_high + y_low - 6.0 * value
            local_terms[rows, :] = transl_diff * lap - damp_ref[rows, :] * value
            terms = [diff_x, diff_y, flow[0] * diff_x + flow[1] * diff_y]
            terms += [flow[3 + n] * value for n in range(8)]
            for n, term in enumerate(terms):
                operand[n * ALL_PAD + g * PAD : n * ALL_PAD + (g + 1) * PAD, :] = term.astype(bf16)

    def rows(i, carry):
        for n in range(2):
            build(2 * i + n, operands.at[n], locals_.at[n])
        for n in range(2):
            where = pl.ds(pl.multiple_of((2 * i + n) * NX, NX), NX)
            out_ref[:, where] = locals_[n] + dot(weight_ref[:, : blocks * ALL_PAD], operands[n])
        return carry

    lax.fori_loop(0, ROWS // 2, rows, 0)


def rate_kernel(group_ref, inner_ref, zlow_ref, zhigh_ref, flow_ref, weight_ref, *refs):
    outs, (operands, locals_, *stages) = refs[:GROUPS], refs[GROUPS:]
    group = group_ref[0]
    skip = (BLOCKS - 2) * ALL_PAD

    def build(r, operand, local_terms):
        here = pl.multiple_of(r * NX, NX)
        drift = flow_ref[2, pl.ds(r, 1), :]
        for g in range(GROUPS):
            rows = slice(g * PAD, (g + 1) * PAD)
            z_low = zlow_ref[rows, pl.ds(here, NX)].astype(f32)
            z_high = zhigh_ref[rows, pl.ds(here, NX)].astype(f32)
            diff_z = z_high - z_low
            local_terms[rows, :] = transl_diff * (z_high + z_low) + inner_ref[rows, pl.ds(here, NX)]
            operand[rows, :] = diff_z.astype(bf16)
            operand[ALL_PAD + g * PAD : ALL_PAD + (g + 1) * PAD, :] = (drift * diff_z).astype(bf16)

    def rows(i, carry):
        for n in range(2):
            build(2 * i + n, operands.at[n], locals_.at[n])
        for n in range(2):
            result = dot(weight_ref[:, skip:], operands[n]) + locals_[n]
            for side, stage in enumerate(stages):
                stage[pl.ds(2 * i + n, ALL_PAD, stride=CHUNK), :] = result[
                    :, side * LANES : (side + 1) * LANES
                ]
        return carry

    lax.fori_loop(0, CHUNK // 2, rows, 0)
    for j in range(GROUPS):
        for c in range(OWN):
            first = pl.multiple_of(((group ^ j) * PAD + c) * CHUNK, CHUNK)
            for side, stage in enumerate(stages):
                outs[j][c, :, side * LANES : (side + 1) * LANES] = stage[
                    pl.ds(first, CHUNK), :
                ].astype(bf16)


def place_kernel(block_ref, *refs):
    out_ref = refs[-1]
    for part in range(PARTS):
        for j in range(GROUPS):
            first = pl.multiple_of((block_ref[0] ^ j) * ROWS + part * CHUNK, CHUNK)
            out_ref[:, pl.ds(first, CHUNK), :] = refs[part * GROUPS + j][...]


def call(kernel, out_shape, ins, scratch=(), scalars=0, flops=0, byte_count=0, specs=None):
    return pl.pallas_call(
        kernel,
        out_shape=out_shape,
        grid=(1,) if specs else (),
        in_specs=specs or [SMEM] * scalars + [VMEM] * (len(ins) - scalars),
        out_specs=jax.tree.map(lambda _: VMEM, out_shape),
        scratch_shapes=list(scratch),
        compiler_params=PARAMS,
        cost_estimate=pl.CostEstimate(flops=flops, bytes_accessed=byte_count, transcendentals=0),
    )(*ins)


def shape(*dims, dtype=bf16):
    return jax.ShapeDtypeStruct(dims, dtype)


def pad_groups(value, axis):
    parts = value.reshape(*value.shape[:axis], GROUPS, OWN, *value.shape[axis + 1 :])
    widths = [(0, 0)] * parts.ndim
    widths[axis + 1] = (0, PAD - OWN)
    parts = jnp.pad(parts, widths)
    return parts.reshape(*value.shape[:axis], ALL_PAD, *value.shape[axis + 1 :])


def stress_table(synthesis, directions, group):
    dir_x, dir_y, dir_z = directions
    third = 1.0 / 3.0
    moments = np.stack(
        [
            dir_x * dir_x - third,
            dir_y * dir_y - third,
            dir_z * dir_z - third,
            dir_x * dir_y,
            dir_x * dir_z,
            dir_y * dir_z,
        ]
    ).astype(np.float32)
    own = lax.dynamic_slice_in_dim(synthesis, group * OWN, OWN, 1).astype(f32)
    table = jnp.dot(moments, own, precision=lax.Precision.HIGHEST)
    table = (table * (activity / math.sqrt(QUAD))).astype(bf16).astype(f32)
    return jnp.concatenate([table[0:2] - table[2:3], table[3:6]])


def partner(j):
    return [(i, i ^ j) for i in range(GROUPS)]


def exchanged(chunks):
    return [chunks[0]] + [lax.ppermute(c, "harm", partner(j + 1)) for j, c in enumerate(chunks[1:])]


def odd(plane):
    return (plane // RUN) % 2


def pairs(target):
    found = []
    for plane in range(SPACES):
        for group in range(GROUPS):
            to_plane, to_block = target(plane, group ^ (FLIP * odd(plane)))
            to_group = to_block ^ (FLIP * odd(to_plane))
            found.append((plane * GROUPS + group, to_plane * GROUPS + to_group))
    return found


def local(coeffs, synthesis, projection, turn_projection, damping):
    group = lax.axis_index("harm")
    plane = lax.axis_index("space")
    both = ("space", "harm")
    everyone = ("harm", "space")
    position = group * SPACES + plane
    forward_x, forward_z, forward_y, back_z, back_y, back_x = tables()
    directions = sphere_directions()
    own = coeffs.reshape(OWN, NY, NX)
    group_arg = group.astype(jnp.int32).reshape(1)
    block_arg = group_arg ^ (FLIP * odd(plane)).astype(jnp.int32)

    table = stress_table(synthesis, directions, group)
    high, low = split_table(forward_x)
    sent = call(
        stress_kernel, shape(NX, 10 * HALF), [table, own, high, low],
        [pltpu.VMEM((5, NY, NX), bf16)] * 2, 1, 1 << 30, 3 << 20,
    )
    columns = lax.all_to_all(sent, everyone, 0, 0, tiled=True)

    later, _ = lax.optimization_barrier((own, sent))
    chunks = call(
        regroup_kernel, [shape(PAD, CELLS)] * FLIP + [shape(FLIP * PAD, CELLS)], [block_arg, later],
        [pltpu.VMEM((PAD * (ROWS + 2 * PAD), LANES), f32)] * 2, 1, 0, 4 << 20,
    )
    crossed = lax.ppermute(chunks[FLIP], "harm", partner(FLIP))
    arrived = exchanged(chunks[:FLIP])
    arrived += exchanged([crossed[m * PAD : (m + 1) * PAD] for m in range(FLIP)])

    wave = (position % HALF).astype(f32) * (2.0 * math.pi / NX)
    half = (position // HALF).astype(jnp.int32)
    bz_high, bz_low = split_table(back_z)
    sent = call(
        solve_kernel, shape(NX, 16 * ROWS),
        [
            wave.reshape(1), half.reshape(1),
            signed_wave(NY).astype(np.float32)[None, :], signed_wave(NZ).astype(np.float32)[:, None],
            columns, *split_table(forward_z), *split_table(forward_y),
            np.concatenate([bz_high, bz_high, bz_low], axis=1), *split_table(back_y),
        ],
        (), 2, 1 << 30, 3 << 20,
    )
    mixed = lax.all_to_all(sent, everyone, 0, 0, tiled=True)
    arrived, _ = lax.optimization_barrier((arrived, mixed))
    center = call(assemble_kernel, shape(ALL_PAD, CELLS), [group_arg, *arrived], (), 1, 0, 4 << 20)
    z_low = lax.ppermute(center, both, pairs(lambda s, b: ((s + 1) % SPACES, b)))
    z_high = lax.ppermute(center, both, pairs(lambda s, b: ((s - 1) % SPACES, b)))

    weights = call(
        weights_kernel, shape(ALL_PAD, BLOCKS * ALL_PAD),
        [
            directions.astype(np.float32), pad_groups(synthesis, 1),
            pad_groups(projection, 0), pad_groups(turn_projection, 1),
        ],
        (), 0, 1 << 28, 1 << 20,
    )
    flow = call(fields_kernel, shape(11, ROWS, NX, dtype=f32), [mixed, *split_table(back_x)], (), 0, 1 << 29, 2 << 20)
    swap = pairs(lambda s, b: (s, b ^ (FLIP * odd(s))))
    velocity = lax.ppermute(flow[0:3], both, swap)
    flow, velocity = lax.optimization_barrier((flow, velocity))

    damp = pad_groups(damping, 0)[:, None]
    inner = call(
        inner_kernel, shape(ALL_PAD, ROWS * NX, dtype=f32), [center, flow, weights, damp],
        [pltpu.VMEM((2, (BLOCKS - 2) * ALL_PAD, NX), bf16), pltpu.VMEM((2, ALL_PAD, NX), f32)],
        0, 6 << 30, 7 << 20,
    )
    returned = []
    for part in range(PARTS):
        here = pl.BlockSpec((ALL_PAD, CHUNK * NX), lambda i, part=part: (0, part))
        beyond = pl.BlockSpec(
            (pl.Element(ALL_PAD), pl.Element(CHUNK * NX)), lambda i, part=part: (0, (part * CHUNK + 1) * NX)
        )
        rates = call(
            rate_kernel, [shape(OWN, CHUNK, NX)] * GROUPS,
            [group_arg, inner, z_low, z_high, flow, weights],
            [
                pltpu.VMEM((2, 2 * ALL_PAD, NX), bf16),
                pltpu.VMEM((2, ALL_PAD, NX), f32),
                pltpu.VMEM((ALL_PAD * CHUNK, LANES), f32),
                pltpu.VMEM((ALL_PAD * CHUNK, LANES), f32),
            ],
            1, 1 << 29, 9 << 19,
            [
                SMEM, here, beyond, beyond,
                pl.BlockSpec((11, CHUNK, NX), lambda i, part=part: (0, part, 0)), VMEM,
            ],
        )
        returned += exchanged(rates)
    rate = call(place_kernel, shape(OWN, NY, NX), [block_arg, *returned], (), 1, 0, 4 << 20)
    return (rate.reshape(OWN, 1, NY, NX), velocity.reshape(3, 1, ROWS, NX))


def solution(mesh):
    in_specs = (P("harm", "space", None, None), P(), P(), P(), P())
    out_specs = (P("harm", "space", None, None), P(None, "space", "harm", None))
    return jax.shard_map(local, mesh=mesh, in_specs=in_specs, out_specs=out_specs, check_vma=False)
```

```python
import functools
import math

import jax
import jax.numpy as jnp
import ml_dtypes
import numpy as np
from jax import lax
from jax.experimental import pallas as pl
from jax.experimental.pallas import tpu as pltpu
from jax.sharding import PartitionSpec as P

activity = -3.0
swim_speed = 1.0
transl_diff = 0.25
shape_factor = 0.9
golden_angle = math.pi * (3.0 - math.sqrt(5.0))

NX, NY, NZ = 256, 256, 32
COEFS, QUAD = 120, 256
SPACES, GROUPS = 32, 8
OWN = COEFS // GROUPS
PAD = 16
ROWS = NY // GROUPS
CELLS = ROWS * NX
HALF = NX // 2
ALL_PAD = GROUPS * PAD
LANES = 128
RUN = 8
FLIP = GROUPS // 2
PARTS = 2
CHUNK = ROWS // PARTS
BLOCKS = 12
bf16, f32 = jnp.bfloat16, jnp.float32
VMEM = pl.BlockSpec(memory_space=pltpu.VMEM)
SMEM = pl.BlockSpec(memory_space=pltpu.SMEM)
PARAMS = pltpu.CompilerParams(vmem_limit_bytes=56 * 1024 * 1024)


def split_table(table):
    high = table.astype(ml_dtypes.bfloat16)
    low = (table - high.astype(np.float64)).astype(ml_dtypes.bfloat16)
    return (high, low)


def signed_wave(length):
    index = np.arange(length)
    signed = np.where(index < length // 2, index, index - length)
    return 2.0 * math.pi / length * np.where(index == length // 2, 0, signed)


def sphere_directions():
    position = np.arange(QUAD, dtype=np.float64)
    height = 1.0 - (2.0 * position + 1.0) / QUAD
    radius = np.sqrt(1.0 - height * height)
    turning = position * golden_angle
    return np.stack([radius * np.cos(turning), radius * np.sin(turning), height])


def tables():
    x = np.arange(NX)[None, :]
    k = np.arange(HALF)[:, None]
    angle = 2.0 * math.pi * (k * x % NX) / NX
    cos_x, sin_x = np.cos(angle), np.sin(angle)
    sign = (-1.0) ** x[0]
    minus = -sin_x
    minus[0] = sign
    forward_x = np.concatenate([cos_x, minus])
    scale = 1.0 / (NX * NY * NZ)
    weight = np.where(k == 0, 1.0, 2.0) * scale
    wave = 2.0 * math.pi / NX * k
    real_x = weight * cos_x
    imag_x = -weight * sin_x
    imag_x[0] = sign * scale
    slope_real = -weight * wave * sin_x
    slope_imag = -weight * wave * cos_x
    back_x = np.concatenate([real_x, imag_x, slope_real, slope_imag], axis=1)
    back_x = np.concatenate([back_x, back_x])

    z = np.arange(NZ)
    angle = 2.0 * math.pi * (z[:, None] * z[None, :] % NZ) / NZ
    both_z = np.concatenate([np.cos(angle), np.sin(angle)])
    forward_z = np.tile(both_z, (1, GROUPS))

    y = np.arange(HALF)[:, None]
    ky = np.arange(NY)[None, :]
    angle = 2.0 * math.pi * (y * ky % NY) / NY
    forward_y = np.block([[np.cos(angle), -np.sin(angle)], [np.sin(angle), np.cos(angle)]])

    ky = np.arange(NY)[:, None]
    angle = 2.0 * math.pi * (ky * np.arange(NY)[None, :] % NY) / NY
    cos_y = np.cos(angle).reshape(NY, GROUPS, 1, ROWS)
    sin_y = np.sin(angle).reshape(NY, GROUPS, 1, ROWS)
    from_real = np.concatenate([cos_y, sin_y], axis=2).reshape(NY, 2 * NY)
    from_imag = np.concatenate([-sin_y, cos_y], axis=2).reshape(NY, 2 * NY)
    back_y = np.concatenate([from_real, from_imag])
    return forward_x, forward_z, forward_y, both_z, back_y, back_x


def halves(value):
    high = value.astype(bf16)
    return high, (value - high.astype(f32)).astype(bf16)


def dot(a, b):
    return jnp.dot(a, b, preferred_element_type=f32)


def regroup_kernel(block_ref, coef_ref, *refs):
    outs, stages = refs[:GROUPS], refs[GROUPS:]
    block = block_ref[0]
    for stage in stages:
        stage[pl.ds(OWN * ROWS, ROWS), :] = jnp.zeros((ROWS, LANES), f32)
    for j in range(GROUPS):
        first = pl.multiple_of((block ^ j) * ROWS, ROWS)
        rows = coef_ref[:, pl.ds(first, ROWS), :].astype(f32)
        rows = rows.reshape(OWN * ROWS, NX)
        for side, stage in enumerate(stages):
            stage[pl.ds(0, OWN * ROWS), :] = rows[:, side * LANES : (side + 1) * LANES]
            for r in range(ROWS):
                lane = r * NX + side * LANES
                outs[j][:, lane : lane + LANES] = stage[pl.ds(r, PAD, stride=ROWS), :].astype(bf16)


def stress_kernel(table_ref, coef_ref, high_ref, low_ref, out_ref, stress_high, stress_low):
    step = 32

    def rows(i, carry):
        first = pl.multiple_of(i * step, step)
        sums = [jnp.zeros((step, NX), f32)] * 5
        for c in range(OWN):
            value = coef_ref[c, pl.ds(first, step), :].astype(f32)
            sums = [s + table_ref[r, c] * value for r, s in enumerate(sums)]
        for r in range(5):
            high, low = halves(sums[r])
            stress_high[r, pl.ds(first, step), :] = high
            stress_low[r, pl.ds(first, step), :] = low
        return carry

    lax.fori_loop(0, NY // step, rows, 0)

    def across(a, b):
        return lax.dot_general(a, b, (((1,), (1,)), ((), ())), preferred_element_type=f32)

    for r in range(5):
        high, low = high_ref[...], low_ref[...]
        result = (
            across(high, stress_high[r]) + across(low, stress_high[r]) + across(high, stress_low[r])
        ).astype(bf16)
        for half in range(2):
            for part in range(2):
                lane = (2 * r + part) * HALF
                out_ref[half * HALF : (half + 1) * HALF, lane : lane + HALF] = result[
                    part * HALF : (part + 1) * HALF, half * HALF : (half + 1) * HALF
                ]


def solve_kernel(
    wave_ref, half_ref, ky_ref, kz_ref, recv_ref,
    fz_high, fz_low, fy_high, fy_low, bz, by_high, by_low, out_ref,
):
    recv = recv_ref[...]
    by_z = dot(fz_high[...], recv) + dot(fz_low[...], recv)
    lines = []
    for r in range(5):
        lane = 2 * r * HALF
        cos_re, cos_im = by_z[:NZ, lane : lane + HALF], by_z[:NZ, lane + HALF : lane + 2 * HALF]
        sin_re, sin_im = by_z[NZ:, lane : lane + HALF], by_z[NZ:, lane + HALF : lane + 2 * HALF]
        lines.append(jnp.concatenate([cos_re + sin_im, cos_im - sin_re], axis=1))
    high, low = halves(jnp.concatenate(lines))
    spec = dot(high, fy_high[...]) + dot(low, fy_high[...]) + dot(high, fy_low[...])
    lane = lax.broadcasted_iota(jnp.int32, (NZ, NY), 1)
    flip = jnp.where((lane % 2) * half_ref[0] == 1, -1.0, 1.0)
    real = [spec[r * NZ : (r + 1) * NZ, :NY] * flip for r in range(5)]
    imag = [spec[r * NZ : (r + 1) * NZ, NY:] * flip for r in range(5)]
    kx = jnp.full((NZ, NY), wave_ref[0], f32)
    ky = jnp.broadcast_to(ky_ref[...], (NZ, NY))
    kz = jnp.broadcast_to(kz_ref[...], (NZ, NY))
    square = kx * kx + ky * ky + kz * kz
    inverse = jnp.where(square > 0, 1.0 / jnp.where(square > 0, square, 1.0), 0.0)

    def force(part):
        xx, yy, xy, xz, yz = part
        return (
            kx * xx + ky * xy + kz * xz,
            kx * xy + ky * yy + kz * yz,
            kx * xz + ky * yz,
        )

    def solve(f):
        along = (kx * f[0] + ky * f[1] + kz * f[2]) * inverse
        return [(f[i] - k * along) * inverse for i, k in enumerate((kx, ky, kz))]

    flow_re = solve([-f for f in force(imag)])
    flow_im = solve(force(real))
    fields = list(zip(flow_re, flow_im))
    fields += [(-ky * flow_im[i], ky * flow_re[i]) for i in range(3)]
    fields += [(-kz * flow_im[i], kz * flow_re[i]) for i in range(2)]
    back = []
    for re, im in fields:
        high, low = halves(jnp.concatenate([re, im], axis=1))
        both = dot(bz[...], jnp.concatenate([high, low, high]))
        back.append(
            jnp.concatenate(
                [both[:NZ, :NY] - both[NZ:, NY:], both[:NZ, NY:] + both[NZ:, :NY]], axis=1
            )
        )
    high, low = halves(jnp.concatenate(back))
    done = dot(high, by_high[...]) + dot(low, by_high[...]) + dot(high, by_low[...])
    blocks = []
    for h in range(GROUPS):
        lane = 2 * ROWS * h
        pieces = [done[f * NZ : (f + 1) * NZ, lane : lane + 2 * ROWS] for f in range(8)]
        blocks.append(jnp.concatenate(pieces, axis=1))
    plane = lax.broadcasted_iota(jnp.int32, blocks[0].shape, 0)
    flipped = (plane // RUN) % 2 == 1
    for h in range(GROUPS):
        value = jnp.where(flipped, blocks[h ^ FLIP], blocks[h])
        out_ref[h * NZ : (h + 1) * NZ, :] = value.astype(bf16)


def fields_kernel(recv_ref, high_ref, low_ref, out_ref):
    flat = recv_ref[...].astype(f32).T.astype(bf16)
    both = dot(flat, high_ref[...]) + dot(flat, low_ref[...])

    def field(f, lane):
        row = 2 * ROWS * f
        return (
            both[row : row + ROWS, lane : lane + NX]
            + both[row + ROWS : row + 2 * ROWS, lane + NX : lane + 2 * NX]
        )

    for i in range(3):
        out_ref[i] = field(i, 0)
        out_ref[3 + i] = field(i, 2 * NX)
    for i in range(5):
        out_ref[6 + i] = field(3 + i, 0)


def weights_kernel(dir_ref, synth_ref, proj_ref, turn_ref, out_ref):
    synth = synth_ref[...]
    p = [dir_ref[j : j + 1, :] for j in range(3)]
    proj = proj_ref[...].astype(f32)
    turn = [turn_ref[k].astype(f32) for k in range(3)]
    radial = turn[0] * p[0] + turn[1] * p[1] + turn[2] * p[2]
    same = 0.5 * (shape_factor + 1.0)
    swap = 0.5 * (shape_factor - 1.0)

    def plain(i, j):
        return turn[i] * p[j] - radial * (p[i] * p[j])

    def strain(i, j):
        return same * plain(i, j) + swap * plain(j, i)

    left = [-0.5 * swim_speed * proj * p[j] for j in range(3)] + [-0.5 * proj]
    trace = strain(2, 2)
    left += [strain(0, 0) - trace, strain(1, 0), strain(2, 0)]
    left += [strain(0, 1), strain(1, 1) - trace, strain(2, 1)]
    left += [strain(0, 2), strain(1, 2)]
    for n, value in enumerate(left):
        high, low = halves(value)
        out_ref[:, n * ALL_PAD : (n + 1) * ALL_PAD] = (dot(high, synth) + dot(low, synth)).astype(bf16)


def assemble_kernel(group_ref, *refs):
    out_ref = refs[GROUPS]
    group = group_ref[0]
    for j in range(GROUPS):
        out_ref[pl.ds(pl.multiple_of((group ^ j) * PAD, PAD), PAD), :] = refs[j][...]


def rate_kernel(
    center_ref, zlow_ref, zhigh_ref, ylow_ref, yhigh_ref, flow_ref, weight_ref, damp_ref,
    *refs,
):
    out_ref, padded, operands, locals_, *stages = refs
    cells = CHUNK * NX
    padded[:, :NX] = ylow_ref[...]
    padded[:, NX : NX + cells] = center_ref[...]
    padded[:, NX + cells :] = yhigh_ref[...]

    def build(r, operand, local_terms):
        here = pl.multiple_of(r * NX, NX)
        flow = [flow_ref[f, pl.ds(r, 1), :] for f in range(11)]
        for g in range(GROUPS):
            rows = slice(g * PAD, (g + 1) * PAD)
            value = padded[rows, pl.ds(here + NX, NX)].astype(f32)
            y_low = padded[rows, pl.ds(here, NX)].astype(f32)
            y_high = padded[rows, pl.ds(here + 2 * NX, NX)].astype(f32)
            z_low = zlow_ref[rows, pl.ds(here, NX)].astype(f32)
            z_high = zhigh_ref[rows, pl.ds(here, NX)].astype(f32)
            x_low = pltpu.roll(value, 1, 1)
            x_high = pltpu.roll(value, NX - 1, 1)
            diffs = (x_high - x_low, y_high - y_low, z_high - z_low)
            drift = flow[0] * diffs[0] + flow[1] * diffs[1] + flow[2] * diffs[2]
            lap = x_high + x_low + y_high + y_low + z_high + z_low - 6.0 * value
            local_terms[rows, :] = transl_diff * lap - damp_ref[rows, :] * value
            terms = list(diffs) + [drift] + [flow[3 + n] * value for n in range(8)]
            for n, term in enumerate(terms):
                operand[n * ALL_PAD + g * PAD : n * ALL_PAD + (g + 1) * PAD, :] = term.astype(bf16)

    def rows(i, carry):
        for n in range(2):
            build(2 * i + n, operands.at[n], locals_.at[n])
        for n in range(2):
            result = dot(weight_ref[...], operands[n]) + locals_[n]
            for side, stage in enumerate(stages):
                stage[pl.ds(2 * i + n, ALL_PAD, stride=CHUNK), :] = result[
                    :, side * LANES : (side + 1) * LANES
                ]
        return carry

    lax.fori_loop(0, CHUNK // 2, rows, 0)
    for g in range(GROUPS):
        for c in range(OWN):
            first = (g * PAD + c) * CHUNK
            for side, stage in enumerate(stages):
                out_ref[g, c, :, side * LANES : (side + 1) * LANES] = stage[
                    first : first + CHUNK, :
                ].astype(bf16)


def place_kernel(swap_ref, *refs):
    out_ref = refs[-1]
    for part in range(PARTS):
        for g in range(GROUPS):
            first = pl.multiple_of((swap_ref[0] ^ g) * ROWS + part * CHUNK, CHUNK)
            out_ref[:, pl.ds(first, CHUNK), :] = refs[part][g]


def call(kernel, out_shape, ins, scratch=(), scalars=0, flops=0, byte_count=0, specs=None):
    return pl.pallas_call(
        kernel,
        out_shape=out_shape,
        grid=(1,) if specs else (),
        in_specs=specs or [SMEM] * scalars + [VMEM] * (len(ins) - scalars),
        out_specs=jax.tree.map(lambda _: VMEM, out_shape),
        scratch_shapes=list(scratch),
        compiler_params=PARAMS,
        cost_estimate=pl.CostEstimate(flops=flops, bytes_accessed=byte_count, transcendentals=0),
    )(*ins)


def shape(*dims, dtype=bf16):
    return jax.ShapeDtypeStruct(dims, dtype)


def pad_groups(value, axis):
    parts = value.reshape(*value.shape[:axis], GROUPS, OWN, *value.shape[axis + 1 :])
    widths = [(0, 0)] * parts.ndim
    widths[axis + 1] = (0, PAD - OWN)
    parts = jnp.pad(parts, widths)
    return parts.reshape(*value.shape[:axis], ALL_PAD, *value.shape[axis + 1 :])


def stress_table(synthesis, directions, group):
    dir_x, dir_y, dir_z = directions
    third = 1.0 / 3.0
    moments = np.stack(
        [
            dir_x * dir_x - third,
            dir_y * dir_y - third,
            dir_z * dir_z - third,
            dir_x * dir_y,
            dir_x * dir_z,
            dir_y * dir_z,
        ]
    ).astype(np.float32)
    own = lax.dynamic_slice_in_dim(synthesis, group * OWN, OWN, 1).astype(f32)
    table = jnp.dot(moments, own, precision=lax.Precision.HIGHEST)
    table = (table * (activity / math.sqrt(QUAD))).astype(bf16).astype(f32)
    return jnp.concatenate([table[0:2] - table[2:3], table[3:6]])


def odd(plane):
    return (plane // RUN) % 2


def pairs(target):
    found = []
    for plane in range(SPACES):
        for group in range(GROUPS):
            to_plane, to_block = target(plane, group ^ (FLIP * odd(plane)))
            to_group = to_block ^ (FLIP * odd(to_plane))
            found.append((plane * GROUPS + group, to_plane * GROUPS + to_group))
    return found


def local(coeffs, synthesis, projection, turn_projection, damping):
    group = lax.axis_index("harm")
    plane = lax.axis_index("space")
    both = ("space", "harm")
    everyone = ("harm", "space")
    position = group * SPACES + plane
    forward_x, forward_z, forward_y, back_z, back_y, back_x = tables()
    directions = sphere_directions()
    own = coeffs.reshape(OWN, NY, NX)
    group_arg = group.astype(jnp.int32).reshape(1)
    block_arg = group_arg ^ (FLIP * odd(plane)).astype(jnp.int32)

    table = stress_table(synthesis, directions, group)
    high, low = split_table(forward_x)
    sent = call(
        stress_kernel, shape(NX, 10 * HALF), [table, own, high, low],
        [pltpu.VMEM((5, NY, NX), bf16)] * 2, 1, 1 << 30, 3 << 20,
    )
    columns = lax.all_to_all(sent, everyone, 0, 0, tiled=True)

    later, _ = lax.optimization_barrier((own, sent))
    chunks = call(
        regroup_kernel, [shape(PAD, CELLS)] * GROUPS, [block_arg, later],
        [pltpu.VMEM((PAD * ROWS, LANES), f32)] * 2, 1, 0, 4 << 20,
    )
    arrived = [chunks[0]]
    for j in range(1, GROUPS):
        arrived.append(lax.ppermute(chunks[j], "harm", [(i, i ^ j) for i in range(GROUPS)]))

    wave = (position % HALF).astype(f32) * (2.0 * math.pi / NX)
    half = (position // HALF).astype(jnp.int32)
    bz_high, bz_low = split_table(back_z)
    sent = call(
        solve_kernel, shape(NX, 16 * ROWS),
        [
            wave.reshape(1), half.reshape(1),
            signed_wave(NY).astype(np.float32)[None, :], signed_wave(NZ).astype(np.float32)[:, None],
            columns, *split_table(forward_z), *split_table(forward_y),
            np.concatenate([bz_high, bz_high, bz_low], axis=1), *split_table(back_y),
        ],
        (), 2, 1 << 30, 3 << 20,
    )
    mixed = lax.all_to_all(sent, everyone, 0, 0, tiled=True)
    arrived, _ = lax.optimization_barrier((arrived, sent))
    center = call(assemble_kernel, shape(ALL_PAD, CELLS), [group_arg, *arrived], (), 1, 0, 4 << 20)
    z_low = lax.ppermute(center, both, pairs(lambda s, b: ((s + 1) % SPACES, b)))
    z_high = lax.ppermute(center, both, pairs(lambda s, b: ((s - 1) % SPACES, b)))
    y_low = lax.ppermute(center[:, -NX:], both, pairs(lambda s, b: (s, (b + 1) % GROUPS)))
    y_high = lax.ppermute(center[:, :NX], both, pairs(lambda s, b: (s, (b - 1) % GROUPS)))

    z_low, z_high, y_low, y_high = lax.optimization_barrier((z_low, z_high, y_low, y_high))
    weights = call(
        weights_kernel, shape(ALL_PAD, BLOCKS * ALL_PAD),
        [
            directions.astype(np.float32), pad_groups(synthesis, 1),
            pad_groups(projection, 0), pad_groups(turn_projection, 1),
        ],
        (), 0, 1 << 28, 1 << 20,
    )
    flow = call(fields_kernel, shape(11, ROWS, NX, dtype=f32), [mixed, *split_table(back_x)], (), 0, 1 << 29, 2 << 20)
    damp = pad_groups(damping, 0)[:, None]
    returned, parts = [], []
    for part in range(PARTS):
        here = pl.BlockSpec((ALL_PAD, CHUNK * NX), lambda i, part=part: (0, part))
        first, last = part * CHUNK, (part + 1) * CHUNK

        def edge(row):
            return pl.BlockSpec((ALL_PAD, NX), lambda i: (0, row))

        low = (y_low, VMEM) if first == 0 else (center, edge(first - 1))
        high = (y_high, VMEM) if last == ROWS else (center, edge(last))
        rates = call(
            rate_kernel, shape(GROUPS, OWN, CHUNK, NX),
            [center, z_low, z_high, low[0], high[0], flow, weights, damp],
            [
                pltpu.VMEM((ALL_PAD, (CHUNK + 2) * NX), bf16),
                pltpu.VMEM((2, BLOCKS * ALL_PAD, NX), bf16),
                pltpu.VMEM((2, ALL_PAD, NX), f32),
                pltpu.VMEM((ALL_PAD * CHUNK, LANES), f32),
                pltpu.VMEM((ALL_PAD * CHUNK, LANES), f32),
            ],
            0, 7 << 29, 9 << 19,
            [
                here, here, here, low[1], high[1],
                pl.BlockSpec((11, CHUNK, NX), lambda i, part=part: (0, part, 0)), VMEM, VMEM,
            ],
        )
        parts.append(rates)
        returned.append(lax.all_to_all(rates, "harm", 0, 0, tiled=True))
    swap = pairs(lambda s, b: (s, b ^ (FLIP * odd(s))))
    late, _ = lax.optimization_barrier((flow[0:3], parts[0]))
    velocity = lax.ppermute(late, both, swap)
    rate = call(place_kernel, shape(OWN, NY, NX), [group_arg ^ block_arg, *returned], (), 1, 0, 4 << 20)
    return (rate.reshape(OWN, 1, NY, NX), velocity.reshape(3, 1, ROWS, NX))


def solution(mesh):
    in_specs = (P("harm", "space", None, None), P(), P(), P(), P())
    out_specs = (P("harm", "space", None, None), P(None, "space", "harm", None))
    return jax.shard_map(local, mesh=mesh, in_specs=in_specs, out_specs=out_specs, check_vma=False)
```

```python
import functools
import math

import jax
import jax.numpy as jnp
import ml_dtypes
import numpy as np
from jax import lax
from jax.experimental import pallas as pl
from jax.experimental.pallas import tpu as pltpu
from jax.sharding import PartitionSpec as P

activity = -3.0
swim_speed = 1.0
transl_diff = 0.25
shape_factor = 0.9
golden_angle = math.pi * (3.0 - math.sqrt(5.0))

NX, NY, NZ = 256, 256, 32
COEFS, QUAD = 120, 256
SPACES, GROUPS = 32, 8
OWN = COEFS // GROUPS
PAD = 16
ROWS = NY // GROUPS
EDGED = ROWS + 2
CELLS = EDGED * NX
HALF = NX // 2
ALL_PAD = GROUPS * PAD
LANES = 128
RUN = 8
FLIP = GROUPS // 2
PARTS = 2
CHUNK = ROWS // PARTS
BLOCKS = 13
bf16, f32 = jnp.bfloat16, jnp.float32
VMEM = pl.BlockSpec(memory_space=pltpu.VMEM)
SMEM = pl.BlockSpec(memory_space=pltpu.SMEM)
PARAMS = pltpu.CompilerParams(vmem_limit_bytes=56 * 1024 * 1024)


def split_table(table):
    high = table.astype(ml_dtypes.bfloat16)
    low = (table - high.astype(np.float64)).astype(ml_dtypes.bfloat16)
    return (high, low)


def signed_wave(length):
    index = np.arange(length)
    signed = np.where(index < length // 2, index, index - length)
    return 2.0 * math.pi / length * np.where(index == length // 2, 0, signed)


def sphere_directions():
    position = np.arange(QUAD, dtype=np.float64)
    height = 1.0 - (2.0 * position + 1.0) / QUAD
    radius = np.sqrt(1.0 - height * height)
    turning = position * golden_angle
    return np.stack([radius * np.cos(turning), radius * np.sin(turning), height])


def tables():
    x = np.arange(NX)[None, :]
    k = np.arange(HALF)[:, None]
    angle = 2.0 * math.pi * (k * x % NX) / NX
    cos_x, sin_x = np.cos(angle), np.sin(angle)
    sign = (-1.0) ** x[0]
    minus = -sin_x
    minus[0] = sign
    forward_x = np.concatenate([cos_x, minus])
    scale = 1.0 / (NX * NY * NZ)
    weight = np.where(k == 0, 1.0, 2.0) * scale
    wave = 2.0 * math.pi / NX * k
    real_x = weight * cos_x
    imag_x = -weight * sin_x
    imag_x[0] = sign * scale
    slope_real = -weight * wave * sin_x
    slope_imag = -weight * wave * cos_x
    back_x = np.concatenate([real_x, imag_x, slope_real, slope_imag], axis=1)
    back_x = np.concatenate([back_x, back_x])

    z = np.arange(NZ)
    angle = 2.0 * math.pi * (z[:, None] * z[None, :] % NZ) / NZ
    both_z = np.concatenate([np.cos(angle), np.sin(angle)])
    forward_z = np.tile(both_z, (1, GROUPS))

    y = np.arange(HALF)[:, None]
    ky = np.arange(NY)[None, :]
    angle = 2.0 * math.pi * (y * ky % NY) / NY
    forward_y = np.block([[np.cos(angle), -np.sin(angle)], [np.sin(angle), np.cos(angle)]])

    ky = np.arange(NY)[:, None]
    angle = 2.0 * math.pi * (ky * np.arange(NY)[None, :] % NY) / NY
    cos_y = np.cos(angle).reshape(NY, GROUPS, 1, ROWS)
    sin_y = np.sin(angle).reshape(NY, GROUPS, 1, ROWS)
    from_real = np.concatenate([cos_y, sin_y], axis=2).reshape(NY, 2 * NY)
    from_imag = np.concatenate([-sin_y, cos_y], axis=2).reshape(NY, 2 * NY)
    back_y = np.concatenate([from_real, from_imag])
    return forward_x, forward_z, forward_y, both_z, back_y, back_x


def halves(value):
    high = value.astype(bf16)
    return high, (value - high.astype(f32)).astype(bf16)


def dot(a, b):
    return jnp.dot(a, b, preferred_element_type=f32)


def regroup_kernel(block_ref, coef_ref, *refs):
    near, rest, last, stages = refs[:FLIP], refs[FLIP], refs[FLIP + 1], refs[FLIP + 2 :]
    block = block_ref[0]
    height = ROWS + 2 * PAD
    for stage in stages:
        stage[pl.ds(OWN * height, height), :] = jnp.zeros((height, LANES), f32)
    for j in range(GROUPS):
        first = (block ^ j) * ROWS
        for start, size, at in ((NY - PAD, PAD, 0), (0, ROWS, PAD), (ROWS, PAD, PAD + ROWS)):
            rows = coef_ref[:, pl.ds(pl.multiple_of((first + start) % NY, PAD), size), :].astype(f32)
            for side, stage in enumerate(stages):
                for c in range(OWN):
                    stage[c * height + at : c * height + at + size, :] = rows[
                        c, :, side * LANES : (side + 1) * LANES
                    ]
        for side, stage in enumerate(stages):
            for r in range(EDGED):
                lane = r * NX + side * LANES
                rows = stage[pl.ds(PAD - 1 + r, PAD, stride=height), :]
                if j < FLIP:
                    near[j][:, lane : lane + LANES] = rows.astype(bf16)
                elif j == FLIP:
                    last[:, lane : lane + LANES] = rows.astype(bf16)
                else:
                    at = (j - FLIP - 1) * PAD
                    rest[at : at + PAD, lane : lane + LANES] = rows.astype(bf16)


def stress_kernel(table_ref, coef_ref, high_ref, low_ref, out_ref, stress_high, stress_low):
    step = 32

    def rows(i, carry):
        first = pl.multiple_of(i * step, step)
        sums = [jnp.zeros((step, NX), f32)] * 5
        for c in range(OWN):
            value = coef_ref[c, pl.ds(first, step), :].astype(f32)
            sums = [s + table_ref[r, c] * value for r, s in enumerate(sums)]
        for r in range(5):
            high, low = halves(sums[r])
            stress_high[r, pl.ds(first, step), :] = high
            stress_low[r, pl.ds(first, step), :] = low
        return carry

    lax.fori_loop(0, NY // step, rows, 0)

    def across(a, b):
        return lax.dot_general(a, b, (((1,), (1,)), ((), ())), preferred_element_type=f32)

    for r in range(5):
        high, low = high_ref[...], low_ref[...]
        result = (
            across(high, stress_high[r]) + across(low, stress_high[r]) + across(high, stress_low[r])
        ).astype(bf16)
        for half in range(2):
            for part in range(2):
                lane = (2 * r + part) * HALF
                out_ref[half * HALF : (half + 1) * HALF, lane : lane + HALF] = result[
                    part * HALF : (part + 1) * HALF, half * HALF : (half + 1) * HALF
                ]


def solve_kernel(
    wave_ref, half_ref, ky_ref, kz_ref, recv_ref,
    fz_high, fz_low, fy_high, fy_low, bz, by_high, by_low, out_ref,
):
    recv = recv_ref[...]
    by_z = dot(fz_high[...], recv) + dot(fz_low[...], recv)
    lines = []
    for r in range(5):
        lane = 2 * r * HALF
        cos_re, cos_im = by_z[:NZ, lane : lane + HALF], by_z[:NZ, lane + HALF : lane + 2 * HALF]
        sin_re, sin_im = by_z[NZ:, lane : lane + HALF], by_z[NZ:, lane + HALF : lane + 2 * HALF]
        lines.append(jnp.concatenate([cos_re + sin_im, cos_im - sin_re], axis=1))
    high, low = halves(jnp.concatenate(lines))
    spec = dot(high, fy_high[...]) + dot(low, fy_high[...]) + dot(high, fy_low[...])
    lane = lax.broadcasted_iota(jnp.int32, (NZ, NY), 1)
    flip = jnp.where((lane % 2) * half_ref[0] == 1, -1.0, 1.0)
    real = [spec[r * NZ : (r + 1) * NZ, :NY] * flip for r in range(5)]
    imag = [spec[r * NZ : (r + 1) * NZ, NY:] * flip for r in range(5)]
    kx = jnp.full((NZ, NY), wave_ref[0], f32)
    ky = jnp.broadcast_to(ky_ref[...], (NZ, NY))
    kz = jnp.broadcast_to(kz_ref[...], (NZ, NY))
    square = kx * kx + ky * ky + kz * kz
    inverse = jnp.where(square > 0, 1.0 / jnp.where(square > 0, square, 1.0), 0.0)

    def force(part):
        xx, yy, xy, xz, yz = part
        return (
            kx * xx + ky * xy + kz * xz,
            kx * xy + ky * yy + kz * yz,
            kx * xz + ky * yz,
        )

    def solve(f):
        along = (kx * f[0] + ky * f[1] + kz * f[2]) * inverse
        return [(f[i] - k * along) * inverse for i, k in enumerate((kx, ky, kz))]

    flow_re = solve([-f for f in force(imag)])
    flow_im = solve(force(real))
    fields = list(zip(flow_re, flow_im))
    fields += [(-ky * flow_im[i], ky * flow_re[i]) for i in range(3)]
    fields += [(-kz * flow_im[i], kz * flow_re[i]) for i in range(2)]
    back = []
    for re, im in fields:
        high, low = halves(jnp.concatenate([re, im], axis=1))
        both = dot(bz[...], jnp.concatenate([high, low, high]))
        back.append(
            jnp.concatenate(
                [both[:NZ, :NY] - both[NZ:, NY:], both[:NZ, NY:] + both[NZ:, :NY]], axis=1
            )
        )
    high, low = halves(jnp.concatenate(back))
    done = dot(high, by_high[...]) + dot(low, by_high[...]) + dot(high, by_low[...])
    blocks = []
    for h in range(GROUPS):
        lane = 2 * ROWS * h
        pieces = [done[f * NZ : (f + 1) * NZ, lane : lane + 2 * ROWS] for f in range(8)]
        blocks.append(jnp.concatenate(pieces, axis=1))
    plane = lax.broadcasted_iota(jnp.int32, blocks[0].shape, 0)
    flipped = (plane // RUN) % 2 == 1
    for h in range(GROUPS):
        value = jnp.where(flipped, blocks[h ^ FLIP], blocks[h])
        out_ref[h * NZ : (h + 1) * NZ, :] = value.astype(bf16)


def fields_kernel(recv_ref, high_ref, low_ref, out_ref):
    flat = recv_ref[...].astype(f32).T.astype(bf16)
    both = dot(flat, high_ref[...]) + dot(flat, low_ref[...])

    def field(f, lane):
        row = 2 * ROWS * f
        return (
            both[row : row + ROWS, lane : lane + NX]
            + both[row + ROWS : row + 2 * ROWS, lane + NX : lane + 2 * NX]
        )

    for i in range(3):
        out_ref[i] = field(i, 0)
        out_ref[3 + i] = field(i, 2 * NX)
    for i in range(5):
        out_ref[6 + i] = field(3 + i, 0)


def weights_kernel(dir_ref, synth_ref, proj_ref, turn_ref, out_ref):
    synth = synth_ref[...]
    p = [dir_ref[j : j + 1, :] for j in range(3)]
    proj = proj_ref[...].astype(f32)
    turn = [turn_ref[k].astype(f32) for k in range(3)]
    radial = turn[0] * p[0] + turn[1] * p[1] + turn[2] * p[2]
    same = 0.5 * (shape_factor + 1.0)
    swap = 0.5 * (shape_factor - 1.0)

    def plain(i, j):
        return turn[i] * p[j] - radial * (p[i] * p[j])

    def strain(i, j):
        return same * plain(i, j) + swap * plain(j, i)

    left = [-0.5 * swim_speed * proj * p[j] for j in range(2)] + [-0.5 * proj]
    trace = strain(2, 2)
    left += [strain(0, 0) - trace, strain(1, 0), strain(2, 0)]
    left += [strain(0, 1), strain(1, 1) - trace, strain(2, 1)]
    left += [strain(0, 2), strain(1, 2)]
    left += [-0.5 * swim_speed * proj * p[2], -0.5 * proj]
    for n, value in enumerate(left):
        high, low = halves(value)
        out_ref[:, n * ALL_PAD : (n + 1) * ALL_PAD] = (dot(high, synth) + dot(low, synth)).astype(bf16)


def assemble_kernel(group_ref, *refs):
    out_ref = refs[GROUPS]
    group = group_ref[0]
    for j in range(GROUPS):
        out_ref[pl.ds(pl.multiple_of((group ^ j) * PAD, PAD), PAD), :] = refs[j][...]


def inner_kernel(center_ref, flow_ref, weight_ref, damp_ref, out_ref, operands, locals_):
    blocks = BLOCKS - 2

    def build(r, operand, local_terms):
        here = pl.multiple_of(r * NX, NX)
        flow = [flow_ref[f, pl.ds(r, 1), :] for f in range(11)]
        for g in range(GROUPS):
            rows = slice(g * PAD, (g + 1) * PAD)
            value = center_ref[rows, pl.ds(here + NX, NX)].astype(f32)
            y_low = center_ref[rows, pl.ds(here, NX)].astype(f32)
            y_high = center_ref[rows, pl.ds(here + 2 * NX, NX)].astype(f32)
            x_low = pltpu.roll(value, 1, 1)
            x_high = pltpu.roll(value, NX - 1, 1)
            diff_x, diff_y = x_high - x_low, y_high - y_low
            lap = x_high + x_low + y_high + y_low - 6.0 * value
            local_terms[rows, :] = transl_diff * lap - damp_ref[rows, :] * value
            terms = [diff_x, diff_y, flow[0] * diff_x + flow[1] * diff_y]
            terms += [flow[3 + n] * value for n in range(8)]
            for n, term in enumerate(terms):
                operand[n * ALL_PAD + g * PAD : n * ALL_PAD + (g + 1) * PAD, :] = term.astype(bf16)

    def rows(i, carry):
        for n in range(2):
            build(2 * i + n, operands.at[n], locals_.at[n])
        for n in range(2):
            where = pl.ds(pl.multiple_of((2 * i + n) * NX, NX), NX)
            out_ref[:, where] = locals_[n] + dot(weight_ref[:, : blocks * ALL_PAD], operands[n])
        return carry

    lax.fori_loop(0, ROWS // 2, rows, 0)


def rate_kernel(
    inner_ref, zlow_ref, zhigh_ref, flow_ref, weight_ref, out_ref, operands, locals_, *stages
):
    skip = (BLOCKS - 2) * ALL_PAD

    def build(r, operand, local_terms):
        here = pl.multiple_of(r * NX, NX)
        drift = flow_ref[2, pl.ds(r, 1), :]
        for g in range(GROUPS):
            rows = slice(g * PAD, (g + 1) * PAD)
            z_low = zlow_ref[rows, pl.ds(here, NX)].astype(f32)
            z_high = zhigh_ref[rows, pl.ds(here, NX)].astype(f32)
            diff_z = z_high - z_low
            local_terms[rows, :] = transl_diff * (z_high + z_low) + inner_ref[rows, pl.ds(here, NX)]
            operand[rows, :] = diff_z.astype(bf16)
            operand[ALL_PAD + g * PAD : ALL_PAD + (g + 1) * PAD, :] = (drift * diff_z).astype(bf16)

    def rows(i, carry):
        for n in range(2):
            build(2 * i + n, operands.at[n], locals_.at[n])
        for n in range(2):
            result = dot(weight_ref[:, skip:], operands[n]) + locals_[n]
            for side, stage in enumerate(stages):
                stage[pl.ds(2 * i + n, ALL_PAD, stride=CHUNK), :] = result[
                    :, side * LANES : (side + 1) * LANES
                ]
        return carry

    lax.fori_loop(0, CHUNK // 2, rows, 0)
    for g in range(GROUPS):
        for c in range(OWN):
            first = (g * PAD + c) * CHUNK
            for side, stage in enumerate(stages):
                out_ref[g, c, :, side * LANES : (side + 1) * LANES] = stage[
                    first : first + CHUNK, :
                ].astype(bf16)


def place_kernel(swap_ref, *refs):
    out_ref = refs[-1]
    for part in range(PARTS):
        for g in range(GROUPS):
            first = pl.multiple_of((swap_ref[0] ^ g) * ROWS + part * CHUNK, CHUNK)
            out_ref[:, pl.ds(first, CHUNK), :] = refs[part][g]


def call(kernel, out_shape, ins, scratch=(), scalars=0, flops=0, byte_count=0, specs=None):
    return pl.pallas_call(
        kernel,
        out_shape=out_shape,
        grid=(1,) if specs else (),
        in_specs=specs or [SMEM] * scalars + [VMEM] * (len(ins) - scalars),
        out_specs=jax.tree.map(lambda _: VMEM, out_shape),
        scratch_shapes=list(scratch),
        compiler_params=PARAMS,
        cost_estimate=pl.CostEstimate(flops=flops, bytes_accessed=byte_count, transcendentals=0),
    )(*ins)


def shape(*dims, dtype=bf16):
    return jax.ShapeDtypeStruct(dims, dtype)


def pad_groups(value, axis):
    parts = value.reshape(*value.shape[:axis], GROUPS, OWN, *value.shape[axis + 1 :])
    widths = [(0, 0)] * parts.ndim
    widths[axis + 1] = (0, PAD - OWN)
    parts = jnp.pad(parts, widths)
    return parts.reshape(*value.shape[:axis], ALL_PAD, *value.shape[axis + 1 :])


def stress_table(synthesis, directions, group):
    dir_x, dir_y, dir_z = directions
    third = 1.0 / 3.0
    moments = np.stack(
        [
            dir_x * dir_x - third,
            dir_y * dir_y - third,
            dir_z * dir_z - third,
            dir_x * dir_y,
            dir_x * dir_z,
            dir_y * dir_z,
        ]
    ).astype(np.float32)
    own = lax.dynamic_slice_in_dim(synthesis, group * OWN, OWN, 1).astype(f32)
    table = jnp.dot(moments, own, precision=lax.Precision.HIGHEST)
    table = (table * (activity / math.sqrt(QUAD))).astype(bf16).astype(f32)
    return jnp.concatenate([table[0:2] - table[2:3], table[3:6]])


def partner(j):
    return [(i, i ^ j) for i in range(GROUPS)]


def exchanged(chunks):
    return [chunks[0]] + [lax.ppermute(c, "harm", partner(j + 1)) for j, c in enumerate(chunks[1:])]


def odd(plane):
    return (plane // RUN) % 2


def pairs(target):
    found = []
    for plane in range(SPACES):
        for group in range(GROUPS):
            to_plane, to_block = target(plane, group ^ (FLIP * odd(plane)))
            to_group = to_block ^ (FLIP * odd(to_plane))
            found.append((plane * GROUPS + group, to_plane * GROUPS + to_group))
    return found


def local(coeffs, synthesis, projection, turn_projection, damping):
    group = lax.axis_index("harm")
    plane = lax.axis_index("space")
    both = ("space", "harm")
    everyone = ("harm", "space")
    position = group * SPACES + plane
    forward_x, forward_z, forward_y, back_z, back_y, back_x = tables()
    directions = sphere_directions()
    own = coeffs.reshape(OWN, NY, NX)
    group_arg = group.astype(jnp.int32).reshape(1)
    block_arg = group_arg ^ (FLIP * odd(plane)).astype(jnp.int32)

    table = stress_table(synthesis, directions, group)
    high, low = split_table(forward_x)
    sent = call(
        stress_kernel, shape(NX, 10 * HALF), [table, own, high, low],
        [pltpu.VMEM((5, NY, NX), bf16)] * 2, 1, 1 << 30, 3 << 20,
    )
    columns = lax.all_to_all(sent, everyone, 0, 0, tiled=True)

    later, _ = lax.optimization_barrier((own, sent))
    chunks = call(
        regroup_kernel,
        [shape(PAD, CELLS)] * FLIP + [shape((FLIP - 1) * PAD, CELLS), shape(PAD, CELLS)], [block_arg, later],
        [pltpu.VMEM((PAD * (ROWS + 2 * PAD), LANES), f32)] * 2, 1, 0, 4 << 20,
    )
    chunks, columns = lax.optimization_barrier((chunks, columns))
    rest = lax.ppermute(chunks[FLIP], "harm", partner(FLIP))
    last = lax.ppermute(chunks[FLIP + 1], "harm", partner(FLIP))
    arrived = exchanged(chunks[:FLIP])
    arrived += exchanged([last] + [rest[m * PAD : (m + 1) * PAD] for m in range(FLIP - 1)])

    wave = (position % HALF).astype(f32) * (2.0 * math.pi / NX)
    half = (position // HALF).astype(jnp.int32)
    bz_high, bz_low = split_table(back_z)
    sent = call(
        solve_kernel, shape(NX, 16 * ROWS),
        [
            wave.reshape(1), half.reshape(1),
            signed_wave(NY).astype(np.float32)[None, :], signed_wave(NZ).astype(np.float32)[:, None],
            columns, *split_table(forward_z), *split_table(forward_y),
            np.concatenate([bz_high, bz_high, bz_low], axis=1), *split_table(back_y),
        ],
        (), 2, 1 << 30, 3 << 20,
    )
    mixed = lax.all_to_all(sent, everyone, 0, 0, tiled=True)
    arrived, _ = lax.optimization_barrier((arrived, mixed))
    center = call(assemble_kernel, shape(ALL_PAD, CELLS), [group_arg, *arrived], (), 1, 0, 4 << 20)
    z_low = lax.ppermute(center, both, pairs(lambda s, b: ((s + 1) % SPACES, b)))
    z_high = lax.ppermute(center, both, pairs(lambda s, b: ((s - 1) % SPACES, b)))

    weights = call(
        weights_kernel, shape(ALL_PAD, BLOCKS * ALL_PAD),
        [
            directions.astype(np.float32), pad_groups(synthesis, 1),
            pad_groups(projection, 0), pad_groups(turn_projection, 1),
        ],
        (), 0, 1 << 28, 1 << 20,
    )
    flow = call(fields_kernel, shape(11, ROWS, NX, dtype=f32), [mixed, *split_table(back_x)], (), 0, 1 << 29, 2 << 20)
    damp = pad_groups(damping, 0)[:, None]
    inner = call(
        inner_kernel, shape(ALL_PAD, ROWS * NX, dtype=f32), [center, flow, weights, damp],
        [pltpu.VMEM((2, (BLOCKS - 2) * ALL_PAD, NX), bf16), pltpu.VMEM((2, ALL_PAD, NX), f32)],
        0, 6 << 30, 7 << 20,
    )
    returned, parts = [], []
    for part in range(PARTS):
        here = pl.BlockSpec((ALL_PAD, CHUNK * NX), lambda i, part=part: (0, part))
        beyond = pl.BlockSpec(
            (pl.Element(ALL_PAD), pl.Element(CHUNK * NX)), lambda i, part=part: (0, (part * CHUNK + 1) * NX)
        )
        rates = call(
            rate_kernel, shape(GROUPS, OWN, CHUNK, NX),
            [inner, z_low, z_high, flow, weights],
            [
                pltpu.VMEM((2, 2 * ALL_PAD, NX), bf16),
                pltpu.VMEM((2, ALL_PAD, NX), f32),
                pltpu.VMEM((ALL_PAD * CHUNK, LANES), f32),
                pltpu.VMEM((ALL_PAD * CHUNK, LANES), f32),
            ],
            0, 1 << 29, 9 << 19,
            [
                here, beyond, beyond,
                pl.BlockSpec((11, CHUNK, NX), lambda i, part=part: (0, part, 0)), VMEM,
            ],
        )
        parts.append(rates)
        returned.append(lax.all_to_all(rates, "harm", 0, 0, tiled=True))
    swap = pairs(lambda s, b: (s, b ^ (FLIP * odd(s))))
    late, _ = lax.optimization_barrier((flow[0:3], parts[0]))
    velocity = lax.ppermute(late, both, swap)
    rate = call(place_kernel, shape(OWN, NY, NX), [group_arg ^ block_arg, *returned], (), 1, 0, 4 << 20)
    return (rate.reshape(OWN, 1, NY, NX), velocity.reshape(3, 1, ROWS, NX))


def solution(mesh):
    in_specs = (P("harm", "space", None, None), P(), P(), P(), P())
    out_specs = (P("harm", "space", None, None), P(None, "space", "harm", None))
    return jax.shard_map(local, mesh=mesh, in_specs=in_specs, out_specs=out_specs, check_vma=False)
```

```python
import functools
import math

import jax
import jax.numpy as jnp
import ml_dtypes
import numpy as np
from jax import lax
from jax.experimental import pallas as pl
from jax.experimental.pallas import tpu as pltpu
from jax.sharding import PartitionSpec as P

activity = -3.0
swim_speed = 1.0
transl_diff = 0.25
shape_factor = 0.9
golden_angle = math.pi * (3.0 - math.sqrt(5.0))

NX, NY, NZ = 256, 256, 32
COEFS, QUAD = 120, 256
SPACES, GROUPS = 32, 8
OWN = COEFS // GROUPS
PAD = 16
ROWS = NY // GROUPS
EDGED = ROWS + 2
CELLS = EDGED * NX
HALF = NX // 2
ALL_PAD = GROUPS * PAD
LANES = 128
RUN = 8
FLIP = GROUPS // 2
AHEAD = 6
PARTS = 2
CHUNK = ROWS // PARTS
BLOCKS = 12
bf16, f32 = jnp.bfloat16, jnp.float32
VMEM = pl.BlockSpec(memory_space=pltpu.VMEM)
SMEM = pl.BlockSpec(memory_space=pltpu.SMEM)
PARAMS = pltpu.CompilerParams(vmem_limit_bytes=56 * 1024 * 1024)


def split_table(table):
    high = table.astype(ml_dtypes.bfloat16)
    low = (table - high.astype(np.float64)).astype(ml_dtypes.bfloat16)
    return (high, low)


def signed_wave(length):
    index = np.arange(length)
    signed = np.where(index < length // 2, index, index - length)
    return 2.0 * math.pi / length * np.where(index == length // 2, 0, signed)


def sphere_directions():
    position = np.arange(QUAD, dtype=np.float64)
    height = 1.0 - (2.0 * position + 1.0) / QUAD
    radius = np.sqrt(1.0 - height * height)
    turning = position * golden_angle
    return np.stack([radius * np.cos(turning), radius * np.sin(turning), height])


def tables():
    x = np.arange(NX)[None, :]
    k = np.arange(HALF)[:, None]
    angle = 2.0 * math.pi * (k * x % NX) / NX
    cos_x, sin_x = np.cos(angle), np.sin(angle)
    sign = (-1.0) ** x[0]
    minus = -sin_x
    minus[0] = sign
    forward_x = np.concatenate([cos_x, minus])
    scale = 1.0 / (NX * NY * NZ)
    weight = np.where(k == 0, 1.0, 2.0) * scale
    wave = 2.0 * math.pi / NX * k
    real_x = weight * cos_x
    imag_x = -weight * sin_x
    imag_x[0] = sign * scale
    slope_real = -weight * wave * sin_x
    slope_imag = -weight * wave * cos_x
    back_x = np.concatenate([real_x, imag_x, slope_real, slope_imag], axis=1)
    back_x = np.concatenate([back_x, back_x])

    z = np.arange(NZ)
    angle = 2.0 * math.pi * (z[:, None] * z[None, :] % NZ) / NZ
    both_z = np.concatenate([np.cos(angle), np.sin(angle)])
    forward_z = np.tile(both_z, (1, GROUPS))

    y = np.arange(HALF)[:, None]
    ky = np.arange(NY)[None, :]
    angle = 2.0 * math.pi * (y * ky % NY) / NY
    forward_y = np.block([[np.cos(angle), -np.sin(angle)], [np.sin(angle), np.cos(angle)]])

    ky = np.arange(NY)[:, None]
    angle = 2.0 * math.pi * (ky * np.arange(NY)[None, :] % NY) / NY
    cos_y = np.cos(angle).reshape(NY, GROUPS, 1, ROWS)
    sin_y = np.sin(angle).reshape(NY, GROUPS, 1, ROWS)
    from_real = np.concatenate([cos_y, sin_y], axis=2).reshape(NY, 2 * NY)
    from_imag = np.concatenate([-sin_y, cos_y], axis=2).reshape(NY, 2 * NY)
    back_y = np.concatenate([from_real, from_imag])
    return forward_x, forward_z, forward_y, both_z, back_y, back_x


def halves(value):
    high = value.astype(bf16)
    return high, (value - high.astype(f32)).astype(bf16)


def dot(a, b):
    return jnp.dot(a, b, preferred_element_type=f32)


def regroup_kernel(block_ref, coef_ref, *refs):
    outs, stages = refs[:GROUPS], refs[GROUPS:]
    block = block_ref[0]
    height = ROWS + 2 * PAD
    for stage in stages:
        stage[pl.ds(OWN * height, height), :] = jnp.zeros((height, LANES), f32)
    for j in range(GROUPS):
        first = (block ^ j) * ROWS
        for start, size, at in ((NY - PAD, PAD, 0), (0, ROWS, PAD), (ROWS, PAD, PAD + ROWS)):
            rows = coef_ref[:, pl.ds(pl.multiple_of((first + start) % NY, PAD), size), :].astype(f32)
            for side, stage in enumerate(stages):
                for c in range(OWN):
                    stage[c * height + at : c * height + at + size, :] = rows[
                        c, :, side * LANES : (side + 1) * LANES
                    ]
        for side, stage in enumerate(stages):
            for r in range(EDGED):
                lane = r * NX + side * LANES
                rows = stage[pl.ds(PAD - 1 + r, PAD, stride=height), :]
                outs[j][:, lane : lane + LANES] = rows.astype(bf16)


def stress_kernel(table_ref, coef_ref, high_ref, low_ref, out_ref, stress_high, stress_low):
    step = 32

    def rows(i, carry):
        first = pl.multiple_of(i * step, step)
        sums = [jnp.zeros((step, NX), f32)] * 5
        for c in range(OWN):
            value = coef_ref[c, pl.ds(first, step), :].astype(f32)
            sums = [s + table_ref[r, c] * value for r, s in enumerate(sums)]
        for r in range(5):
            high, low = halves(sums[r])
            stress_high[r, pl.ds(first, step), :] = high
            stress_low[r, pl.ds(first, step), :] = low
        return carry

    lax.fori_loop(0, NY // step, rows, 0)

    def across(a, b):
        return lax.dot_general(a, b, (((1,), (1,)), ((), ())), preferred_element_type=f32)

    for r in range(5):
        high, low = high_ref[...], low_ref[...]
        result = (
            across(high, stress_high[r]) + across(low, stress_high[r]) + across(high, stress_low[r])
        ).astype(bf16)
        for half in range(2):
            for part in range(2):
                lane = (2 * r + part) * HALF
                out_ref[half * HALF : (half + 1) * HALF, lane : lane + HALF] = result[
                    part * HALF : (part + 1) * HALF, half * HALF : (half + 1) * HALF
                ]


def solve_kernel(
    wave_ref, half_ref, ky_ref, kz_ref, recv_ref,
    fz_high, fz_low, fy_high, fy_low, bz, by_high, by_low, out_ref,
):
    recv = recv_ref[...]
    by_z = dot(fz_high[...], recv) + dot(fz_low[...], recv)
    lines = []
    for r in range(5):
        lane = 2 * r * HALF
        cos_re, cos_im = by_z[:NZ, lane : lane + HALF], by_z[:NZ, lane + HALF : lane + 2 * HALF]
        sin_re, sin_im = by_z[NZ:, lane : lane + HALF], by_z[NZ:, lane + HALF : lane + 2 * HALF]
        lines.append(jnp.concatenate([cos_re + sin_im, cos_im - sin_re], axis=1))
    high, low = halves(jnp.concatenate(lines))
    spec = dot(high, fy_high[...]) + dot(low, fy_high[...]) + dot(high, fy_low[...])
    lane = lax.broadcasted_iota(jnp.int32, (NZ, NY), 1)
    flip = jnp.where((lane % 2) * half_ref[0] == 1, -1.0, 1.0)
    real = [spec[r * NZ : (r + 1) * NZ, :NY] * flip for r in range(5)]
    imag = [spec[r * NZ : (r + 1) * NZ, NY:] * flip for r in range(5)]
    kx = jnp.full((NZ, NY), wave_ref[0], f32)
    ky = jnp.broadcast_to(ky_ref[...], (NZ, NY))
    kz = jnp.broadcast_to(kz_ref[...], (NZ, NY))
    square = kx * kx + ky * ky + kz * kz
    inverse = jnp.where(square > 0, 1.0 / jnp.where(square > 0, square, 1.0), 0.0)

    def force(part):
        xx, yy, xy, xz, yz = part
        return (
            kx * xx + ky * xy + kz * xz,
            kx * xy + ky * yy + kz * yz,
            kx * xz + ky * yz,
        )

    def solve(f):
        along = (kx * f[0] + ky * f[1] + kz * f[2]) * inverse
        return [(f[i] - k * along) * inverse for i, k in enumerate((kx, ky, kz))]

    flow_re = solve([-f for f in force(imag)])
    flow_im = solve(force(real))
    fields = list(zip(flow_re, flow_im))
    fields += [(-ky * flow_im[i], ky * flow_re[i]) for i in range(3)]
    fields += [(-kz * flow_im[i], kz * flow_re[i]) for i in range(2)]
    back = []
    for re, im in fields:
        high, low = halves(jnp.concatenate([re, im], axis=1))
        both = dot(bz[...], jnp.concatenate([high, low, high]))
        back.append(
            jnp.concatenate(
                [both[:NZ, :NY] - both[NZ:, NY:], both[:NZ, NY:] + both[NZ:, :NY]], axis=1
            )
        )
    high, low = halves(jnp.concatenate(back))
    done = dot(high, by_high[...]) + dot(low, by_high[...]) + dot(high, by_low[...])
    blocks = []
    for h in range(GROUPS):
        lane = 2 * ROWS * h
        pieces = [done[f * NZ : (f + 1) * NZ, lane : lane + 2 * ROWS] for f in range(8)]
        blocks.append(jnp.concatenate(pieces, axis=1))
    plane = lax.broadcasted_iota(jnp.int32, blocks[0].shape, 0)
    flipped = (plane // RUN) % 2 == 1
    for h in range(GROUPS):
        value = jnp.where(flipped, blocks[h ^ FLIP], blocks[h])
        out_ref[h * NZ : (h + 1) * NZ, :] = value.astype(bf16)


def fields_kernel(recv_ref, high_ref, low_ref, out_ref):
    flat = recv_ref[...].astype(f32).T.astype(bf16)
    both = dot(flat, high_ref[...]) + dot(flat, low_ref[...])

    def field(f, lane):
        row = 2 * ROWS * f
        return (
            both[row : row + ROWS, lane : lane + NX]
            + both[row + ROWS : row + 2 * ROWS, lane + NX : lane + 2 * NX]
        )

    for i in range(3):
        out_ref[i] = field(i, 0)
        out_ref[3 + i] = field(i, 2 * NX)
    for i in range(5):
        out_ref[6 + i] = field(3 + i, 0)


def weights_kernel(dir_ref, synth_ref, proj_ref, turn_ref, out_ref):
    synth = synth_ref[...]
    p = [dir_ref[j : j + 1, :] for j in range(3)]
    proj = proj_ref[...].astype(f32)
    turn = [turn_ref[k].astype(f32) for k in range(3)]
    radial = turn[0] * p[0] + turn[1] * p[1] + turn[2] * p[2]
    same = 0.5 * (shape_factor + 1.0)
    swap = 0.5 * (shape_factor - 1.0)

    def plain(i, j):
        return turn[i] * p[j] - radial * (p[i] * p[j])

    def strain(i, j):
        return same * plain(i, j) + swap * plain(j, i)

    left = [-0.5 * swim_speed * proj * p[j] for j in range(3)] + [-0.5 * proj]
    trace = strain(2, 2)
    left += [strain(0, 0) - trace, strain(1, 0), strain(2, 0)]
    left += [strain(0, 1), strain(1, 1) - trace, strain(2, 1)]
    left += [strain(0, 2), strain(1, 2)]
    for n, value in enumerate(left):
        high, low = halves(value)
        out_ref[:, n * ALL_PAD : (n + 1) * ALL_PAD] = (dot(high, synth) + dot(low, synth)).astype(bf16)


def assemble_kernel(group_ref, *refs):
    out_ref = refs[GROUPS]
    group = group_ref[0]
    for j in range(GROUPS):
        out_ref[pl.ds(pl.multiple_of((group ^ j) * PAD, PAD), PAD), :] = refs[j][...]


def rate_kernel(
    center_ref, zlow_ref, zhigh_ref, flow_ref, weight_ref, damp_ref,
    out_ref, operands, locals_, *stages,
):
    def build(r, operand, local_terms):
        here = pl.multiple_of(r * NX, NX)
        flow = [flow_ref[f, pl.ds(r, 1), :] for f in range(11)]
        for g in range(GROUPS):
            rows = slice(g * PAD, (g + 1) * PAD)
            value = center_ref[rows, pl.ds(here + NX, NX)].astype(f32)
            y_low = center_ref[rows, pl.ds(here, NX)].astype(f32)
            y_high = center_ref[rows, pl.ds(here + 2 * NX, NX)].astype(f32)
            z_low = zlow_ref[rows, pl.ds(here, NX)].astype(f32)
            z_high = zhigh_ref[rows, pl.ds(here, NX)].astype(f32)
            x_low = pltpu.roll(value, 1, 1)
            x_high = pltpu.roll(value, NX - 1, 1)
            diffs = (x_high - x_low, y_high - y_low, z_high - z_low)
            drift = flow[0] * diffs[0] + flow[1] * diffs[1] + flow[2] * diffs[2]
            lap = x_high + x_low + y_high + y_low + z_high + z_low - 6.0 * value
            local_terms[rows, :] = transl_diff * lap - damp_ref[rows, :] * value
            terms = list(diffs) + [drift] + [flow[3 + n] * value for n in range(8)]
            for n, term in enumerate(terms):
                operand[n * ALL_PAD + g * PAD : n * ALL_PAD + (g + 1) * PAD, :] = term.astype(bf16)

    def rows(i, carry):
        for n in range(2):
            build(2 * i + n, operands.at[n], locals_.at[n])
        for n in range(2):
            result = dot(weight_ref[...], operands[n]) + locals_[n]
            for side, stage in enumerate(stages):
                stage[pl.ds(2 * i + n, ALL_PAD, stride=CHUNK), :] = result[
                    :, side * LANES : (side + 1) * LANES
                ]
        return carry

    lax.fori_loop(0, CHUNK // 2, rows, 0)
    for g in range(GROUPS):
        for c in range(OWN):
            first = (g * PAD + c) * CHUNK
            for side, stage in enumerate(stages):
                out_ref[g, c, :, side * LANES : (side + 1) * LANES] = stage[
                    first : first + CHUNK, :
                ].astype(bf16)


def place_kernel(swap_ref, *refs):
    out_ref = refs[-1]
    for part in range(PARTS):
        for g in range(GROUPS):
            first = pl.multiple_of((swap_ref[0] ^ g) * ROWS + part * CHUNK, CHUNK)
            out_ref[:, pl.ds(first, CHUNK), :] = refs[part][g]


def call(kernel, out_shape, ins, scratch=(), scalars=0, flops=0, byte_count=0, specs=None):
    return pl.pallas_call(
        kernel,
        out_shape=out_shape,
        grid=(1,) if specs else (),
        in_specs=specs or [SMEM] * scalars + [VMEM] * (len(ins) - scalars),
        out_specs=jax.tree.map(lambda _: VMEM, out_shape),
        scratch_shapes=list(scratch),
        compiler_params=PARAMS,
        cost_estimate=pl.CostEstimate(flops=flops, bytes_accessed=byte_count, transcendentals=0),
    )(*ins)


def shape(*dims, dtype=bf16):
    return jax.ShapeDtypeStruct(dims, dtype)


def pad_groups(value, axis):
    parts = value.reshape(*value.shape[:axis], GROUPS, OWN, *value.shape[axis + 1 :])
    widths = [(0, 0)] * parts.ndim
    widths[axis + 1] = (0, PAD - OWN)
    parts = jnp.pad(parts, widths)
    return parts.reshape(*value.shape[:axis], ALL_PAD, *value.shape[axis + 1 :])


def stress_table(synthesis, directions, group):
    dir_x, dir_y, dir_z = directions
    third = 1.0 / 3.0
    moments = np.stack(
        [
            dir_x * dir_x - third,
            dir_y * dir_y - third,
            dir_z * dir_z - third,
            dir_x * dir_y,
            dir_x * dir_z,
            dir_y * dir_z,
        ]
    ).astype(np.float32)
    own = lax.dynamic_slice_in_dim(synthesis, group * OWN, OWN, 1).astype(f32)
    table = jnp.dot(moments, own, precision=lax.Precision.HIGHEST)
    table = (table * (activity / math.sqrt(QUAD))).astype(bf16).astype(f32)
    return jnp.concatenate([table[0:2] - table[2:3], table[3:6]])


def odd(plane):
    return (plane // RUN) % 2


def pairs(target):
    found = []
    for plane in range(SPACES):
        for group in range(GROUPS):
            to_plane, to_block = target(plane, group ^ (FLIP * odd(plane)))
            to_group = to_block ^ (FLIP * odd(to_plane))
            found.append((plane * GROUPS + group, to_plane * GROUPS + to_group))
    return found


def local(coeffs, synthesis, projection, turn_projection, damping):
    group = lax.axis_index("harm")
    plane = lax.axis_index("space")
    both = ("space", "harm")
    everyone = ("harm", "space")
    position = group * SPACES + plane
    forward_x, forward_z, forward_y, back_z, back_y, back_x = tables()
    directions = sphere_directions()
    own = coeffs.reshape(OWN, NY, NX)
    group_arg = group.astype(jnp.int32).reshape(1)
    block_arg = group_arg ^ (FLIP * odd(plane)).astype(jnp.int32)

    chunks = call(
        regroup_kernel, [shape(PAD, CELLS)] * GROUPS, [block_arg, own],
        [pltpu.VMEM((PAD * (ROWS + 2 * PAD), LANES), f32)] * 2, 1, 0, 4 << 20,
    )
    arrived = [chunks[0]]
    for j in range(1, GROUPS):
        arrived.append(lax.ppermute(chunks[j], "harm", [(i, i ^ j) for i in range(GROUPS)]))
    own, _ = lax.optimization_barrier((own, chunks))

    table = stress_table(synthesis, directions, group)
    high, low = split_table(forward_x)
    sent = call(
        stress_kernel, shape(NX, 10 * HALF), [table, own, high, low],
        [pltpu.VMEM((5, NY, NX), bf16)] * 2, 1, 1 << 30, 3 << 20,
    )
    sent, arrived[:AHEAD] = lax.optimization_barrier((sent, arrived[:AHEAD]))
    columns = lax.all_to_all(sent, everyone, 0, 0, tiled=True)

    wave = (position % HALF).astype(f32) * (2.0 * math.pi / NX)
    half = (position // HALF).astype(jnp.int32)
    bz_high, bz_low = split_table(back_z)
    sent = call(
        solve_kernel, shape(NX, 16 * ROWS),
        [
            wave.reshape(1), half.reshape(1),
            signed_wave(NY).astype(np.float32)[None, :], signed_wave(NZ).astype(np.float32)[:, None],
            columns, *split_table(forward_z), *split_table(forward_y),
            np.concatenate([bz_high, bz_high, bz_low], axis=1), *split_table(back_y),
        ],
        (), 2, 1 << 30, 3 << 20,
    )
    mixed = lax.all_to_all(sent, everyone, 0, 0, tiled=True)
    arrived, _ = lax.optimization_barrier((arrived, sent))
    center = call(assemble_kernel, shape(ALL_PAD, CELLS), [group_arg, *arrived], (), 1, 0, 4 << 20)
    z_low = lax.ppermute(center, both, pairs(lambda s, b: ((s + 1) % SPACES, b)))
    z_high = lax.ppermute(center, both, pairs(lambda s, b: ((s - 1) % SPACES, b)))

    weights = call(
        weights_kernel, shape(ALL_PAD, BLOCKS * ALL_PAD),
        [
            directions.astype(np.float32), pad_groups(synthesis, 1),
            pad_groups(projection, 0), pad_groups(turn_projection, 1),
        ],
        (), 0, 1 << 28, 1 << 20,
    )
    flow = call(fields_kernel, shape(11, ROWS, NX, dtype=f32), [mixed, *split_table(back_x)], (), 0, 1 << 29, 2 << 20)
    damp = pad_groups(damping, 0)[:, None]
    returned, parts = [], []
    for part in range(PARTS):
        def lines(first, count, part=part):
            size = (pl.Element(ALL_PAD), pl.Element(count * NX))
            return pl.BlockSpec(size, lambda i: (0, (part * CHUNK + first) * NX))

        rates = call(
            rate_kernel, shape(GROUPS, OWN, CHUNK, NX),
            [center, z_low, z_high, flow, weights, damp],
            [
                pltpu.VMEM((2, BLOCKS * ALL_PAD, NX), bf16),
                pltpu.VMEM((2, ALL_PAD, NX), f32),
                pltpu.VMEM((ALL_PAD * CHUNK, LANES), f32),
                pltpu.VMEM((ALL_PAD * CHUNK, LANES), f32),
            ],
            0, 7 << 29, 9 << 19,
            [
                lines(0, CHUNK + 2), lines(1, CHUNK), lines(1, CHUNK),
                pl.BlockSpec((11, CHUNK, NX), lambda i, part=part: (0, part, 0)), VMEM, VMEM,
            ],
        )
        parts.append(rates)
        returned.append(lax.all_to_all(rates, "harm", 0, 0, tiled=True))
    swap = pairs(lambda s, b: (s, b ^ (FLIP * odd(s))))
    late, _ = lax.optimization_barrier((flow[0:3], parts[0]))
    velocity = lax.ppermute(late, both, swap)
    rate = call(place_kernel, shape(OWN, NY, NX), [group_arg ^ block_arg, *returned], (), 1, 0, 4 << 20)
    return (rate.reshape(OWN, 1, NY, NX), velocity.reshape(3, 1, ROWS, NX))


def solution(mesh):
    in_specs = (P("harm", "space", None, None), P(), P(), P(), P())
    out_specs = (P("harm", "space", None, None), P(None, "space", "harm", None))
    return jax.shard_map(local, mesh=mesh, in_specs=in_specs, out_specs=out_specs, check_vma=False)
```

```python
import functools
import math

import jax
import jax.numpy as jnp
import ml_dtypes
import numpy as np
from jax import lax
from jax.experimental import pallas as pl
from jax.experimental.pallas import tpu as pltpu
from jax.sharding import PartitionSpec as P

activity = -3.0
swim_speed = 1.0
transl_diff = 0.25
shape_factor = 0.9
golden_angle = math.pi * (3.0 - math.sqrt(5.0))

NX, NY, NZ = 256, 256, 32
COEFS, QUAD = 120, 256
SPACES, GROUPS = 32, 8
OWN = COEFS // GROUPS
PAD = 16
ROWS = NY // GROUPS
EDGED = ROWS + 2
CELLS = EDGED * NX
HALF = NX // 2
ALL_PAD = GROUPS * PAD
LANES = 128
RUN = 8
FLIP = GROUPS // 2
PARTS = 2
CHUNK = ROWS // PARTS
BLOCKS = 13
bf16, f32 = jnp.bfloat16, jnp.float32
VMEM = pl.BlockSpec(memory_space=pltpu.VMEM)
SMEM = pl.BlockSpec(memory_space=pltpu.SMEM)
PARAMS = pltpu.CompilerParams(vmem_limit_bytes=56 * 1024 * 1024)


def split_table(table):
    high = table.astype(ml_dtypes.bfloat16)
    low = (table - high.astype(np.float64)).astype(ml_dtypes.bfloat16)
    return (high, low)


def signed_wave(length):
    index = np.arange(length)
    signed = np.where(index < length // 2, index, index - length)
    return 2.0 * math.pi / length * np.where(index == length // 2, 0, signed)


def sphere_directions():
    position = np.arange(QUAD, dtype=np.float64)
    height = 1.0 - (2.0 * position + 1.0) / QUAD
    radius = np.sqrt(1.0 - height * height)
    turning = position * golden_angle
    return np.stack([radius * np.cos(turning), radius * np.sin(turning), height])


def tables():
    x = np.arange(NX)[None, :]
    k = np.arange(HALF)[:, None]
    angle = 2.0 * math.pi * (k * x % NX) / NX
    cos_x, sin_x = np.cos(angle), np.sin(angle)
    sign = (-1.0) ** x[0]
    minus = -sin_x
    minus[0] = sign
    forward_x = np.concatenate([cos_x, minus])
    scale = 1.0 / (NX * NY * NZ)
    weight = np.where(k == 0, 1.0, 2.0) * scale
    wave = 2.0 * math.pi / NX * k
    real_x = weight * cos_x
    imag_x = -weight * sin_x
    imag_x[0] = sign * scale
    slope_real = -weight * wave * sin_x
    slope_imag = -weight * wave * cos_x
    back_x = np.concatenate([real_x, imag_x, slope_real, slope_imag], axis=1)
    back_x = np.concatenate([back_x, back_x])

    z = np.arange(NZ)
    angle = 2.0 * math.pi * (z[:, None] * z[None, :] % NZ) / NZ
    both_z = np.concatenate([np.cos(angle), np.sin(angle)])
    forward_z = np.tile(both_z, (1, GROUPS))

    y = np.arange(HALF)[:, None]
    ky = np.arange(NY)[None, :]
    angle = 2.0 * math.pi * (y * ky % NY) / NY
    forward_y = np.block([[np.cos(angle), -np.sin(angle)], [np.sin(angle), np.cos(angle)]])

    ky = np.arange(NY)[:, None]
    angle = 2.0 * math.pi * (ky * np.arange(NY)[None, :] % NY) / NY
    cos_y = np.cos(angle).reshape(NY, GROUPS, 1, ROWS)
    sin_y = np.sin(angle).reshape(NY, GROUPS, 1, ROWS)
    from_real = np.concatenate([cos_y, sin_y], axis=2).reshape(NY, 2 * NY)
    from_imag = np.concatenate([-sin_y, cos_y], axis=2).reshape(NY, 2 * NY)
    back_y = np.concatenate([from_real, from_imag])
    return forward_x, forward_z, forward_y, both_z, back_y, back_x


def halves(value):
    high = value.astype(bf16)
    return high, (value - high.astype(f32)).astype(bf16)


def dot(a, b):
    return jnp.dot(a, b, preferred_element_type=f32)


def regroup_kernel(block_ref, coef_ref, *refs):
    outs, stages = refs[:GROUPS], refs[GROUPS:]
    block = block_ref[0]
    height = ROWS + 2 * PAD
    for stage in stages:
        stage[pl.ds(OWN * height, height), :] = jnp.zeros((height, LANES), f32)
    for j in range(GROUPS):
        first = (block ^ j) * ROWS
        for start, size, at in ((NY - PAD, PAD, 0), (0, ROWS, PAD), (ROWS, PAD, PAD + ROWS)):
            rows = coef_ref[:, pl.ds(pl.multiple_of((first + start) % NY, PAD), size), :].astype(f32)
            for side, stage in enumerate(stages):
                for c in range(OWN):
                    stage[c * height + at : c * height + at + size, :] = rows[
                        c, :, side * LANES : (side + 1) * LANES
                    ]
        for side, stage in enumerate(stages):
            for r in range(EDGED):
                lane = r * NX + side * LANES
                rows = stage[pl.ds(PAD - 1 + r, PAD, stride=height), :]
                outs[j][:, lane : lane + LANES] = rows.astype(bf16)


def stress_kernel(table_ref, coef_ref, high_ref, low_ref, out_ref, stress_high, stress_low):
    step = 32

    def rows(i, carry):
        first = pl.multiple_of(i * step, step)
        sums = [jnp.zeros((step, NX), f32)] * 5
        for c in range(OWN):
            value = coef_ref[c, pl.ds(first, step), :].astype(f32)
            sums = [s + table_ref[r, c] * value for r, s in enumerate(sums)]
        for r in range(5):
            high, low = halves(sums[r])
            stress_high[r, pl.ds(first, step), :] = high
            stress_low[r, pl.ds(first, step), :] = low
        return carry

    lax.fori_loop(0, NY // step, rows, 0)

    def across(a, b):
        return lax.dot_general(a, b, (((1,), (1,)), ((), ())), preferred_element_type=f32)

    for r in range(5):
        high, low = high_ref[...], low_ref[...]
        result = (
            across(high, stress_high[r]) + across(low, stress_high[r]) + across(high, stress_low[r])
        ).astype(bf16)
        for half in range(2):
            for part in range(2):
                lane = (2 * r + part) * HALF
                out_ref[half * HALF : (half + 1) * HALF, lane : lane + HALF] = result[
                    part * HALF : (part + 1) * HALF, half * HALF : (half + 1) * HALF
                ]


def solve_kernel(
    wave_ref, half_ref, ky_ref, kz_ref, recv_ref,
    fz_high, fz_low, fy_high, fy_low, bz, by_high, by_low, out_ref,
):
    recv = recv_ref[...]
    by_z = dot(fz_high[...], recv) + dot(fz_low[...], recv)
    lines = []
    for r in range(5):
        lane = 2 * r * HALF
        cos_re, cos_im = by_z[:NZ, lane : lane + HALF], by_z[:NZ, lane + HALF : lane + 2 * HALF]
        sin_re, sin_im = by_z[NZ:, lane : lane + HALF], by_z[NZ:, lane + HALF : lane + 2 * HALF]
        lines.append(jnp.concatenate([cos_re + sin_im, cos_im - sin_re], axis=1))
    high, low = halves(jnp.concatenate(lines))
    spec = dot(high, fy_high[...]) + dot(low, fy_high[...]) + dot(high, fy_low[...])
    lane = lax.broadcasted_iota(jnp.int32, (NZ, NY), 1)
    flip = jnp.where((lane % 2) * half_ref[0] == 1, -1.0, 1.0)
    real = [spec[r * NZ : (r + 1) * NZ, :NY] * flip for r in range(5)]
    imag = [spec[r * NZ : (r + 1) * NZ, NY:] * flip for r in range(5)]
    kx = jnp.full((NZ, NY), wave_ref[0], f32)
    ky = jnp.broadcast_to(ky_ref[...], (NZ, NY))
    kz = jnp.broadcast_to(kz_ref[...], (NZ, NY))
    square = kx * kx + ky * ky + kz * kz
    inverse = jnp.where(square > 0, 1.0 / jnp.where(square > 0, square, 1.0), 0.0)

    def force(part):
        xx, yy, xy, xz, yz = part
        return (
            kx * xx + ky * xy + kz * xz,
            kx * xy + ky * yy + kz * yz,
            kx * xz + ky * yz,
        )

    def solve(f):
        along = (kx * f[0] + ky * f[1] + kz * f[2]) * inverse
        return [(f[i] - k * along) * inverse for i, k in enumerate((kx, ky, kz))]

    flow_re = solve([-f for f in force(imag)])
    flow_im = solve(force(real))
    fields = list(zip(flow_re, flow_im))
    fields += [(-ky * flow_im[i], ky * flow_re[i]) for i in range(3)]
    fields += [(-kz * flow_im[i], kz * flow_re[i]) for i in range(2)]
    back = []
    for re, im in fields:
        high, low = halves(jnp.concatenate([re, im], axis=1))
        both = dot(bz[...], jnp.concatenate([high, low, high]))
        back.append(
            jnp.concatenate(
                [both[:NZ, :NY] - both[NZ:, NY:], both[:NZ, NY:] + both[NZ:, :NY]], axis=1
            )
        )
    high, low = halves(jnp.concatenate(back))
    done = dot(high, by_high[...]) + dot(low, by_high[...]) + dot(high, by_low[...])
    blocks = []
    for h in range(GROUPS):
        lane = 2 * ROWS * h
        pieces = [done[f * NZ : (f + 1) * NZ, lane : lane + 2 * ROWS] for f in range(8)]
        blocks.append(jnp.concatenate(pieces, axis=1))
    plane = lax.broadcasted_iota(jnp.int32, blocks[0].shape, 0)
    flipped = (plane // RUN) % 2 == 1
    for h in range(GROUPS):
        value = jnp.where(flipped, blocks[h ^ FLIP], blocks[h])
        out_ref[h * NZ : (h + 1) * NZ, :] = value.astype(bf16)


def fields_kernel(recv_ref, high_ref, low_ref, out_ref):
    flat = recv_ref[...].astype(f32).T.astype(bf16)
    both = dot(flat, high_ref[...]) + dot(flat, low_ref[...])

    def field(f, lane):
        row = 2 * ROWS * f
        return (
            both[row : row + ROWS, lane : lane + NX]
            + both[row + ROWS : row + 2 * ROWS, lane + NX : lane + 2 * NX]
        )

    for i in range(3):
        out_ref[i] = field(i, 0)
        out_ref[3 + i] = field(i, 2 * NX)
    for i in range(5):
        out_ref[6 + i] = field(3 + i, 0)


def weights_kernel(dir_ref, synth_ref, proj_ref, turn_ref, out_ref):
    synth = synth_ref[...]
    p = [dir_ref[j : j + 1, :] for j in range(3)]
    proj = proj_ref[...].astype(f32)
    turn = [turn_ref[k].astype(f32) for k in range(3)]
    radial = turn[0] * p[0] + turn[1] * p[1] + turn[2] * p[2]
    same = 0.5 * (shape_factor + 1.0)
    swap = 0.5 * (shape_factor - 1.0)

    def plain(i, j):
        return turn[i] * p[j] - radial * (p[i] * p[j])

    def strain(i, j):
        return same * plain(i, j) + swap * plain(j, i)

    left = [-0.5 * swim_speed * proj * p[j] for j in range(2)] + [-0.5 * proj]
    trace = strain(2, 2)
    left += [strain(0, 0) - trace, strain(1, 0), strain(2, 0)]
    left += [strain(0, 1), strain(1, 1) - trace, strain(2, 1)]
    left += [strain(0, 2), strain(1, 2)]
    left += [-0.5 * swim_speed * proj * p[2], -0.5 * proj]
    for n, value in enumerate(left):
        high, low = halves(value)
        out_ref[:, n * ALL_PAD : (n + 1) * ALL_PAD] = (dot(high, synth) + dot(low, synth)).astype(bf16)


def assemble_kernel(group_ref, *refs):
    out_ref = refs[GROUPS]
    group = group_ref[0]
    for j in range(GROUPS):
        out_ref[pl.ds(pl.multiple_of((group ^ j) * PAD, PAD), PAD), :] = refs[j][...]


def inner_kernel(center_ref, flow_ref, weight_ref, damp_ref, out_ref, operands, locals_):
    blocks = BLOCKS - 2

    def build(r, operand, local_terms):
        here = pl.multiple_of(r * NX, NX)
        flow = [flow_ref[f, pl.ds(r, 1), :] for f in range(11)]
        for g in range(GROUPS):
            rows = slice(g * PAD, (g + 1) * PAD)
            value = center_ref[rows, pl.ds(here + NX, NX)].astype(f32)
            y_low = center_ref[rows, pl.ds(here, NX)].astype(f32)
            y_high = center_ref[rows, pl.ds(here + 2 * NX, NX)].astype(f32)
            x_low = pltpu.roll(value, 1, 1)
            x_high = pltpu.roll(value, NX - 1, 1)
            diff_x, diff_y = x_high - x_low, y_high - y_low
            lap = x_high + x_low + y_high + y_low - 6.0 * value
            local_terms[rows, :] = transl_diff * lap - damp_ref[rows, :] * value
            terms = [diff_x, diff_y, flow[0] * diff_x + flow[1] * diff_y]
            terms += [flow[3 + n] * value for n in range(8)]
            for n, term in enumerate(terms):
                operand[n * ALL_PAD + g * PAD : n * ALL_PAD + (g + 1) * PAD, :] = term.astype(bf16)

    def rows(i, carry):
        for n in range(2):
            build(2 * i + n, operands.at[n], locals_.at[n])
        for n in range(2):
            where = pl.ds(pl.multiple_of((2 * i + n) * NX, NX), NX)
            out_ref[:, where] = locals_[n] + dot(weight_ref[:, : blocks * ALL_PAD], operands[n])
        return carry

    lax.fori_loop(0, ROWS // 2, rows, 0)


def rate_kernel(
    inner_ref, zlow_ref, zhigh_ref, flow_ref, weight_ref, out_ref, operands, locals_, *stages
):
    skip = (BLOCKS - 2) * ALL_PAD

    def build(r, operand, local_terms):
        here = pl.multiple_of(r * NX, NX)
        drift = flow_ref[2, pl.ds(r, 1), :]
        for g in range(GROUPS):
            rows = slice(g * PAD, (g + 1) * PAD)
            z_low = zlow_ref[rows, pl.ds(here, NX)].astype(f32)
            z_high = zhigh_ref[rows, pl.ds(here, NX)].astype(f32)
            diff_z = z_high - z_low
            local_terms[rows, :] = transl_diff * (z_high + z_low) + inner_ref[rows, pl.ds(here, NX)]
            operand[rows, :] = diff_z.astype(bf16)
            operand[ALL_PAD + g * PAD : ALL_PAD + (g + 1) * PAD, :] = (drift * diff_z).astype(bf16)

    def rows(i, carry):
        for n in range(2):
            build(2 * i + n, operands.at[n], locals_.at[n])
        for n in range(2):
            result = dot(weight_ref[:, skip:], operands[n]) + locals_[n]
            for side, stage in enumerate(stages):
                stage[pl.ds(2 * i + n, ALL_PAD, stride=CHUNK), :] = result[
                    :, side * LANES : (side + 1) * LANES
                ]
        return carry

    lax.fori_loop(0, CHUNK // 2, rows, 0)
    for g in range(GROUPS):
        for c in range(OWN):
            first = (g * PAD + c) * CHUNK
            for side, stage in enumerate(stages):
                out_ref[g, c, :, side * LANES : (side + 1) * LANES] = stage[
                    first : first + CHUNK, :
                ].astype(bf16)


def place_kernel(swap_ref, *refs):
    out_ref = refs[-1]
    for part in range(PARTS):
        for g in range(GROUPS):
            first = pl.multiple_of((swap_ref[0] ^ g) * ROWS + part * CHUNK, CHUNK)
            out_ref[:, pl.ds(first, CHUNK), :] = refs[part][g]


def call(kernel, out_shape, ins, scratch=(), scalars=0, flops=0, byte_count=0, specs=None):
    return pl.pallas_call(
        kernel,
        out_shape=out_shape,
        grid=(1,) if specs else (),
        in_specs=specs or [SMEM] * scalars + [VMEM] * (len(ins) - scalars),
        out_specs=jax.tree.map(lambda _: VMEM, out_shape),
        scratch_shapes=list(scratch),
        compiler_params=PARAMS,
        cost_estimate=pl.CostEstimate(flops=flops, bytes_accessed=byte_count, transcendentals=0),
    )(*ins)


def shape(*dims, dtype=bf16):
    return jax.ShapeDtypeStruct(dims, dtype)


def pad_groups(value, axis):
    parts = value.reshape(*value.shape[:axis], GROUPS, OWN, *value.shape[axis + 1 :])
    widths = [(0, 0)] * parts.ndim
    widths[axis + 1] = (0, PAD - OWN)
    parts = jnp.pad(parts, widths)
    return parts.reshape(*value.shape[:axis], ALL_PAD, *value.shape[axis + 1 :])


def stress_table(synthesis, directions, group):
    dir_x, dir_y, dir_z = directions
    third = 1.0 / 3.0
    moments = np.stack(
        [
            dir_x * dir_x - third,
            dir_y * dir_y - third,
            dir_z * dir_z - third,
            dir_x * dir_y,
            dir_x * dir_z,
            dir_y * dir_z,
        ]
    ).astype(np.float32)
    own = lax.dynamic_slice_in_dim(synthesis, group * OWN, OWN, 1).astype(f32)
    table = jnp.dot(moments, own, precision=lax.Precision.HIGHEST)
    table = (table * (activity / math.sqrt(QUAD))).astype(bf16).astype(f32)
    return jnp.concatenate([table[0:2] - table[2:3], table[3:6]])


def partner(j):
    return [(i, i ^ j) for i in range(GROUPS)]


def exchanged(chunks):
    return [chunks[0]] + [lax.ppermute(c, "harm", partner(j + 1)) for j, c in enumerate(chunks[1:])]


def odd(plane):
    return (plane // RUN) % 2


def pairs(target):
    found = []
    for plane in range(SPACES):
        for group in range(GROUPS):
            to_plane, to_block = target(plane, group ^ (FLIP * odd(plane)))
            to_group = to_block ^ (FLIP * odd(to_plane))
            found.append((plane * GROUPS + group, to_plane * GROUPS + to_group))
    return found


def local(coeffs, synthesis, projection, turn_projection, damping):
    group = lax.axis_index("harm")
    plane = lax.axis_index("space")
    both = ("space", "harm")
    everyone = ("harm", "space")
    position = group * SPACES + plane
    forward_x, forward_z, forward_y, back_z, back_y, back_x = tables()
    directions = sphere_directions()
    own = coeffs.reshape(OWN, NY, NX)
    group_arg = group.astype(jnp.int32).reshape(1)
    block_arg = group_arg ^ (FLIP * odd(plane)).astype(jnp.int32)

    table = stress_table(synthesis, directions, group)
    high, low = split_table(forward_x)
    sent = call(
        stress_kernel, shape(NX, 10 * HALF), [table, own, high, low],
        [pltpu.VMEM((5, NY, NX), bf16)] * 2, 1, 1 << 30, 3 << 20,
    )
    columns = lax.all_to_all(sent, everyone, 0, 0, tiled=True)

    later, _ = lax.optimization_barrier((own, sent))
    chunks = call(
        regroup_kernel, [shape(PAD, CELLS)] * GROUPS, [block_arg, later],
        [pltpu.VMEM((PAD * (ROWS + 2 * PAD), LANES), f32)] * 2, 1, 0, 4 << 20,
    )
    arrived = exchanged(chunks)

    wave = (position % HALF).astype(f32) * (2.0 * math.pi / NX)
    half = (position // HALF).astype(jnp.int32)
    bz_high, bz_low = split_table(back_z)
    sent = call(
        solve_kernel, shape(NX, 16 * ROWS),
        [
            wave.reshape(1), half.reshape(1),
            signed_wave(NY).astype(np.float32)[None, :], signed_wave(NZ).astype(np.float32)[:, None],
            columns, *split_table(forward_z), *split_table(forward_y),
            np.concatenate([bz_high, bz_high, bz_low], axis=1), *split_table(back_y),
        ],
        (), 2, 1 << 30, 3 << 20,
    )
    mixed = lax.all_to_all(sent, everyone, 0, 0, tiled=True)
    arrived, _ = lax.optimization_barrier((arrived, sent))
    center = call(assemble_kernel, shape(ALL_PAD, CELLS), [group_arg, *arrived], (), 1, 1 << 32, 4 << 20)
    z_low = lax.ppermute(center, both, pairs(lambda s, b: ((s + 1) % SPACES, b)))
    z_high = lax.ppermute(center, both, pairs(lambda s, b: ((s - 1) % SPACES, b)))

    weights = call(
        weights_kernel, shape(ALL_PAD, BLOCKS * ALL_PAD),
        [
            directions.astype(np.float32), pad_groups(synthesis, 1),
            pad_groups(projection, 0), pad_groups(turn_projection, 1),
        ],
        (), 0, 1 << 28, 1 << 20,
    )
    flow = call(fields_kernel, shape(11, ROWS, NX, dtype=f32), [mixed, *split_table(back_x)], (), 0, 1 << 29, 2 << 20)
    damp = pad_groups(damping, 0)[:, None]
    inner = call(
        inner_kernel, shape(ALL_PAD, ROWS * NX, dtype=f32), [center, flow, weights, damp],
        [pltpu.VMEM((2, (BLOCKS - 2) * ALL_PAD, NX), bf16), pltpu.VMEM((2, ALL_PAD, NX), f32)],
        0, 1 << 37, 7 << 20,
    )
    returned, parts = [], []
    for part in range(PARTS):
        here = pl.BlockSpec((ALL_PAD, CHUNK * NX), lambda i, part=part: (0, part))
        beyond = pl.BlockSpec(
            (pl.Element(ALL_PAD), pl.Element(CHUNK * NX)), lambda i, part=part: (0, (part * CHUNK + 1) * NX)
        )
        rates = call(
            rate_kernel, shape(GROUPS, OWN, CHUNK, NX),
            [inner, z_low, z_high, flow, weights],
            [
                pltpu.VMEM((2, 2 * ALL_PAD, NX), bf16),
                pltpu.VMEM((2, ALL_PAD, NX), f32),
                pltpu.VMEM((ALL_PAD * CHUNK, LANES), f32),
                pltpu.VMEM((ALL_PAD * CHUNK, LANES), f32),
            ],
            0, 1 << 29, 9 << 19,
            [
                here, beyond, beyond,
                pl.BlockSpec((11, CHUNK, NX), lambda i, part=part: (0, part, 0)), VMEM,
            ],
        )
        parts.append(rates)
        returned.append(lax.all_to_all(rates, "harm", 0, 0, tiled=True))
    swap = pairs(lambda s, b: (s, b ^ (FLIP * odd(s))))
    late, _ = lax.optimization_barrier((flow[0:3], parts[0]))
    velocity = lax.ppermute(late, both, swap)
    rate = call(place_kernel, shape(OWN, NY, NX), [group_arg ^ block_arg, *returned], (), 1, 0, 4 << 20)
    return (rate.reshape(OWN, 1, NY, NX), velocity.reshape(3, 1, ROWS, NX))


def solution(mesh):
    in_specs = (P("harm", "space", None, None), P(), P(), P(), P())
    out_specs = (P("harm", "space", None, None), P(None, "space", "harm", None))
    return jax.shard_map(local, mesh=mesh, in_specs=in_specs, out_specs=out_specs, check_vma=False)
```

```python
import functools
import math

import jax
import jax.numpy as jnp
import ml_dtypes
import numpy as np
from jax import lax
from jax.experimental import pallas as pl
from jax.experimental.pallas import tpu as pltpu
from jax.sharding import PartitionSpec as P

activity = -3.0
swim_speed = 1.0
transl_diff = 0.25
shape_factor = 0.9
golden_angle = math.pi * (3.0 - math.sqrt(5.0))

NX, NY, NZ = 256, 256, 32
COEFS, QUAD = 120, 256
SPACES, GROUPS = 32, 8
OWN = COEFS // GROUPS
PAD = 16
ROWS = NY // GROUPS
EDGED = ROWS + 2
CELLS = EDGED * NX
HALF = NX // 2
ALL_PAD = GROUPS * PAD
LANES = 128
RUN = 8
FLIP = GROUPS // 2
PARTS = 2
CHUNK = ROWS // PARTS
BLOCKS = 13
bf16, f32 = jnp.bfloat16, jnp.float32
VMEM = pl.BlockSpec(memory_space=pltpu.VMEM)
SMEM = pl.BlockSpec(memory_space=pltpu.SMEM)
PARAMS = pltpu.CompilerParams(vmem_limit_bytes=56 * 1024 * 1024)


def split_table(table):
    high = table.astype(ml_dtypes.bfloat16)
    low = (table - high.astype(np.float64)).astype(ml_dtypes.bfloat16)
    return (high, low)


def signed_wave(length):
    index = np.arange(length)
    signed = np.where(index < length // 2, index, index - length)
    return 2.0 * math.pi / length * np.where(index == length // 2, 0, signed)


def sphere_directions():
    position = np.arange(QUAD, dtype=np.float64)
    height = 1.0 - (2.0 * position + 1.0) / QUAD
    radius = np.sqrt(1.0 - height * height)
    turning = position * golden_angle
    return np.stack([radius * np.cos(turning), radius * np.sin(turning), height])


def tables():
    x = np.arange(NX)[None, :]
    k = np.arange(HALF)[:, None]
    angle = 2.0 * math.pi * (k * x % NX) / NX
    cos_x, sin_x = np.cos(angle), np.sin(angle)
    sign = (-1.0) ** x[0]
    minus = -sin_x
    minus[0] = sign
    forward_x = np.concatenate([cos_x, minus])
    scale = 1.0 / (NX * NY * NZ)
    weight = np.where(k == 0, 1.0, 2.0) * scale
    wave = 2.0 * math.pi / NX * k
    real_x = weight * cos_x
    imag_x = -weight * sin_x
    imag_x[0] = sign * scale
    slope_real = -weight * wave * sin_x
    slope_imag = -weight * wave * cos_x
    back_x = np.concatenate([real_x, imag_x, slope_real, slope_imag], axis=1)
    back_x = np.concatenate([back_x, back_x])

    z = np.arange(NZ)
    angle = 2.0 * math.pi * (z[:, None] * z[None, :] % NZ) / NZ
    both_z = np.concatenate([np.cos(angle), np.sin(angle)])
    forward_z = np.tile(both_z, (1, GROUPS))

    y = np.arange(HALF)[:, None]
    ky = np.arange(NY)[None, :]
    angle = 2.0 * math.pi * (y * ky % NY) / NY
    forward_y = np.block([[np.cos(angle), -np.sin(angle)], [np.sin(angle), np.cos(angle)]])

    ky = np.arange(NY)[:, None]
    angle = 2.0 * math.pi * (ky * np.arange(NY)[None, :] % NY) / NY
    cos_y = np.cos(angle).reshape(NY, GROUPS, 1, ROWS)
    sin_y = np.sin(angle).reshape(NY, GROUPS, 1, ROWS)
    from_real = np.concatenate([cos_y, sin_y], axis=2).reshape(NY, 2 * NY)
    from_imag = np.concatenate([-sin_y, cos_y], axis=2).reshape(NY, 2 * NY)
    back_y = np.concatenate([from_real, from_imag])
    return forward_x, forward_z, forward_y, both_z, back_y, back_x


def halves(value):
    high = value.astype(bf16)
    return high, (value - high.astype(f32)).astype(bf16)


def dot(a, b):
    return jnp.dot(a, b, preferred_element_type=f32)


def regroup_kernel(block_ref, coef_ref, *refs):
    outs, stages = refs[:GROUPS], refs[GROUPS:]
    block = block_ref[0]
    height = ROWS + 2 * PAD
    for stage in stages:
        stage[pl.ds(OWN * height, height), :] = jnp.zeros((height, LANES), f32)
    for j in range(GROUPS):
        first = (block ^ j) * ROWS
        for start, size, at in ((NY - PAD, PAD, 0), (0, ROWS, PAD), (ROWS, PAD, PAD + ROWS)):
            rows = coef_ref[:, pl.ds(pl.multiple_of((first + start) % NY, PAD), size), :].astype(f32)
            for side, stage in enumerate(stages):
                for c in range(OWN):
                    stage[c * height + at : c * height + at + size, :] = rows[
                        c, :, side * LANES : (side + 1) * LANES
                    ]
        for side, stage in enumerate(stages):
            for r in range(EDGED):
                lane = r * NX + side * LANES
                rows = stage[pl.ds(PAD - 1 + r, PAD, stride=height), :]
                outs[j][:, lane : lane + LANES] = rows.astype(bf16)


def stress_kernel(table_ref, coef_ref, high_ref, low_ref, out_ref, stress_high, stress_low):
    step = 32

    def rows(i, carry):
        first = pl.multiple_of(i * step, step)
        sums = [jnp.zeros((step, NX), f32)] * 5
        for c in range(OWN):
            value = coef_ref[c, pl.ds(first, step), :].astype(f32)
            sums = [s + table_ref[r, c] * value for r, s in enumerate(sums)]
        for r in range(5):
            high, low = halves(sums[r])
            stress_high[r, pl.ds(first, step), :] = high
            stress_low[r, pl.ds(first, step), :] = low
        return carry

    lax.fori_loop(0, NY // step, rows, 0)

    def across(a, b):
        return lax.dot_general(a, b, (((1,), (1,)), ((), ())), preferred_element_type=f32)

    for r in range(5):
        high, low = high_ref[...], low_ref[...]
        result = (
            across(high, stress_high[r]) + across(low, stress_high[r]) + across(high, stress_low[r])
        ).astype(bf16)
        for half in range(2):
            for part in range(2):
                lane = (2 * r + part) * HALF
                out_ref[half * HALF : (half + 1) * HALF, lane : lane + HALF] = result[
                    part * HALF : (part + 1) * HALF, half * HALF : (half + 1) * HALF
                ]


def solve_kernel(
    wave_ref, half_ref, ky_ref, kz_ref, recv_ref,
    fz_high, fz_low, fy_high, fy_low, bz, by_high, by_low, out_ref,
):
    recv = recv_ref[...]
    by_z = dot(fz_high[...], recv) + dot(fz_low[...], recv)
    lines = []
    for r in range(5):
        lane = 2 * r * HALF
        cos_re, cos_im = by_z[:NZ, lane : lane + HALF], by_z[:NZ, lane + HALF : lane + 2 * HALF]
        sin_re, sin_im = by_z[NZ:, lane : lane + HALF], by_z[NZ:, lane + HALF : lane + 2 * HALF]
        lines.append(jnp.concatenate([cos_re + sin_im, cos_im - sin_re], axis=1))
    high, low = halves(jnp.concatenate(lines))
    spec = dot(high, fy_high[...]) + dot(low, fy_high[...]) + dot(high, fy_low[...])
    lane = lax.broadcasted_iota(jnp.int32, (NZ, NY), 1)
    flip = jnp.where((lane % 2) * half_ref[0] == 1, -1.0, 1.0)
    real = [spec[r * NZ : (r + 1) * NZ, :NY] * flip for r in range(5)]
    imag = [spec[r * NZ : (r + 1) * NZ, NY:] * flip for r in range(5)]
    kx = jnp.full((NZ, NY), wave_ref[0], f32)
    ky = jnp.broadcast_to(ky_ref[...], (NZ, NY))
    kz = jnp.broadcast_to(kz_ref[...], (NZ, NY))
    square = kx * kx + ky * ky + kz * kz
    inverse = jnp.where(square > 0, 1.0 / jnp.where(square > 0, square, 1.0), 0.0)

    def force(part):
        xx, yy, xy, xz, yz = part
        return (
            kx * xx + ky * xy + kz * xz,
            kx * xy + ky * yy + kz * yz,
            kx * xz + ky * yz,
        )

    def solve(f):
        along = (kx * f[0] + ky * f[1] + kz * f[2]) * inverse
        return [(f[i] - k * along) * inverse for i, k in enumerate((kx, ky, kz))]

    flow_re = solve([-f for f in force(imag)])
    flow_im = solve(force(real))
    fields = list(zip(flow_re, flow_im))
    fields += [(-ky * flow_im[i], ky * flow_re[i]) for i in range(3)]
    fields += [(-kz * flow_im[i], kz * flow_re[i]) for i in range(2)]
    back = []
    for re, im in fields:
        high, low = halves(jnp.concatenate([re, im], axis=1))
        both = dot(bz[...], jnp.concatenate([high, low, high]))
        back.append(
            jnp.concatenate(
                [both[:NZ, :NY] - both[NZ:, NY:], both[:NZ, NY:] + both[NZ:, :NY]], axis=1
            )
        )
    high, low = halves(jnp.concatenate(back))
    done = dot(high, by_high[...]) + dot(low, by_high[...]) + dot(high, by_low[...])
    blocks = []
    for h in range(GROUPS):
        lane = 2 * ROWS * h
        pieces = [done[f * NZ : (f + 1) * NZ, lane : lane + 2 * ROWS] for f in range(8)]
        blocks.append(jnp.concatenate(pieces, axis=1))
    plane = lax.broadcasted_iota(jnp.int32, blocks[0].shape, 0)
    flipped = (plane // RUN) % 2 == 1
    for h in range(GROUPS):
        value = jnp.where(flipped, blocks[h ^ FLIP], blocks[h])
        out_ref[h * NZ : (h + 1) * NZ, :] = value.astype(bf16)


def fields_kernel(recv_ref, high_ref, low_ref, out_ref):
    flat = recv_ref[...].astype(f32).T.astype(bf16)
    both = dot(flat, high_ref[...]) + dot(flat, low_ref[...])

    def field(f, lane):
        row = 2 * ROWS * f
        return (
            both[row : row + ROWS, lane : lane + NX]
            + both[row + ROWS : row + 2 * ROWS, lane + NX : lane + 2 * NX]
        )

    for i in range(3):
        out_ref[i] = field(i, 0)
        out_ref[3 + i] = field(i, 2 * NX)
    for i in range(5):
        out_ref[6 + i] = field(3 + i, 0)


def weights_kernel(dir_ref, synth_ref, proj_ref, turn_ref, out_ref):
    synth = synth_ref[...]
    p = [dir_ref[j : j + 1, :] for j in range(3)]
    proj = proj_ref[...].astype(f32)
    turn = [turn_ref[k].astype(f32) for k in range(3)]
    radial = turn[0] * p[0] + turn[1] * p[1] + turn[2] * p[2]
    same = 0.5 * (shape_factor + 1.0)
    swap = 0.5 * (shape_factor - 1.0)

    def plain(i, j):
        return turn[i] * p[j] - radial * (p[i] * p[j])

    def strain(i, j):
        return same * plain(i, j) + swap * plain(j, i)

    left = [-0.5 * swim_speed * proj * p[j] for j in range(2)] + [-0.5 * proj]
    trace = strain(2, 2)
    left += [strain(0, 0) - trace, strain(1, 0), strain(2, 0)]
    left += [strain(0, 1), strain(1, 1) - trace, strain(2, 1)]
    left += [strain(0, 2), strain(1, 2)]
    left += [-0.5 * swim_speed * proj * p[2], -0.5 * proj]
    for n, value in enumerate(left):
        high, low = halves(value)
        out_ref[:, n * ALL_PAD : (n + 1) * ALL_PAD] = (dot(high, synth) + dot(low, synth)).astype(bf16)


def assemble_kernel(group_ref, *refs):
    out_ref, *parts = refs[GROUPS:]
    group = group_ref[0]
    for j in range(GROUPS):
        where = pl.ds(pl.multiple_of((group ^ j) * PAD, PAD), PAD)
        out_ref[where, :] = refs[j][...]
        for n, part in enumerate(parts):
            part[where, :] = refs[j][:, (n * CHUNK + 1) * NX : ((n + 1) * CHUNK + 1) * NX]


def inner_kernel(center_ref, flow_ref, weight_ref, damp_ref, out_ref, operands, locals_):
    blocks = BLOCKS - 2

    def build(r, operand, local_terms):
        here = pl.multiple_of(r * NX, NX)
        flow = [flow_ref[f, pl.ds(r, 1), :] for f in range(11)]
        for g in range(GROUPS):
            rows = slice(g * PAD, (g + 1) * PAD)
            value = center_ref[rows, pl.ds(here + NX, NX)].astype(f32)
            y_low = center_ref[rows, pl.ds(here, NX)].astype(f32)
            y_high = center_ref[rows, pl.ds(here + 2 * NX, NX)].astype(f32)
            x_low = pltpu.roll(value, 1, 1)
            x_high = pltpu.roll(value, NX - 1, 1)
            diff_x, diff_y = x_high - x_low, y_high - y_low
            lap = x_high + x_low + y_high + y_low - 6.0 * value
            local_terms[rows, :] = transl_diff * lap - damp_ref[rows, :] * value
            terms = [diff_x, diff_y, flow[0] * diff_x + flow[1] * diff_y]
            terms += [flow[3 + n] * value for n in range(8)]
            for n, term in enumerate(terms):
                operand[n * ALL_PAD + g * PAD : n * ALL_PAD + (g + 1) * PAD, :] = term.astype(bf16)

    def rows(i, carry):
        for n in range(2):
            build(2 * i + n, operands.at[n], locals_.at[n])
        for n in range(2):
            where = pl.ds(pl.multiple_of((2 * i + n) * NX, NX), NX)
            out_ref[:, where] = locals_[n] + dot(weight_ref[:, : blocks * ALL_PAD], operands[n])
        return carry

    lax.fori_loop(0, ROWS // 2, rows, 0)


def rate_kernel(
    inner_ref, zlow_ref, zhigh_ref, flow_ref, weight_ref, out_ref, operands, locals_, *stages
):
    skip = (BLOCKS - 2) * ALL_PAD

    def build(r, operand, local_terms):
        here = pl.multiple_of(r * NX, NX)
        drift = flow_ref[2, pl.ds(r, 1), :]
        for g in range(GROUPS):
            rows = slice(g * PAD, (g + 1) * PAD)
            z_low = zlow_ref[rows, pl.ds(here, NX)].astype(f32)
            z_high = zhigh_ref[rows, pl.ds(here, NX)].astype(f32)
            diff_z = z_high - z_low
            local_terms[rows, :] = transl_diff * (z_high + z_low) + inner_ref[rows, pl.ds(here, NX)]
            operand[rows, :] = diff_z.astype(bf16)
            operand[ALL_PAD + g * PAD : ALL_PAD + (g + 1) * PAD, :] = (drift * diff_z).astype(bf16)

    def rows(i, carry):
        for n in range(2):
            build(2 * i + n, operands.at[n], locals_.at[n])
        for n in range(2):
            result = dot(weight_ref[:, skip:], operands[n]) + locals_[n]
            for side, stage in enumerate(stages):
                stage[pl.ds(2 * i + n, ALL_PAD, stride=CHUNK), :] = result[
                    :, side * LANES : (side + 1) * LANES
                ]
        return carry

    lax.fori_loop(0, CHUNK // 2, rows, 0)
    for g in range(GROUPS):
        for c in range(OWN):
            first = (g * PAD + c) * CHUNK
            for side, stage in enumerate(stages):
                out_ref[g, c, :, side * LANES : (side + 1) * LANES] = stage[
                    first : first + CHUNK, :
                ].astype(bf16)


def place_kernel(swap_ref, *refs):
    out_ref = refs[-1]
    for part in range(PARTS):
        for g in range(GROUPS):
            first = pl.multiple_of((swap_ref[0] ^ g) * ROWS + part * CHUNK, CHUNK)
            out_ref[:, pl.ds(first, CHUNK), :] = refs[part][g]


def call(kernel, out_shape, ins, scratch=(), scalars=0, flops=0, byte_count=0, specs=None):
    return pl.pallas_call(
        kernel,
        out_shape=out_shape,
        grid=(1,) if specs else (),
        in_specs=specs or [SMEM] * scalars + [VMEM] * (len(ins) - scalars),
        out_specs=jax.tree.map(lambda _: VMEM, out_shape),
        scratch_shapes=list(scratch),
        compiler_params=PARAMS,
        cost_estimate=pl.CostEstimate(flops=flops, bytes_accessed=byte_count, transcendentals=0),
    )(*ins)


def shape(*dims, dtype=bf16):
    return jax.ShapeDtypeStruct(dims, dtype)


def pad_groups(value, axis):
    parts = value.reshape(*value.shape[:axis], GROUPS, OWN, *value.shape[axis + 1 :])
    widths = [(0, 0)] * parts.ndim
    widths[axis + 1] = (0, PAD - OWN)
    parts = jnp.pad(parts, widths)
    return parts.reshape(*value.shape[:axis], ALL_PAD, *value.shape[axis + 1 :])


def stress_table(synthesis, directions, group):
    dir_x, dir_y, dir_z = directions
    third = 1.0 / 3.0
    moments = np.stack(
        [
            dir_x * dir_x - third,
            dir_y * dir_y - third,
            dir_z * dir_z - third,
            dir_x * dir_y,
            dir_x * dir_z,
            dir_y * dir_z,
        ]
    ).astype(np.float32)
    own = lax.dynamic_slice_in_dim(synthesis, group * OWN, OWN, 1).astype(f32)
    table = jnp.dot(moments, own, precision=lax.Precision.HIGHEST)
    table = (table * (activity / math.sqrt(QUAD))).astype(bf16).astype(f32)
    return jnp.concatenate([table[0:2] - table[2:3], table[3:6]])


def partner(j):
    return [(i, i ^ j) for i in range(GROUPS)]


def exchanged(chunks):
    return [chunks[0]] + [lax.ppermute(c, "harm", partner(j + 1)) for j, c in enumerate(chunks[1:])]


def odd(plane):
    return (plane // RUN) % 2


def pairs(target):
    found = []
    for plane in range(SPACES):
        for group in range(GROUPS):
            to_plane, to_block = target(plane, group ^ (FLIP * odd(plane)))
            to_group = to_block ^ (FLIP * odd(to_plane))
            found.append((plane * GROUPS + group, to_plane * GROUPS + to_group))
    return found


def local(coeffs, synthesis, projection, turn_projection, damping):
    group = lax.axis_index("harm")
    plane = lax.axis_index("space")
    both = ("space", "harm")
    everyone = ("harm", "space")
    position = group * SPACES + plane
    forward_x, forward_z, forward_y, back_z, back_y, back_x = tables()
    directions = sphere_directions()
    own = coeffs.reshape(OWN, NY, NX)
    group_arg = group.astype(jnp.int32).reshape(1)
    block_arg = group_arg ^ (FLIP * odd(plane)).astype(jnp.int32)

    table = stress_table(synthesis, directions, group)
    high, low = split_table(forward_x)
    sent = call(
        stress_kernel, shape(NX, 10 * HALF), [table, own, high, low],
        [pltpu.VMEM((5, NY, NX), bf16)] * 2, 1, 1 << 30, 3 << 20,
    )
    columns = lax.all_to_all(sent, everyone, 0, 0, tiled=True)

    later, _ = lax.optimization_barrier((own, sent))
    chunks = call(
        regroup_kernel, [shape(PAD, CELLS)] * GROUPS, [block_arg, later],
        [pltpu.VMEM((PAD * (ROWS + 2 * PAD), LANES), f32)] * 2, 1, 0, 4 << 20,
    )
    arrived = exchanged(chunks)

    weights = call(
        weights_kernel, shape(ALL_PAD, BLOCKS * ALL_PAD),
        [
            directions.astype(np.float32), pad_groups(synthesis, 1),
            pad_groups(projection, 0), pad_groups(turn_projection, 1),
        ],
        (), 0, 1 << 28, 1 << 20,
    )
    columns, weights = lax.optimization_barrier((columns, weights))

    wave = (position % HALF).astype(f32) * (2.0 * math.pi / NX)
    half = (position // HALF).astype(jnp.int32)
    bz_high, bz_low = split_table(back_z)
    sent = call(
        solve_kernel, shape(NX, 16 * ROWS),
        [
            wave.reshape(1), half.reshape(1),
            signed_wave(NY).astype(np.float32)[None, :], signed_wave(NZ).astype(np.float32)[:, None],
            columns, *split_table(forward_z), *split_table(forward_y),
            np.concatenate([bz_high, bz_high, bz_low], axis=1), *split_table(back_y),
        ],
        (), 2, 1 << 30, 3 << 20,
    )
    mixed = lax.all_to_all(sent, everyone, 0, 0, tiled=True)
    arrived, _ = lax.optimization_barrier((arrived, sent))
    center, *own_parts = call(
        assemble_kernel, [shape(ALL_PAD, CELLS)] + [shape(ALL_PAD, CHUNK * NX)] * PARTS,
        [group_arg, *arrived], (), 1, 1 << 32, 4 << 20,
    )
    above = pairs(lambda s, b: ((s + 1) % SPACES, b))
    below = pairs(lambda s, b: ((s - 1) % SPACES, b))
    halo = [(lax.ppermute(rows, both, above), lax.ppermute(rows, both, below)) for rows in own_parts]

    flow = call(fields_kernel, shape(11, ROWS, NX, dtype=f32), [mixed, *split_table(back_x)], (), 0, 1 << 29, 2 << 20)
    damp = pad_groups(damping, 0)[:, None]
    inner = call(
        inner_kernel, shape(ALL_PAD, ROWS * NX, dtype=f32), [center, flow, weights, damp],
        [pltpu.VMEM((2, (BLOCKS - 2) * ALL_PAD, NX), bf16), pltpu.VMEM((2, ALL_PAD, NX), f32)],
        0, 1 << 37, 7 << 20,
    )
    returned = []
    for part in range(PARTS):
        here = pl.BlockSpec((ALL_PAD, CHUNK * NX), lambda i, part=part: (0, part))
        rates = call(
            rate_kernel, shape(GROUPS, OWN, CHUNK, NX),
            [inner, *halo[part], flow, weights],
            [
                pltpu.VMEM((2, 2 * ALL_PAD, NX), bf16),
                pltpu.VMEM((2, ALL_PAD, NX), f32),
                pltpu.VMEM((ALL_PAD * CHUNK, LANES), f32),
                pltpu.VMEM((ALL_PAD * CHUNK, LANES), f32),
            ],
            0, 1 << 33, 9 << 19,
            [
                here, VMEM, VMEM,
                pl.BlockSpec((11, CHUNK, NX), lambda i, part=part: (0, part, 0)), VMEM,
            ],
        )
        inner, rates = lax.optimization_barrier((inner, rates))
        returned, rates = lax.optimization_barrier((returned, rates))
        returned.append(lax.all_to_all(rates, "harm", 0, 0, tiled=True))
    swap = pairs(lambda s, b: (s, b ^ (FLIP * odd(s))))
    late, _ = lax.optimization_barrier((flow[0:3], rates))
    velocity = lax.ppermute(late, both, swap)
    rate = call(place_kernel, shape(OWN, NY, NX), [group_arg ^ block_arg, *returned], (), 1, 0, 4 << 20)
    return (rate.reshape(OWN, 1, NY, NX), velocity.reshape(3, 1, ROWS, NX))


def solution(mesh):
    in_specs = (P("harm", "space", None, None), P(), P(), P(), P())
    out_specs = (P("harm", "space", None, None), P(None, "space", "harm", None))
    return jax.shard_map(local, mesh=mesh, in_specs=in_specs, out_specs=out_specs, check_vma=False)
```

```python
import functools
import math

import jax
import jax.numpy as jnp
import ml_dtypes
import numpy as np
from jax import lax
from jax.experimental import pallas as pl
from jax.experimental.pallas import tpu as pltpu
from jax.sharding import PartitionSpec as P

activity = -3.0
swim_speed = 1.0
transl_diff = 0.25
shape_factor = 0.9
golden_angle = math.pi * (3.0 - math.sqrt(5.0))

NX, NY, NZ = 256, 256, 32
COEFS, QUAD = 120, 256
SPACES, GROUPS = 32, 8
OWN = COEFS // GROUPS
PAD = 16
ROWS = NY // GROUPS
EDGED = ROWS + 2
CELLS = EDGED * NX
HALF = NX // 2
ALL_PAD = GROUPS * PAD
LANES = 128
RUN = 8
FLIP = GROUPS // 2
PARTS = 2
CHUNK = ROWS // PARTS
BLOCKS = 13
bf16, f32 = jnp.bfloat16, jnp.float32
VMEM = pl.BlockSpec(memory_space=pltpu.VMEM)
SMEM = pl.BlockSpec(memory_space=pltpu.SMEM)
PARAMS = pltpu.CompilerParams(vmem_limit_bytes=56 * 1024 * 1024)


def split_table(table):
    high = table.astype(ml_dtypes.bfloat16)
    low = (table - high.astype(np.float64)).astype(ml_dtypes.bfloat16)
    return (high, low)


def signed_wave(length):
    index = np.arange(length)
    signed = np.where(index < length // 2, index, index - length)
    return 2.0 * math.pi / length * np.where(index == length // 2, 0, signed)


def sphere_directions():
    position = np.arange(QUAD, dtype=np.float64)
    height = 1.0 - (2.0 * position + 1.0) / QUAD
    radius = np.sqrt(1.0 - height * height)
    turning = position * golden_angle
    return np.stack([radius * np.cos(turning), radius * np.sin(turning), height])


def tables():
    x = np.arange(NX)[None, :]
    k = np.arange(HALF)[:, None]
    angle = 2.0 * math.pi * (k * x % NX) / NX
    cos_x, sin_x = np.cos(angle), np.sin(angle)
    sign = (-1.0) ** x[0]
    minus = -sin_x
    minus[0] = sign
    forward_x = np.concatenate([cos_x, minus])
    scale = 1.0 / (NX * NY * NZ)
    weight = np.where(k == 0, 1.0, 2.0) * scale
    wave = 2.0 * math.pi / NX * k
    real_x = weight * cos_x
    imag_x = -weight * sin_x
    imag_x[0] = sign * scale
    slope_real = -weight * wave * sin_x
    slope_imag = -weight * wave * cos_x
    back_x = np.concatenate([real_x, imag_x, slope_real, slope_imag], axis=1)
    back_x = np.concatenate([back_x, back_x])

    z = np.arange(NZ)
    angle = 2.0 * math.pi * (z[:, None] * z[None, :] % NZ) / NZ
    both_z = np.concatenate([np.cos(angle), np.sin(angle)])
    forward_z = np.tile(both_z, (1, GROUPS))

    y = np.arange(HALF)[:, None]
    ky = np.arange(NY)[None, :]
    angle = 2.0 * math.pi * (y * ky % NY) / NY
    forward_y = np.block([[np.cos(angle), -np.sin(angle)], [np.sin(angle), np.cos(angle)]])

    ky = np.arange(NY)[:, None]
    angle = 2.0 * math.pi * (ky * np.arange(NY)[None, :] % NY) / NY
    cos_y = np.cos(angle).reshape(NY, GROUPS, 1, ROWS)
    sin_y = np.sin(angle).reshape(NY, GROUPS, 1, ROWS)
    from_real = np.concatenate([cos_y, sin_y], axis=2).reshape(NY, 2 * NY)
    from_imag = np.concatenate([-sin_y, cos_y], axis=2).reshape(NY, 2 * NY)
    back_y = np.concatenate([from_real, from_imag])
    return forward_x, forward_z, forward_y, both_z, back_y, back_x


def halves(value):
    high = value.astype(bf16)
    return high, (value - high.astype(f32)).astype(bf16)


def dot(a, b):
    return jnp.dot(a, b, preferred_element_type=f32)


def regroup_kernel(block_ref, coef_ref, *refs):
    outs, stages = refs[:GROUPS], refs[GROUPS:]
    block = block_ref[0]
    height = ROWS + 2 * PAD
    for stage in stages:
        stage[pl.ds(OWN * height, height), :] = jnp.zeros((height, LANES), f32)
    for j in range(GROUPS):
        first = (block ^ j) * ROWS
        for start, size, at in ((NY - PAD, PAD, 0), (0, ROWS, PAD), (ROWS, PAD, PAD + ROWS)):
            rows = coef_ref[:, pl.ds(pl.multiple_of((first + start) % NY, PAD), size), :].astype(f32)
            for side, stage in enumerate(stages):
                for c in range(OWN):
                    stage[c * height + at : c * height + at + size, :] = rows[
                        c, :, side * LANES : (side + 1) * LANES
                    ]
        for side, stage in enumerate(stages):
            for r in range(EDGED):
                lane = r * NX + side * LANES
                rows = stage[pl.ds(PAD - 1 + r, PAD, stride=height), :]
                outs[j][:, lane : lane + LANES] = rows.astype(bf16)


def stress_kernel(table_ref, coef_ref, high_ref, low_ref, out_ref, stress_high, stress_low):
    step = 32

    def rows(i, carry):
        first = pl.multiple_of(i * step, step)
        sums = [jnp.zeros((step, NX), f32)] * 5
        for c in range(OWN):
            value = coef_ref[c, pl.ds(first, step), :].astype(f32)
            sums = [s + table_ref[r, c] * value for r, s in enumerate(sums)]
        for r in range(5):
            high, low = halves(sums[r])
            stress_high[r, pl.ds(first, step), :] = high
            stress_low[r, pl.ds(first, step), :] = low
        return carry

    lax.fori_loop(0, NY // step, rows, 0)

    def across(a, b):
        return lax.dot_general(a, b, (((1,), (1,)), ((), ())), preferred_element_type=f32)

    for r in range(5):
        high, low = high_ref[...], low_ref[...]
        result = (
            across(high, stress_high[r]) + across(low, stress_high[r]) + across(high, stress_low[r])
        ).astype(bf16)
        for half in range(2):
            for part in range(2):
                lane = (2 * r + part) * HALF
                out_ref[half * HALF : (half + 1) * HALF, lane : lane + HALF] = result[
                    part * HALF : (part + 1) * HALF, half * HALF : (half + 1) * HALF
                ]


def solve_kernel(
    wave_ref, half_ref, ky_ref, kz_ref, recv_ref,
    fz_high, fz_low, fy_high, fy_low, bz, by_high, by_low, out_ref,
):
    recv = recv_ref[...]
    by_z = dot(fz_high[...], recv) + dot(fz_low[...], recv)
    lines = []
    for r in range(5):
        lane = 2 * r * HALF
        cos_re, cos_im = by_z[:NZ, lane : lane + HALF], by_z[:NZ, lane + HALF : lane + 2 * HALF]
        sin_re, sin_im = by_z[NZ:, lane : lane + HALF], by_z[NZ:, lane + HALF : lane + 2 * HALF]
        lines.append(jnp.concatenate([cos_re + sin_im, cos_im - sin_re], axis=1))
    high, low = halves(jnp.concatenate(lines))
    spec = dot(high, fy_high[...]) + dot(low, fy_high[...]) + dot(high, fy_low[...])
    lane = lax.broadcasted_iota(jnp.int32, (NZ, NY), 1)
    flip = jnp.where((lane % 2) * half_ref[0] == 1, -1.0, 1.0)
    real = [spec[r * NZ : (r + 1) * NZ, :NY] * flip for r in range(5)]
    imag = [spec[r * NZ : (r + 1) * NZ, NY:] * flip for r in range(5)]
    kx = jnp.full((NZ, NY), wave_ref[0], f32)
    ky = jnp.broadcast_to(ky_ref[...], (NZ, NY))
    kz = jnp.broadcast_to(kz_ref[...], (NZ, NY))
    square = kx * kx + ky * ky + kz * kz
    inverse = jnp.where(square > 0, 1.0 / jnp.where(square > 0, square, 1.0), 0.0)

    def force(part):
        xx, yy, xy, xz, yz = part
        return (
            kx * xx + ky * xy + kz * xz,
            kx * xy + ky * yy + kz * yz,
            kx * xz + ky * yz,
        )

    def solve(f):
        along = (kx * f[0] + ky * f[1] + kz * f[2]) * inverse
        return [(f[i] - k * along) * inverse for i, k in enumerate((kx, ky, kz))]

    flow_re = solve([-f for f in force(imag)])
    flow_im = solve(force(real))
    fields = list(zip(flow_re, flow_im))
    fields += [(-ky * flow_im[i], ky * flow_re[i]) for i in range(3)]
    fields += [(-kz * flow_im[i], kz * flow_re[i]) for i in range(2)]
    back = []
    for re, im in fields:
        high, low = halves(jnp.concatenate([re, im], axis=1))
        both = dot(bz[...], jnp.concatenate([high, low, high]))
        back.append(
            jnp.concatenate(
                [both[:NZ, :NY] - both[NZ:, NY:], both[:NZ, NY:] + both[NZ:, :NY]], axis=1
            )
        )
    high, low = halves(jnp.concatenate(back))
    done = dot(high, by_high[...]) + dot(low, by_high[...]) + dot(high, by_low[...])
    blocks = []
    for h in range(GROUPS):
        lane = 2 * ROWS * h
        pieces = [done[f * NZ : (f + 1) * NZ, lane : lane + 2 * ROWS] for f in range(8)]
        blocks.append(jnp.concatenate(pieces, axis=1))
    plane = lax.broadcasted_iota(jnp.int32, blocks[0].shape, 0)
    flipped = (plane // RUN) % 2 == 1
    for h in range(GROUPS):
        value = jnp.where(flipped, blocks[h ^ FLIP], blocks[h])
        out_ref[h * NZ : (h + 1) * NZ, :] = value.astype(bf16)


def fields_kernel(recv_ref, high_ref, low_ref, out_ref):
    flat = recv_ref[...].astype(f32).T.astype(bf16)
    both = dot(flat, high_ref[...]) + dot(flat, low_ref[...])

    def field(f, lane):
        row = 2 * ROWS * f
        return (
            both[row : row + ROWS, lane : lane + NX]
            + both[row + ROWS : row + 2 * ROWS, lane + NX : lane + 2 * NX]
        )

    for i in range(3):
        out_ref[i] = field(i, 0)
        out_ref[3 + i] = field(i, 2 * NX)
    for i in range(5):
        out_ref[6 + i] = field(3 + i, 0)


def weights_kernel(dir_ref, synth_ref, proj_ref, turn_ref, out_ref):
    synth = synth_ref[...]
    p = [dir_ref[j : j + 1, :] for j in range(3)]
    proj = proj_ref[...].astype(f32)
    turn = [turn_ref[k].astype(f32) for k in range(3)]
    radial = turn[0] * p[0] + turn[1] * p[1] + turn[2] * p[2]
    same = 0.5 * (shape_factor + 1.0)
    swap = 0.5 * (shape_factor - 1.0)

    def plain(i, j):
        return turn[i] * p[j] - radial * (p[i] * p[j])

    def strain(i, j):
        return same * plain(i, j) + swap * plain(j, i)

    left = [-0.5 * swim_speed * proj * p[j] for j in range(2)] + [-0.5 * proj]
    trace = strain(2, 2)
    left += [strain(0, 0) - trace, strain(1, 0), strain(2, 0)]
    left += [strain(0, 1), strain(1, 1) - trace, strain(2, 1)]
    left += [strain(0, 2), strain(1, 2)]
    left += [-0.5 * swim_speed * proj * p[2], -0.5 * proj]
    for n, value in enumerate(left):
        high, low = halves(value)
        out_ref[:, n * ALL_PAD : (n + 1) * ALL_PAD] = (dot(high, synth) + dot(low, synth)).astype(bf16)


def assemble_kernel(group_ref, *refs):
    out_ref, *parts = refs[GROUPS:]
    group = group_ref[0]
    for j in range(GROUPS):
        where = pl.ds(pl.multiple_of((group ^ j) * PAD, PAD), PAD)
        out_ref[where, :] = refs[j][...]
        for n, part in enumerate(parts):
            part[where, :] = refs[j][:, (n * CHUNK + 1) * NX : ((n + 1) * CHUNK + 1) * NX]


def inner_kernel(center_ref, flow_ref, weight_ref, damp_ref, out_ref, operands, locals_):
    blocks = BLOCKS - 2

    def build(r, operand, local_terms):
        here = pl.multiple_of(r * NX, NX)
        flow = [flow_ref[f, pl.ds(r, 1), :] for f in range(11)]
        for g in range(GROUPS):
            rows = slice(g * PAD, (g + 1) * PAD)
            value = center_ref[rows, pl.ds(here + NX, NX)].astype(f32)
            y_low = center_ref[rows, pl.ds(here, NX)].astype(f32)
            y_high = center_ref[rows, pl.ds(here + 2 * NX, NX)].astype(f32)
            x_low = pltpu.roll(value, 1, 1)
            x_high = pltpu.roll(value, NX - 1, 1)
            diff_x, diff_y = x_high - x_low, y_high - y_low
            lap = x_high + x_low + y_high + y_low - 6.0 * value
            local_terms[rows, :] = transl_diff * lap - damp_ref[rows, :] * value
            terms = [diff_x, diff_y, flow[0] * diff_x + flow[1] * diff_y]
            terms += [flow[3 + n] * value for n in range(8)]
            for n, term in enumerate(terms):
                operand[n * ALL_PAD + g * PAD : n * ALL_PAD + (g + 1) * PAD, :] = term.astype(bf16)

    def rows(i, carry):
        for n in range(2):
            build(2 * i + n, operands.at[n], locals_.at[n])
        for n in range(2):
            where = pl.ds(pl.multiple_of((2 * i + n) * NX, NX), NX)
            out_ref[:, where] = locals_[n] + dot(weight_ref[:, : blocks * ALL_PAD], operands[n])
        return carry

    lax.fori_loop(0, CHUNK // 2, rows, 0)


def rate_kernel(
    inner_ref, zlow_ref, zhigh_ref, flow_ref, weight_ref, out_ref, operands, locals_, *stages
):
    skip = (BLOCKS - 2) * ALL_PAD

    def build(r, operand, local_terms):
        here = pl.multiple_of(r * NX, NX)
        drift = flow_ref[2, pl.ds(r, 1), :]
        for g in range(GROUPS):
            rows = slice(g * PAD, (g + 1) * PAD)
            z_low = zlow_ref[rows, pl.ds(here, NX)].astype(f32)
            z_high = zhigh_ref[rows, pl.ds(here, NX)].astype(f32)
            diff_z = z_high - z_low
            local_terms[rows, :] = transl_diff * (z_high + z_low) + inner_ref[rows, pl.ds(here, NX)]
            operand[rows, :] = diff_z.astype(bf16)
            operand[ALL_PAD + g * PAD : ALL_PAD + (g + 1) * PAD, :] = (drift * diff_z).astype(bf16)

    def rows(i, carry):
        for n in range(2):
            build(2 * i + n, operands.at[n], locals_.at[n])
        for n in range(2):
            result = dot(weight_ref[:, skip:], operands[n]) + locals_[n]
            for side, stage in enumerate(stages):
                stage[pl.ds(2 * i + n, ALL_PAD, stride=CHUNK), :] = result[
                    :, side * LANES : (side + 1) * LANES
                ]
        return carry

    lax.fori_loop(0, CHUNK // 2, rows, 0)
    for g in range(GROUPS):
        for c in range(OWN):
            first = (g * PAD + c) * CHUNK
            for side, stage in enumerate(stages):
                out_ref[g, c, :, side * LANES : (side + 1) * LANES] = stage[
                    first : first + CHUNK, :
                ].astype(bf16)


def place_kernel(swap_ref, *refs):
    out_ref = refs[-1]
    for part in range(PARTS):
        for g in range(GROUPS):
            first = pl.multiple_of((swap_ref[0] ^ g) * ROWS + part * CHUNK, CHUNK)
            out_ref[:, pl.ds(first, CHUNK), :] = refs[part][g]


def call(kernel, out_shape, ins, scratch=(), scalars=0, flops=0, byte_count=0, specs=None):
    return pl.pallas_call(
        kernel,
        out_shape=out_shape,
        grid=(1,) if specs else (),
        in_specs=specs or [SMEM] * scalars + [VMEM] * (len(ins) - scalars),
        out_specs=jax.tree.map(lambda _: VMEM, out_shape),
        scratch_shapes=list(scratch),
        compiler_params=PARAMS,
        cost_estimate=pl.CostEstimate(flops=flops, bytes_accessed=byte_count, transcendentals=0),
    )(*ins)


def shape(*dims, dtype=bf16):
    return jax.ShapeDtypeStruct(dims, dtype)


def pad_groups(value, axis):
    parts = value.reshape(*value.shape[:axis], GROUPS, OWN, *value.shape[axis + 1 :])
    widths = [(0, 0)] * parts.ndim
    widths[axis + 1] = (0, PAD - OWN)
    parts = jnp.pad(parts, widths)
    return parts.reshape(*value.shape[:axis], ALL_PAD, *value.shape[axis + 1 :])


def stress_table(synthesis, directions, group):
    dir_x, dir_y, dir_z = directions
    third = 1.0 / 3.0
    moments = np.stack(
        [
            dir_x * dir_x - third,
            dir_y * dir_y - third,
            dir_z * dir_z - third,
            dir_x * dir_y,
            dir_x * dir_z,
            dir_y * dir_z,
        ]
    ).astype(np.float32)
    own = lax.dynamic_slice_in_dim(synthesis, group * OWN, OWN, 1).astype(f32)
    table = jnp.dot(moments, own, precision=lax.Precision.HIGHEST)
    table = (table * (activity / math.sqrt(QUAD))).astype(bf16).astype(f32)
    return jnp.concatenate([table[0:2] - table[2:3], table[3:6]])


def partner(j):
    return [(i, i ^ j) for i in range(GROUPS)]


def exchanged(chunks):
    return [chunks[0]] + [lax.ppermute(c, "harm", partner(j + 1)) for j, c in enumerate(chunks[1:])]


def odd(plane):
    return (plane // RUN) % 2


def pairs(target):
    found = []
    for plane in range(SPACES):
        for group in range(GROUPS):
            to_plane, to_block = target(plane, group ^ (FLIP * odd(plane)))
            to_group = to_block ^ (FLIP * odd(to_plane))
            found.append((plane * GROUPS + group, to_plane * GROUPS + to_group))
    return found


def local(coeffs, synthesis, projection, turn_projection, damping):
    group = lax.axis_index("harm")
    plane = lax.axis_index("space")
    both = ("space", "harm")
    everyone = ("harm", "space")
    position = group * SPACES + plane
    forward_x, forward_z, forward_y, back_z, back_y, back_x = tables()
    directions = sphere_directions()
    own = coeffs.reshape(OWN, NY, NX)
    group_arg = group.astype(jnp.int32).reshape(1)
    block_arg = group_arg ^ (FLIP * odd(plane)).astype(jnp.int32)

    table = stress_table(synthesis, directions, group)
    high, low = split_table(forward_x)
    sent = call(
        stress_kernel, shape(NX, 10 * HALF), [table, own, high, low],
        [pltpu.VMEM((5, NY, NX), bf16)] * 2, 1, 1 << 30, 3 << 20,
    )
    columns = lax.all_to_all(sent, everyone, 0, 0, tiled=True)

    later, _ = lax.optimization_barrier((own, sent))
    chunks = call(
        regroup_kernel, [shape(PAD, CELLS)] * GROUPS, [block_arg, later],
        [pltpu.VMEM((PAD * (ROWS + 2 * PAD), LANES), f32)] * 2, 1, 0, 4 << 20,
    )
    arrived = exchanged(chunks)

    weights = call(
        weights_kernel, shape(ALL_PAD, BLOCKS * ALL_PAD),
        [
            directions.astype(np.float32), pad_groups(synthesis, 1),
            pad_groups(projection, 0), pad_groups(turn_projection, 1),
        ],
        (), 0, 1 << 28, 1 << 20,
    )
    columns, weights = lax.optimization_barrier((columns, weights))

    wave = (position % HALF).astype(f32) * (2.0 * math.pi / NX)
    half = (position // HALF).astype(jnp.int32)
    bz_high, bz_low = split_table(back_z)
    sent = call(
        solve_kernel, shape(NX, 16 * ROWS),
        [
            wave.reshape(1), half.reshape(1),
            signed_wave(NY).astype(np.float32)[None, :], signed_wave(NZ).astype(np.float32)[:, None],
            columns, *split_table(forward_z), *split_table(forward_y),
            np.concatenate([bz_high, bz_high, bz_low], axis=1), *split_table(back_y),
        ],
        (), 2, 1 << 30, 3 << 20,
    )
    mixed = lax.all_to_all(sent, everyone, 0, 0, tiled=True)
    arrived, _ = lax.optimization_barrier((arrived, sent))
    center, *own_parts = call(
        assemble_kernel, [shape(ALL_PAD, CELLS)] + [shape(ALL_PAD, CHUNK * NX)] * PARTS,
        [group_arg, *arrived], (), 1, 1 << 32, 4 << 20,
    )
    above = pairs(lambda s, b: ((s + 1) % SPACES, b))
    below = pairs(lambda s, b: ((s - 1) % SPACES, b))
    halo = [(lax.ppermute(rows, both, above), lax.ppermute(rows, both, below)) for rows in own_parts]

    flow = call(fields_kernel, shape(11, ROWS, NX, dtype=f32), [mixed, *split_table(back_x)], (), 0, 1 << 29, 2 << 20)
    damp = pad_groups(damping, 0)[:, None]
    returned = []
    for part in range(PARTS):
        size = (pl.Element(ALL_PAD), pl.Element((CHUNK + 2) * NX))
        here = pl.BlockSpec(size, lambda i, part=part: (0, part * CHUNK * NX))
        flow_here = pl.BlockSpec((11, CHUNK, NX), lambda i, part=part: (0, part, 0))
        inner = call(
            inner_kernel, shape(ALL_PAD, CHUNK * NX, dtype=f32), [center, flow, weights, damp],
            [pltpu.VMEM((2, (BLOCKS - 2) * ALL_PAD, NX), bf16), pltpu.VMEM((2, ALL_PAD, NX), f32)],
            0, 1 << 37, 7 << 19, [here, flow_here, VMEM, VMEM],
        )
        rates = call(
            rate_kernel, shape(GROUPS, OWN, CHUNK, NX),
            [inner, *halo[part], flow, weights],
            [
                pltpu.VMEM((2, 2 * ALL_PAD, NX), bf16),
                pltpu.VMEM((2, ALL_PAD, NX), f32),
                pltpu.VMEM((ALL_PAD * CHUNK, LANES), f32),
                pltpu.VMEM((ALL_PAD * CHUNK, LANES), f32),
            ],
            0, 1 << 33, 9 << 19,
            [VMEM, VMEM, VMEM, flow_here, VMEM],
        )
        center, rates = lax.optimization_barrier((center, rates))
        returned, rates = lax.optimization_barrier((returned, rates))
        returned.append(lax.all_to_all(rates, "harm", 0, 0, tiled=True))
    swap = pairs(lambda s, b: (s, b ^ (FLIP * odd(s))))
    late, _ = lax.optimization_barrier((flow[0:3], rates))
    velocity = lax.ppermute(late, both, swap)
    rate = call(place_kernel, shape(OWN, NY, NX), [group_arg ^ block_arg, *returned], (), 1, 0, 4 << 20)
    return (rate.reshape(OWN, 1, NY, NX), velocity.reshape(3, 1, ROWS, NX))


def solution(mesh):
    in_specs = (P("harm", "space", None, None), P(), P(), P(), P())
    out_specs = (P("harm", "space", None, None), P(None, "space", "harm", None))
    return jax.shard_map(local, mesh=mesh, in_specs=in_specs, out_specs=out_specs, check_vma=False)
```

```python
import functools
import math

import jax
import jax.numpy as jnp
import ml_dtypes
import numpy as np
from jax import lax
from jax.experimental import pallas as pl
from jax.experimental.pallas import tpu as pltpu
from jax.sharding import PartitionSpec as P

activity = -3.0
swim_speed = 1.0
transl_diff = 0.25
shape_factor = 0.9
golden_angle = math.pi * (3.0 - math.sqrt(5.0))

NX, NY, NZ = 256, 256, 32
COEFS, QUAD = 120, 256
SPACES, GROUPS = 32, 8
OWN = COEFS // GROUPS
PAD = 16
ROWS = NY // GROUPS
EDGED = ROWS + 2
CELLS = EDGED * NX
HALF = NX // 2
ALL_PAD = GROUPS * PAD
LANES = 128
RUN = 8
FLIP = GROUPS // 2
PARTS = 2
CHUNK = ROWS // PARTS
BLOCKS = 12
bf16, f32 = jnp.bfloat16, jnp.float32
VMEM = pl.BlockSpec(memory_space=pltpu.VMEM)
SMEM = pl.BlockSpec(memory_space=pltpu.SMEM)
PARAMS = pltpu.CompilerParams(vmem_limit_bytes=56 * 1024 * 1024)


def split_table(table):
    high = table.astype(ml_dtypes.bfloat16)
    low = (table - high.astype(np.float64)).astype(ml_dtypes.bfloat16)
    return (high, low)


def signed_wave(length):
    index = np.arange(length)
    signed = np.where(index < length // 2, index, index - length)
    return 2.0 * math.pi / length * np.where(index == length // 2, 0, signed)


def sphere_directions():
    position = np.arange(QUAD, dtype=np.float64)
    height = 1.0 - (2.0 * position + 1.0) / QUAD
    radius = np.sqrt(1.0 - height * height)
    turning = position * golden_angle
    return np.stack([radius * np.cos(turning), radius * np.sin(turning), height])


def tables():
    x = np.arange(NX)[None, :]
    k = np.arange(HALF)[:, None]
    angle = 2.0 * math.pi * (k * x % NX) / NX
    cos_x, sin_x = np.cos(angle), np.sin(angle)
    sign = (-1.0) ** x[0]
    minus = -sin_x
    minus[0] = sign
    forward_x = np.concatenate([cos_x, minus])
    scale = 1.0 / (NX * NY * NZ)
    weight = np.where(k == 0, 1.0, 2.0) * scale
    wave = 2.0 * math.pi / NX * k
    real_x = weight * cos_x
    imag_x = -weight * sin_x
    imag_x[0] = sign * scale
    slope_real = -weight * wave * sin_x
    slope_imag = -weight * wave * cos_x
    back_x = np.concatenate([real_x, imag_x, slope_real, slope_imag], axis=1)
    back_x = np.concatenate([back_x, back_x])

    z = np.arange(NZ)
    angle = 2.0 * math.pi * (z[:, None] * z[None, :] % NZ) / NZ
    both_z = np.concatenate([np.cos(angle), np.sin(angle)])
    forward_z = np.tile(both_z, (1, GROUPS))

    y = np.arange(HALF)[:, None]
    ky = np.arange(NY)[None, :]
    angle = 2.0 * math.pi * (y * ky % NY) / NY
    forward_y = np.block([[np.cos(angle), -np.sin(angle)], [np.sin(angle), np.cos(angle)]])

    ky = np.arange(NY)[:, None]
    angle = 2.0 * math.pi * (ky * np.arange(NY)[None, :] % NY) / NY
    cos_y = np.cos(angle).reshape(NY, GROUPS, 1, ROWS)
    sin_y = np.sin(angle).reshape(NY, GROUPS, 1, ROWS)
    from_real = np.concatenate([cos_y, sin_y], axis=2).reshape(NY, 2 * NY)
    from_imag = np.concatenate([-sin_y, cos_y], axis=2).reshape(NY, 2 * NY)
    back_y = np.concatenate([from_real, from_imag])
    return forward_x, forward_z, forward_y, both_z, back_y, back_x


def halves(value):
    high = value.astype(bf16)
    return high, (value - high.astype(f32)).astype(bf16)


def dot(a, b):
    return jnp.dot(a, b, preferred_element_type=f32)


def regroup_kernel(block_ref, coef_ref, *refs):
    outs, stages = refs[:GROUPS], refs[GROUPS:]
    block = block_ref[0]
    height = ROWS + 2 * PAD
    for stage in stages:
        stage[pl.ds(OWN * height, height), :] = jnp.zeros((height, LANES), f32)
    for j in range(GROUPS):
        first = (block ^ j) * ROWS
        for start, size, at in ((NY - PAD, PAD, 0), (0, ROWS, PAD), (ROWS, PAD, PAD + ROWS)):
            rows = coef_ref[:, pl.ds(pl.multiple_of((first + start) % NY, PAD), size), :].astype(f32)
            for side, stage in enumerate(stages):
                for c in range(OWN):
                    stage[c * height + at : c * height + at + size, :] = rows[
                        c, :, side * LANES : (side + 1) * LANES
                    ]
        for side, stage in enumerate(stages):
            for r in range(EDGED):
                lane = r * NX + side * LANES
                rows = stage[pl.ds(PAD - 1 + r, PAD, stride=height), :]
                outs[j][:, lane : lane + LANES] = rows.astype(bf16)


def stress_kernel(table_ref, coef_ref, high_ref, low_ref, out_ref, stress_high, stress_low):
    step = 32

    def rows(i, carry):
        first = pl.multiple_of(i * step, step)
        sums = [jnp.zeros((step, NX), f32)] * 5
        for c in range(OWN):
            value = coef_ref[c, pl.ds(first, step), :].astype(f32)
            sums = [s + table_ref[r, c] * value for r, s in enumerate(sums)]
        for r in range(5):
            high, low = halves(sums[r])
            stress_high[r, pl.ds(first, step), :] = high
            stress_low[r, pl.ds(first, step), :] = low
        return carry

    lax.fori_loop(0, NY // step, rows, 0)

    def across(a, b):
        return lax.dot_general(a, b, (((1,), (1,)), ((), ())), preferred_element_type=f32)

    for r in range(5):
        high, low = high_ref[...], low_ref[...]
        result = (
            across(high, stress_high[r]) + across(low, stress_high[r]) + across(high, stress_low[r])
        ).astype(bf16)
        for half in range(2):
            for part in range(2):
                lane = (2 * r + part) * HALF
                out_ref[half * HALF : (half + 1) * HALF, lane : lane + HALF] = result[
                    part * HALF : (part + 1) * HALF, half * HALF : (half + 1) * HALF
                ]


def solve_kernel(
    wave_ref, half_ref, ky_ref, kz_ref, recv_ref,
    fz_high, fz_low, fy_high, fy_low, bz, by_high, by_low, out_ref,
):
    recv = recv_ref[...]
    by_z = dot(fz_high[...], recv) + dot(fz_low[...], recv)
    lines = []
    for r in range(5):
        lane = 2 * r * HALF
        cos_re, cos_im = by_z[:NZ, lane : lane + HALF], by_z[:NZ, lane + HALF : lane + 2 * HALF]
        sin_re, sin_im = by_z[NZ:, lane : lane + HALF], by_z[NZ:, lane + HALF : lane + 2 * HALF]
        lines.append(jnp.concatenate([cos_re + sin_im, cos_im - sin_re], axis=1))
    high, low = halves(jnp.concatenate(lines))
    spec = dot(high, fy_high[...]) + dot(low, fy_high[...]) + dot(high, fy_low[...])
    lane = lax.broadcasted_iota(jnp.int32, (NZ, NY), 1)
    flip = jnp.where((lane % 2) * half_ref[0] == 1, -1.0, 1.0)
    real = [spec[r * NZ : (r + 1) * NZ, :NY] * flip for r in range(5)]
    imag = [spec[r * NZ : (r + 1) * NZ, NY:] * flip for r in range(5)]
    kx = jnp.full((NZ, NY), wave_ref[0], f32)
    ky = jnp.broadcast_to(ky_ref[...], (NZ, NY))
    kz = jnp.broadcast_to(kz_ref[...], (NZ, NY))
    square = kx * kx + ky * ky + kz * kz
    inverse = jnp.where(square > 0, 1.0 / jnp.where(square > 0, square, 1.0), 0.0)

    def force(part):
        xx, yy, xy, xz, yz = part
        return (
            kx * xx + ky * xy + kz * xz,
            kx * xy + ky * yy + kz * yz,
            kx * xz + ky * yz,
        )

    def solve(f):
        along = (kx * f[0] + ky * f[1] + kz * f[2]) * inverse
        return [(f[i] - k * along) * inverse for i, k in enumerate((kx, ky, kz))]

    flow_re = solve([-f for f in force(imag)])
    flow_im = solve(force(real))
    fields = list(zip(flow_re, flow_im))
    fields += [(-ky * flow_im[i], ky * flow_re[i]) for i in range(3)]
    fields += [(-kz * flow_im[i], kz * flow_re[i]) for i in range(2)]
    back = []
    for re, im in fields:
        high, low = halves(jnp.concatenate([re, im], axis=1))
        both = dot(bz[...], jnp.concatenate([high, low, high]))
        back.append(
            jnp.concatenate(
                [both[:NZ, :NY] - both[NZ:, NY:], both[:NZ, NY:] + both[NZ:, :NY]], axis=1
            )
        )
    high, low = halves(jnp.concatenate(back))
    done = dot(high, by_high[...]) + dot(low, by_high[...]) + dot(high, by_low[...])
    blocks = []
    for h in range(GROUPS):
        lane = 2 * ROWS * h
        pieces = [done[f * NZ : (f + 1) * NZ, lane : lane + 2 * ROWS] for f in range(8)]
        blocks.append(jnp.concatenate(pieces, axis=1))
    plane = lax.broadcasted_iota(jnp.int32, blocks[0].shape, 0)
    flipped = (plane // RUN) % 2 == 1
    for h in range(GROUPS):
        value = jnp.where(flipped, blocks[h ^ FLIP], blocks[h])
        out_ref[h * NZ : (h + 1) * NZ, :] = value.astype(bf16)


def fields_kernel(recv_ref, high_ref, low_ref, out_ref):
    flat = recv_ref[...].astype(f32).T.astype(bf16)
    both = dot(flat, high_ref[...]) + dot(flat, low_ref[...])

    def field(f, lane):
        row = 2 * ROWS * f
        return (
            both[row : row + ROWS, lane : lane + NX]
            + both[row + ROWS : row + 2 * ROWS, lane + NX : lane + 2 * NX]
        )

    for i in range(3):
        out_ref[i] = field(i, 0)
        out_ref[3 + i] = field(i, 2 * NX)
    for i in range(5):
        out_ref[6 + i] = field(3 + i, 0)


def weights_kernel(dir_ref, synth_ref, proj_ref, turn_ref, out_ref):
    synth = synth_ref[...]
    p = [dir_ref[j : j + 1, :] for j in range(3)]
    proj = proj_ref[...].astype(f32)
    turn = [turn_ref[k].astype(f32) for k in range(3)]
    radial = turn[0] * p[0] + turn[1] * p[1] + turn[2] * p[2]
    same = 0.5 * (shape_factor + 1.0)
    swap = 0.5 * (shape_factor - 1.0)

    def plain(i, j):
        return turn[i] * p[j] - radial * (p[i] * p[j])

    def strain(i, j):
        return same * plain(i, j) + swap * plain(j, i)

    left = [-0.5 * swim_speed * proj * p[j] for j in range(3)] + [-0.5 * proj]
    trace = strain(2, 2)
    left += [strain(0, 0) - trace, strain(1, 0), strain(2, 0)]
    left += [strain(0, 1), strain(1, 1) - trace, strain(2, 1)]
    left += [strain(0, 2), strain(1, 2)]
    for n, value in enumerate(left):
        high, low = halves(value)
        out_ref[:, n * ALL_PAD : (n + 1) * ALL_PAD] = (dot(high, synth) + dot(low, synth)).astype(bf16)


def assemble_kernel(group_ref, *refs):
    out_ref, *parts = refs[GROUPS:]
    group = group_ref[0]
    for j in range(GROUPS):
        where = pl.ds(pl.multiple_of((group ^ j) * PAD, PAD), PAD)
        out_ref[where, :] = refs[j][...]
        for n, part in enumerate(parts):
            part[where, :] = refs[j][:, (n * CHUNK + 1) * NX : ((n + 1) * CHUNK + 1) * NX]


def rate_kernel(
    center_ref, zlow_ref, zhigh_ref, flow_ref, weight_ref, damp_ref,
    out_ref, operands, locals_, *stages,
):
    def build(r, operand, local_terms):
        here = pl.multiple_of(r * NX, NX)
        flow = [flow_ref[f, pl.ds(r, 1), :] for f in range(11)]
        for g in range(GROUPS):
            rows = slice(g * PAD, (g + 1) * PAD)
            value = center_ref[rows, pl.ds(here + NX, NX)].astype(f32)
            y_low = center_ref[rows, pl.ds(here, NX)].astype(f32)
            y_high = center_ref[rows, pl.ds(here + 2 * NX, NX)].astype(f32)
            z_low = zlow_ref[rows, pl.ds(here, NX)].astype(f32)
            z_high = zhigh_ref[rows, pl.ds(here, NX)].astype(f32)
            x_low = pltpu.roll(value, 1, 1)
            x_high = pltpu.roll(value, NX - 1, 1)
            diffs = (x_high - x_low, y_high - y_low, z_high - z_low)
            drift = flow[0] * diffs[0] + flow[1] * diffs[1] + flow[2] * diffs[2]
            lap = x_high + x_low + y_high + y_low + z_high + z_low - 6.0 * value
            local_terms[rows, :] = transl_diff * lap - damp_ref[rows, :] * value
            terms = list(diffs) + [drift] + [flow[3 + n] * value for n in range(8)]
            for n, term in enumerate(terms):
                operand[n * ALL_PAD + g * PAD : n * ALL_PAD + (g + 1) * PAD, :] = term.astype(bf16)

    def rows(i, carry):
        for n in range(2):
            build(2 * i + n, operands.at[n], locals_.at[n])
        for n in range(2):
            result = dot(weight_ref[...], operands[n]) + locals_[n]
            for side, stage in enumerate(stages):
                stage[pl.ds(2 * i + n, ALL_PAD, stride=CHUNK), :] = result[
                    :, side * LANES : (side + 1) * LANES
                ]
        return carry

    lax.fori_loop(0, CHUNK // 2, rows, 0)
    for g in range(GROUPS):
        for c in range(OWN):
            first = (g * PAD + c) * CHUNK
            for side, stage in enumerate(stages):
                out_ref[g, c, :, side * LANES : (side + 1) * LANES] = stage[
                    first : first + CHUNK, :
                ].astype(bf16)


def place_kernel(swap_ref, *refs):
    out_ref = refs[-1]
    for part in range(PARTS):
        for g in range(GROUPS):
            first = pl.multiple_of((swap_ref[0] ^ g) * ROWS + part * CHUNK, CHUNK)
            out_ref[:, pl.ds(first, CHUNK), :] = refs[part][g]


def call(kernel, out_shape, ins, scratch=(), scalars=0, flops=0, byte_count=0, specs=None):
    return pl.pallas_call(
        kernel,
        out_shape=out_shape,
        grid=(1,) if specs else (),
        in_specs=specs or [SMEM] * scalars + [VMEM] * (len(ins) - scalars),
        out_specs=jax.tree.map(lambda _: VMEM, out_shape),
        scratch_shapes=list(scratch),
        compiler_params=PARAMS,
        cost_estimate=pl.CostEstimate(flops=flops, bytes_accessed=byte_count, transcendentals=0),
    )(*ins)


def shape(*dims, dtype=bf16):
    return jax.ShapeDtypeStruct(dims, dtype)


def pad_groups(value, axis):
    parts = value.reshape(*value.shape[:axis], GROUPS, OWN, *value.shape[axis + 1 :])
    widths = [(0, 0)] * parts.ndim
    widths[axis + 1] = (0, PAD - OWN)
    parts = jnp.pad(parts, widths)
    return parts.reshape(*value.shape[:axis], ALL_PAD, *value.shape[axis + 1 :])


def stress_table(synthesis, directions, group):
    dir_x, dir_y, dir_z = directions
    third = 1.0 / 3.0
    moments = np.stack(
        [
            dir_x * dir_x - third,
            dir_y * dir_y - third,
            dir_z * dir_z - third,
            dir_x * dir_y,
            dir_x * dir_z,
            dir_y * dir_z,
        ]
    ).astype(np.float32)
    own = lax.dynamic_slice_in_dim(synthesis, group * OWN, OWN, 1).astype(f32)
    table = jnp.dot(moments, own, precision=lax.Precision.HIGHEST)
    table = (table * (activity / math.sqrt(QUAD))).astype(bf16).astype(f32)
    return jnp.concatenate([table[0:2] - table[2:3], table[3:6]])


def partner(j):
    return [(i, i ^ j) for i in range(GROUPS)]


def exchanged(chunks):
    return [chunks[0]] + [lax.ppermute(c, "harm", partner(j + 1)) for j, c in enumerate(chunks[1:])]


def odd(plane):
    return (plane // RUN) % 2


def pairs(target):
    found = []
    for plane in range(SPACES):
        for group in range(GROUPS):
            to_plane, to_block = target(plane, group ^ (FLIP * odd(plane)))
            to_group = to_block ^ (FLIP * odd(to_plane))
            found.append((plane * GROUPS + group, to_plane * GROUPS + to_group))
    return found


def local(coeffs, synthesis, projection, turn_projection, damping):
    group = lax.axis_index("harm")
    plane = lax.axis_index("space")
    both = ("space", "harm")
    everyone = ("harm", "space")
    position = group * SPACES + plane
    forward_x, forward_z, forward_y, back_z, back_y, back_x = tables()
    directions = sphere_directions()
    own = coeffs.reshape(OWN, NY, NX)
    group_arg = group.astype(jnp.int32).reshape(1)
    block_arg = group_arg ^ (FLIP * odd(plane)).astype(jnp.int32)

    table = stress_table(synthesis, directions, group)
    high, low = split_table(forward_x)
    sent = call(
        stress_kernel, shape(NX, 10 * HALF), [table, own, high, low],
        [pltpu.VMEM((5, NY, NX), bf16)] * 2, 1, 1 << 30, 3 << 20,
    )
    columns = lax.all_to_all(sent, everyone, 0, 0, tiled=True)

    later, _ = lax.optimization_barrier((own, sent))
    chunks = call(
        regroup_kernel, [shape(PAD, CELLS)] * GROUPS, [block_arg, later],
        [pltpu.VMEM((PAD * (ROWS + 2 * PAD), LANES), f32)] * 2, 1, 0, 4 << 20,
    )
    arrived = exchanged(chunks)

    weights = call(
        weights_kernel, shape(ALL_PAD, BLOCKS * ALL_PAD),
        [
            directions.astype(np.float32), pad_groups(synthesis, 1),
            pad_groups(projection, 0), pad_groups(turn_projection, 1),
        ],
        (), 0, 1 << 28, 1 << 20,
    )
    columns, weights = lax.optimization_barrier((columns, weights))

    wave = (position % HALF).astype(f32) * (2.0 * math.pi / NX)
    half = (position // HALF).astype(jnp.int32)
    bz_high, bz_low = split_table(back_z)
    sent = call(
        solve_kernel, shape(NX, 16 * ROWS),
        [
            wave.reshape(1), half.reshape(1),
            signed_wave(NY).astype(np.float32)[None, :], signed_wave(NZ).astype(np.float32)[:, None],
            columns, *split_table(forward_z), *split_table(forward_y),
            np.concatenate([bz_high, bz_high, bz_low], axis=1), *split_table(back_y),
        ],
        (), 2, 1 << 30, 3 << 20,
    )
    mixed = lax.all_to_all(sent, everyone, 0, 0, tiled=True)
    arrived, _ = lax.optimization_barrier((arrived, sent))
    center, *own_parts = call(
        assemble_kernel, [shape(ALL_PAD, CELLS)] + [shape(ALL_PAD, CHUNK * NX)] * PARTS,
        [group_arg, *arrived], (), 1, 1 << 32, 4 << 20,
    )
    above = pairs(lambda s, b: ((s + 1) % SPACES, b))
    below = pairs(lambda s, b: ((s - 1) % SPACES, b))
    halo = [(lax.ppermute(rows, both, above), lax.ppermute(rows, both, below)) for rows in own_parts]

    flow = call(fields_kernel, shape(11, ROWS, NX, dtype=f32), [mixed, *split_table(back_x)], (), 0, 1 << 37, 2 << 20)
    damp = pad_groups(damping, 0)[:, None]
    returned = []
    for part in range(PARTS):
        size = (pl.Element(ALL_PAD), pl.Element((CHUNK + 2) * NX))
        here = pl.BlockSpec(size, lambda i, part=part: (0, part * CHUNK * NX))
        flow_here = pl.BlockSpec((11, CHUNK, NX), lambda i, part=part: (0, part, 0))
        rates = call(
            rate_kernel, shape(GROUPS, OWN, CHUNK, NX), [center, *halo[part], flow, weights, damp],
            [
                pltpu.VMEM((2, BLOCKS * ALL_PAD, NX), bf16),
                pltpu.VMEM((2, ALL_PAD, NX), f32),
                pltpu.VMEM((ALL_PAD * CHUNK, LANES), f32),
                pltpu.VMEM((ALL_PAD * CHUNK, LANES), f32),
            ],
            0, 1 << 33, 9 << 19, [here, VMEM, VMEM, flow_here, VMEM, VMEM],
        )
        center, rates = lax.optimization_barrier((center, rates))
        returned, rates = lax.optimization_barrier((returned, rates))
        returned.append(lax.all_to_all(rates, "harm", 0, 0, tiled=True))
    swap = pairs(lambda s, b: (s, b ^ (FLIP * odd(s))))
    late, _ = lax.optimization_barrier((flow[0:3], rates))
    velocity = lax.ppermute(late, both, swap)
    rate = call(place_kernel, shape(OWN, NY, NX), [group_arg ^ block_arg, *returned], (), 1, 0, 4 << 20)
    return (rate.reshape(OWN, 1, NY, NX), velocity.reshape(3, 1, ROWS, NX))


def solution(mesh):
    in_specs = (P("harm", "space", None, None), P(), P(), P(), P())
    out_specs = (P("harm", "space", None, None), P(None, "space", "harm", None))
    return jax.shard_map(local, mesh=mesh, in_specs=in_specs, out_specs=out_specs, check_vma=False)
```

```python
import functools
import math

import jax
import jax.numpy as jnp
import ml_dtypes
import numpy as np
from jax import lax
from jax.experimental import pallas as pl
from jax.experimental.pallas import tpu as pltpu
from jax.sharding import PartitionSpec as P

activity = -3.0
swim_speed = 1.0
transl_diff = 0.25
shape_factor = 0.9
golden_angle = math.pi * (3.0 - math.sqrt(5.0))

NX, NY, NZ = 256, 256, 32
COEFS, QUAD = 120, 256
SPACES, GROUPS = 32, 8
OWN = COEFS // GROUPS
PAD = 16
ROWS = NY // GROUPS
EDGED = ROWS + 2
CELLS = EDGED * NX
HALF = NX // 2
ALL_PAD = GROUPS * PAD
LANES = 128
RUN = 8
FLIP = GROUPS // 2
PARTS = 2
CHUNK = ROWS // PARTS
BLOCKS = 12
bf16, f32 = jnp.bfloat16, jnp.float32
VMEM = pl.BlockSpec(memory_space=pltpu.VMEM)
SMEM = pl.BlockSpec(memory_space=pltpu.SMEM)
PARAMS = pltpu.CompilerParams(vmem_limit_bytes=56 * 1024 * 1024)


def split_table(table):
    high = table.astype(ml_dtypes.bfloat16)
    low = (table - high.astype(np.float64)).astype(ml_dtypes.bfloat16)
    return (high, low)


def signed_wave(length):
    index = np.arange(length)
    signed = np.where(index < length // 2, index, index - length)
    return 2.0 * math.pi / length * np.where(index == length // 2, 0, signed)


def sphere_directions():
    position = np.arange(QUAD, dtype=np.float64)
    height = 1.0 - (2.0 * position + 1.0) / QUAD
    radius = np.sqrt(1.0 - height * height)
    turning = position * golden_angle
    return np.stack([radius * np.cos(turning), radius * np.sin(turning), height])


def tables():
    x = np.arange(NX)[None, :]
    k = np.arange(HALF)[:, None]
    angle = 2.0 * math.pi * (k * x % NX) / NX
    cos_x, sin_x = np.cos(angle), np.sin(angle)
    sign = (-1.0) ** x[0]
    minus = -sin_x
    minus[0] = sign
    forward_x = np.concatenate([cos_x, minus])
    scale = 1.0 / (NX * NY * NZ)
    weight = np.where(k == 0, 1.0, 2.0) * scale
    wave = 2.0 * math.pi / NX * k
    real_x = weight * cos_x
    imag_x = -weight * sin_x
    imag_x[0] = sign * scale
    slope_real = -weight * wave * sin_x
    slope_imag = -weight * wave * cos_x
    back_x = np.concatenate([real_x, imag_x, slope_real, slope_imag], axis=1)
    back_x = np.concatenate([back_x, back_x])

    z = np.arange(NZ)
    angle = 2.0 * math.pi * (z[:, None] * z[None, :] % NZ) / NZ
    both_z = np.concatenate([np.cos(angle), np.sin(angle)])
    forward_z = np.tile(both_z, (1, GROUPS))

    y = np.arange(HALF)[:, None]
    ky = np.arange(NY)[None, :]
    angle = 2.0 * math.pi * (y * ky % NY) / NY
    forward_y = np.block([[np.cos(angle), -np.sin(angle)], [np.sin(angle), np.cos(angle)]])

    ky = np.arange(NY)[:, None]
    angle = 2.0 * math.pi * (ky * np.arange(NY)[None, :] % NY) / NY
    cos_y = np.cos(angle).reshape(NY, GROUPS, 1, ROWS)
    sin_y = np.sin(angle).reshape(NY, GROUPS, 1, ROWS)
    from_real = np.concatenate([cos_y, sin_y], axis=2).reshape(NY, 2 * NY)
    from_imag = np.concatenate([-sin_y, cos_y], axis=2).reshape(NY, 2 * NY)
    back_y = np.concatenate([from_real, from_imag])
    return forward_x, forward_z, forward_y, both_z, back_y, back_x


def halves(value):
    high = value.astype(bf16)
    return high, (value - high.astype(f32)).astype(bf16)


def dot(a, b):
    return jnp.dot(a, b, preferred_element_type=f32)


def regroup_kernel(block_ref, coef_ref, *refs):
    outs, stages = refs[:GROUPS], refs[GROUPS:]
    block = block_ref[0]
    height = ROWS + 2 * PAD
    for stage in stages:
        stage[pl.ds(OWN * height, height), :] = jnp.zeros((height, LANES), f32)
    for j in range(GROUPS):
        first = (block ^ j) * ROWS
        for start, size, at in ((NY - PAD, PAD, 0), (0, ROWS, PAD), (ROWS, PAD, PAD + ROWS)):
            rows = coef_ref[:, pl.ds(pl.multiple_of((first + start) % NY, PAD), size), :].astype(f32)
            for side, stage in enumerate(stages):
                for c in range(OWN):
                    stage[c * height + at : c * height + at + size, :] = rows[
                        c, :, side * LANES : (side + 1) * LANES
                    ]
        for side, stage in enumerate(stages):
            for r in range(EDGED):
                lane = r * NX + side * LANES
                rows = stage[pl.ds(PAD - 1 + r, PAD, stride=height), :]
                outs[j][:, lane : lane + LANES] = rows.astype(bf16)


def stress_kernel(table_ref, coef_ref, high_ref, low_ref, out_ref, stress_high, stress_low):
    step = 32

    def rows(i, carry):
        first = pl.multiple_of(i * step, step)
        sums = [jnp.zeros((step, NX), f32)] * 5
        for c in range(OWN):
            value = coef_ref[c, pl.ds(first, step), :].astype(f32)
            sums = [s + table_ref[r, c] * value for r, s in enumerate(sums)]
        for r in range(5):
            high, low = halves(sums[r])
            stress_high[r, pl.ds(first, step), :] = high
            stress_low[r, pl.ds(first, step), :] = low
        return carry

    lax.fori_loop(0, NY // step, rows, 0)

    def across(a, b):
        return lax.dot_general(a, b, (((1,), (1,)), ((), ())), preferred_element_type=f32)

    for r in range(5):
        high, low = high_ref[...], low_ref[...]
        result = (
            across(high, stress_high[r]) + across(low, stress_high[r]) + across(high, stress_low[r])
        ).astype(bf16)
        for half in range(2):
            for part in range(2):
                lane = (2 * r + part) * HALF
                out_ref[half * HALF : (half + 1) * HALF, lane : lane + HALF] = result[
                    part * HALF : (part + 1) * HALF, half * HALF : (half + 1) * HALF
                ]


def solve_kernel(
    wave_ref, half_ref, ky_ref, kz_ref, recv_ref,
    fz_high, fz_low, fy_high, fy_low, bz, by_high, by_low, out_ref,
):
    recv = recv_ref[...]
    by_z = dot(fz_high[...], recv) + dot(fz_low[...], recv)
    lines = []
    for r in range(5):
        lane = 2 * r * HALF
        cos_re, cos_im = by_z[:NZ, lane : lane + HALF], by_z[:NZ, lane + HALF : lane + 2 * HALF]
        sin_re, sin_im = by_z[NZ:, lane : lane + HALF], by_z[NZ:, lane + HALF : lane + 2 * HALF]
        lines.append(jnp.concatenate([cos_re + sin_im, cos_im - sin_re], axis=1))
    high, low = halves(jnp.concatenate(lines))
    spec = dot(high, fy_high[...]) + dot(low, fy_high[...]) + dot(high, fy_low[...])
    lane = lax.broadcasted_iota(jnp.int32, (NZ, NY), 1)
    flip = jnp.where((lane % 2) * half_ref[0] == 1, -1.0, 1.0)
    real = [spec[r * NZ : (r + 1) * NZ, :NY] * flip for r in range(5)]
    imag = [spec[r * NZ : (r + 1) * NZ, NY:] * flip for r in range(5)]
    kx = jnp.full((NZ, NY), wave_ref[0], f32)
    ky = jnp.broadcast_to(ky_ref[...], (NZ, NY))
    kz = jnp.broadcast_to(kz_ref[...], (NZ, NY))
    square = kx * kx + ky * ky + kz * kz
    inverse = jnp.where(square > 0, 1.0 / jnp.where(square > 0, square, 1.0), 0.0)

    def force(part):
        xx, yy, xy, xz, yz = part
        return (
            kx * xx + ky * xy + kz * xz,
            kx * xy + ky * yy + kz * yz,
            kx * xz + ky * yz,
        )

    def solve(f):
        along = (kx * f[0] + ky * f[1] + kz * f[2]) * inverse
        return [(f[i] - k * along) * inverse for i, k in enumerate((kx, ky, kz))]

    flow_re = solve([-f for f in force(imag)])
    flow_im = solve(force(real))
    fields = list(zip(flow_re, flow_im))
    fields += [(-ky * flow_im[i], ky * flow_re[i]) for i in range(3)]
    fields += [(-kz * flow_im[i], kz * flow_re[i]) for i in range(2)]
    back = []
    for re, im in fields:
        high, low = halves(jnp.concatenate([re, im], axis=1))
        both = dot(bz[...], jnp.concatenate([high, low, high]))
        back.append(
            jnp.concatenate(
                [both[:NZ, :NY] - both[NZ:, NY:], both[:NZ, NY:] + both[NZ:, :NY]], axis=1
            )
        )
    high, low = halves(jnp.concatenate(back))
    done = dot(high, by_high[...]) + dot(low, by_high[...]) + dot(high, by_low[...])
    blocks = []
    for h in range(GROUPS):
        lane = 2 * ROWS * h
        pieces = [done[f * NZ : (f + 1) * NZ, lane : lane + 2 * ROWS] for f in range(8)]
        blocks.append(jnp.concatenate(pieces, axis=1))
    plane = lax.broadcasted_iota(jnp.int32, blocks[0].shape, 0)
    flipped = (plane // RUN) % 2 == 1
    for h in range(GROUPS):
        value = jnp.where(flipped, blocks[h ^ FLIP], blocks[h])
        out_ref[h * NZ : (h + 1) * NZ, :] = value.astype(bf16)


def fields_kernel(recv_ref, high_ref, low_ref, out_ref):
    flat = recv_ref[...].astype(f32).T.astype(bf16)
    both = dot(flat, high_ref[...]) + dot(flat, low_ref[...])

    def field(f, lane):
        row = 2 * ROWS * f
        return (
            both[row : row + ROWS, lane : lane + NX]
            + both[row + ROWS : row + 2 * ROWS, lane + NX : lane + 2 * NX]
        )

    for i in range(3):
        out_ref[i] = field(i, 0)
        out_ref[3 + i] = field(i, 2 * NX)
    for i in range(5):
        out_ref[6 + i] = field(3 + i, 0)


def weights_kernel(dir_ref, synth_ref, proj_ref, turn_ref, out_ref):
    synth = synth_ref[...]
    p = [dir_ref[j : j + 1, :] for j in range(3)]
    proj = proj_ref[...].astype(f32)
    turn = [turn_ref[k].astype(f32) for k in range(3)]
    radial = turn[0] * p[0] + turn[1] * p[1] + turn[2] * p[2]
    same = 0.5 * (shape_factor + 1.0)
    swap = 0.5 * (shape_factor - 1.0)

    def plain(i, j):
        return turn[i] * p[j] - radial * (p[i] * p[j])

    def strain(i, j):
        return same * plain(i, j) + swap * plain(j, i)

    left = [-0.5 * swim_speed * proj * p[j] for j in range(3)] + [-0.5 * proj]
    trace = strain(2, 2)
    left += [strain(0, 0) - trace, strain(1, 0), strain(2, 0)]
    left += [strain(0, 1), strain(1, 1) - trace, strain(2, 1)]
    left += [strain(0, 2), strain(1, 2)]
    for n, value in enumerate(left):
        high, low = halves(value)
        out_ref[:, n * ALL_PAD : (n + 1) * ALL_PAD] = (dot(high, synth) + dot(low, synth)).astype(bf16)


def assemble_kernel(group_ref, *refs):
    out_ref, *parts = refs[GROUPS:]
    group = group_ref[0]
    for j in range(GROUPS):
        where = pl.ds(pl.multiple_of((group ^ j) * PAD, PAD), PAD)
        out_ref[where, :] = refs[j][...]
        for n, part in enumerate(parts):
            part[where, :] = refs[j][:, (n * CHUNK + 1) * NX : ((n + 1) * CHUNK + 1) * NX]


def rate_kernel(
    center_ref, zlow_ref, zhigh_ref, flow_ref, weight_ref, damp_ref,
    out_ref, operands, locals_, *stages,
):
    def build(r, operand, local_terms):
        here = pl.multiple_of(r * NX, NX)
        flow = [flow_ref[f, pl.ds(r, 1), :] for f in range(11)]
        for g in range(GROUPS):
            rows = slice(g * PAD, (g + 1) * PAD)
            value = center_ref[rows, pl.ds(here + NX, NX)].astype(f32)
            y_low = center_ref[rows, pl.ds(here, NX)].astype(f32)
            y_high = center_ref[rows, pl.ds(here + 2 * NX, NX)].astype(f32)
            z_low = zlow_ref[rows, pl.ds(here, NX)].astype(f32)
            z_high = zhigh_ref[rows, pl.ds(here, NX)].astype(f32)
            x_low = pltpu.roll(value, 1, 1)
            x_high = pltpu.roll(value, NX - 1, 1)
            diffs = (x_high - x_low, y_high - y_low, z_high - z_low)
            drift = flow[0] * diffs[0] + flow[1] * diffs[1] + flow[2] * diffs[2]
            lap = x_high + x_low + y_high + y_low + z_high + z_low - 6.0 * value
            local_terms[rows, :] = transl_diff * lap - damp_ref[rows, :] * value
            terms = list(diffs) + [drift] + [flow[3 + n] * value for n in range(8)]
            for n, term in enumerate(terms):
                operand[n * ALL_PAD + g * PAD : n * ALL_PAD + (g + 1) * PAD, :] = term.astype(bf16)

    def rows(i, carry):
        for n in range(4):
            build(4 * i + n, operands.at[n], locals_.at[n])
        for n in range(4):
            result = dot(weight_ref[...], operands[n]) + locals_[n]
            for side, stage in enumerate(stages):
                stage[pl.ds(4 * i + n, ALL_PAD, stride=CHUNK), :] = result[
                    :, side * LANES : (side + 1) * LANES
                ]
        return carry

    lax.fori_loop(0, CHUNK // 4, rows, 0)
    for g in range(GROUPS):
        for c in range(OWN):
            first = (g * PAD + c) * CHUNK
            for side, stage in enumerate(stages):
                out_ref[g, c, :, side * LANES : (side + 1) * LANES] = stage[
                    first : first + CHUNK, :
                ].astype(bf16)


def place_kernel(swap_ref, *refs):
    out_ref = refs[-1]
    for part in range(PARTS):
        for g in range(GROUPS):
            first = pl.multiple_of((swap_ref[0] ^ g) * ROWS + part * CHUNK, CHUNK)
            out_ref[:, pl.ds(first, CHUNK), :] = refs[part][g]


def call(kernel, out_shape, ins, scratch=(), scalars=0, flops=0, byte_count=0, specs=None):
    return pl.pallas_call(
        kernel,
        out_shape=out_shape,
        grid=(1,) if specs else (),
        in_specs=specs or [SMEM] * scalars + [VMEM] * (len(ins) - scalars),
        out_specs=jax.tree.map(lambda _: VMEM, out_shape),
        scratch_shapes=list(scratch),
        compiler_params=PARAMS,
        cost_estimate=pl.CostEstimate(flops=flops, bytes_accessed=byte_count, transcendentals=0),
    )(*ins)


def shape(*dims, dtype=bf16):
    return jax.ShapeDtypeStruct(dims, dtype)


def pad_groups(value, axis):
    parts = value.reshape(*value.shape[:axis], GROUPS, OWN, *value.shape[axis + 1 :])
    widths = [(0, 0)] * parts.ndim
    widths[axis + 1] = (0, PAD - OWN)
    parts = jnp.pad(parts, widths)
    return parts.reshape(*value.shape[:axis], ALL_PAD, *value.shape[axis + 1 :])


def stress_table(synthesis, directions, group):
    dir_x, dir_y, dir_z = directions
    third = 1.0 / 3.0
    moments = np.stack(
        [
            dir_x * dir_x - third,
            dir_y * dir_y - third,
            dir_z * dir_z - third,
            dir_x * dir_y,
            dir_x * dir_z,
            dir_y * dir_z,
        ]
    ).astype(np.float32)
    own = lax.dynamic_slice_in_dim(synthesis, group * OWN, OWN, 1).astype(f32)
    table = jnp.dot(moments, own, precision=lax.Precision.HIGHEST)
    table = (table * (activity / math.sqrt(QUAD))).astype(bf16).astype(f32)
    return jnp.concatenate([table[0:2] - table[2:3], table[3:6]])


def partner(j):
    return [(i, i ^ j) for i in range(GROUPS)]


def exchanged(chunks):
    return [chunks[0]] + [lax.ppermute(c, "harm", partner(j + 1)) for j, c in enumerate(chunks[1:])]


def odd(plane):
    return (plane // RUN) % 2


def pairs(target):
    found = []
    for plane in range(SPACES):
        for group in range(GROUPS):
            to_plane, to_block = target(plane, group ^ (FLIP * odd(plane)))
            to_group = to_block ^ (FLIP * odd(to_plane))
            found.append((plane * GROUPS + group, to_plane * GROUPS + to_group))
    return found


def local(coeffs, synthesis, projection, turn_projection, damping):
    group = lax.axis_index("harm")
    plane = lax.axis_index("space")
    both = ("space", "harm")
    everyone = ("harm", "space")
    position = group * SPACES + plane
    forward_x, forward_z, forward_y, back_z, back_y, back_x = tables()
    directions = sphere_directions()
    own = coeffs.reshape(OWN, NY, NX)
    group_arg = group.astype(jnp.int32).reshape(1)
    block_arg = group_arg ^ (FLIP * odd(plane)).astype(jnp.int32)

    table = stress_table(synthesis, directions, group)
    high, low = split_table(forward_x)
    sent = call(
        stress_kernel, shape(NX, 10 * HALF), [table, own, high, low],
        [pltpu.VMEM((5, NY, NX), bf16)] * 2, 1, 1 << 30, 3 << 20,
    )
    columns = lax.all_to_all(sent, everyone, 0, 0, tiled=True)

    later, _ = lax.optimization_barrier((own, sent))
    chunks = call(
        regroup_kernel, [shape(PAD, CELLS)] * GROUPS, [block_arg, later],
        [pltpu.VMEM((PAD * (ROWS + 2 * PAD), LANES), f32)] * 2, 1, 0, 4 << 20,
    )
    arrived = exchanged(chunks)

    weights = call(
        weights_kernel, shape(ALL_PAD, BLOCKS * ALL_PAD),
        [
            directions.astype(np.float32), pad_groups(synthesis, 1),
            pad_groups(projection, 0), pad_groups(turn_projection, 1),
        ],
        (), 0, 1 << 28, 1 << 20,
    )
    columns, weights = lax.optimization_barrier((columns, weights))

    wave = (position % HALF).astype(f32) * (2.0 * math.pi / NX)
    half = (position // HALF).astype(jnp.int32)
    bz_high, bz_low = split_table(back_z)
    sent = call(
        solve_kernel, shape(NX, 16 * ROWS),
        [
            wave.reshape(1), half.reshape(1),
            signed_wave(NY).astype(np.float32)[None, :], signed_wave(NZ).astype(np.float32)[:, None],
            columns, *split_table(forward_z), *split_table(forward_y),
            np.concatenate([bz_high, bz_high, bz_low], axis=1), *split_table(back_y),
        ],
        (), 2, 1 << 30, 3 << 20,
    )
    mixed = lax.all_to_all(sent, everyone, 0, 0, tiled=True)
    arrived, _ = lax.optimization_barrier((arrived, sent))
    center, *own_parts = call(
        assemble_kernel, [shape(ALL_PAD, CELLS)] + [shape(ALL_PAD, CHUNK * NX)] * PARTS,
        [group_arg, *arrived], (), 1, 1 << 32, 4 << 20,
    )
    above = pairs(lambda s, b: ((s + 1) % SPACES, b))
    below = pairs(lambda s, b: ((s - 1) % SPACES, b))
    halo = [(lax.ppermute(rows, both, above), lax.ppermute(rows, both, below)) for rows in own_parts]

    flow = call(fields_kernel, shape(11, ROWS, NX, dtype=f32), [mixed, *split_table(back_x)], (), 0, 1 << 37, 2 << 20)
    damp = pad_groups(damping, 0)[:, None]
    returned = []
    for part in range(PARTS):
        size = (pl.Element(ALL_PAD), pl.Element((CHUNK + 2) * NX))
        here = pl.BlockSpec(size, lambda i, part=part: (0, part * CHUNK * NX))
        flow_here = pl.BlockSpec((11, CHUNK, NX), lambda i, part=part: (0, part, 0))
        rates = call(
            rate_kernel, shape(GROUPS, OWN, CHUNK, NX), [center, *halo[part], flow, weights, damp],
            [
                pltpu.VMEM((4, BLOCKS * ALL_PAD, NX), bf16),
                pltpu.VMEM((4, ALL_PAD, NX), f32),
                pltpu.VMEM((ALL_PAD * CHUNK, LANES), f32),
                pltpu.VMEM((ALL_PAD * CHUNK, LANES), f32),
            ],
            0, 1 << 33, 9 << 19, [here, VMEM, VMEM, flow_here, VMEM, VMEM],
        )
        center, rates = lax.optimization_barrier((center, rates))
        returned, rates = lax.optimization_barrier((returned, rates))
        returned.append(lax.all_to_all(rates, "harm", 0, 0, tiled=True))
    swap = pairs(lambda s, b: (s, b ^ (FLIP * odd(s))))
    late, _ = lax.optimization_barrier((flow[0:3], rates))
    velocity = lax.ppermute(late, both, swap)
    rate = call(place_kernel, shape(OWN, NY, NX), [group_arg ^ block_arg, *returned], (), 1, 0, 4 << 20)
    return (rate.reshape(OWN, 1, NY, NX), velocity.reshape(3, 1, ROWS, NX))


def solution(mesh):
    in_specs = (P("harm", "space", None, None), P(), P(), P(), P())
    out_specs = (P("harm", "space", None, None), P(None, "space", "harm", None))
    return jax.shard_map(local, mesh=mesh, in_specs=in_specs, out_specs=out_specs, check_vma=False)
```
